32 devices in a mesh: segment: 4 (over y, x), dp: 8 (over z, core).
Axes of the slice: x: 2, y: 2, z: 4, core: 2. Of those that a mesh axis runs over, the one named last changes fastest.
Arguments:
- fwd_in: bfloat16 [2, 4, 8, 16, 32, 256], P(None, 'segment', 'dp'), may hold values from -6 to 6
- bwd_in: bfloat16 [4, 4, 8, 16, 32, 256], P(None, 'segment', 'dp'), may hold values from -6 to 6
- fresh: bfloat16 [2, 8, 16, 32, 256], P(None, 'dp'), may hold values from -6 to 6
- top_cot: bfloat16 [2, 8, 16, 32, 256], P(None, 'dp'), may hold values from -6 to 6
- conv_weight: bfloat16 [4, 256, 9, 256], P('segment', 'dp'), may hold values from -0.125 to 0.125
Outputs:
- fwd_out: bfloat16 [2, 4, 8, 16, 32, 256], P(None, 'segment', 'dp')
- bwd_out: bfloat16 [4, 4, 8, 16, 32, 256], P(None, 'segment', 'dp')
- weight_grad: float32 [4, 256, 9, 256], P('segment', 'dp')
The draws below stay inside these ranges and needn't reach their ends.
All inputs are finite; a program needn't handle non-finite values.
Results may differ from the reference program's by a relative error of at most 0.0055.
Values may be sent and summed in bfloat16 or wider, within the bound.
No kernel may reach another device: no remote copies, remote signals or barrier semaphores. Data moves between devices by JAX's collectives and lax.ppermute only.
A program may use at most 64 MiB of HBM per device.

```python
import jax
import jax.numpy as jnp
from jax import lax

C = 256
ROWS = 16
COLS = 32
SEGMENTS = 4
TILES = 8
PIXELS = 4096


def block_scale(rng, shape, shards, smallest, largest):
    factor_of = 1.0
    for position, parts in shards:
        heights = jax.random.uniform(jax.random.fold_in(jax.random.fold_in(rng, 6), position), (parts,), jnp.float32, smallest / len(shards), largest / len(shards))
        factor_of = factor_of * jnp.repeat(jnp.exp(heights), shape[position] // parts).reshape((-1,) + (1,) * (len(shape) - 1 - position))
    return factor_of


def gaussian(own_key, dims, scale, most, cuts=(), kind=jnp.bfloat16):
    entries = jax.random.normal(own_key, dims, jnp.float32) * scale
    if len(cuts) > 0:
        entries = block_scale(own_key, dims, cuts, -0.22, 0.18) * entries
    return jnp.clip(entries, min=-most, max=most).astype(kind)


def setup_inputs(seed: int = 0) -> dict:
    seeds = jax.random.split(jax.random.key(seed), 6)
    return {
        "fwd_in": gaussian(seeds[0], (2, SEGMENTS, TILES, ROWS, COLS, C), 1.0, 6.0, ((1, 4), (2, 8))),
        "bwd_in": gaussian(seeds[1], (4, SEGMENTS, TILES, ROWS, COLS, C), 1.0, 6.0, ((1, 4), (2, 8))),
        "fresh": gaussian(seeds[2], (2, TILES, ROWS, COLS, C), 1.0, 6.0, ((1, 8),)),
        "top_cot": gaussian(seeds[3], (2, TILES, ROWS, COLS, C), 1.0, 6.0, ((1, 8),)),
        "conv_weight": gaussian(seeds[4], (SEGMENTS, C, 9, C), (9 * C) ** -0.5, 0.125, ((0, 4), (1, 8))),
    }


def to_images(tiles):
    return tiles.reshape(tiles.shape[0] // 2, 2 * tiles.shape[1], tiles.shape[2], tiles.shape[3])


def to_tiles(images):
    return images.reshape(images.shape[0] * 2, images.shape[1] // 2, images.shape[2], images.shape[3])


def extended_of(images):
    return jnp.pad(images, ((0, 0), (1, 1), (1, 1), (0, 0)))


def conv_forward(extended, weight):
    height = extended.shape[1] - 2
    width = extended.shape[2] - 2
    channels = extended.shape[3]
    running = jnp.zeros((extended.shape[0] * height * width, weight.shape[2]), jnp.float32)
    for row_off in range(3):
        for col_off in range(3):
            window = extended[:, row_off:row_off + height, col_off:col_off + width, :].reshape(-1, channels)
            running = running + jnp.dot(window, weight[:, 3 * row_off + col_off, :], preferred_element_type=jnp.float32)
    return running.reshape(extended.shape[0], height, width, weight.shape[2])


def conv_back(cot_ext, weight):
    height = cot_ext.shape[1] - 2
    width = cot_ext.shape[2] - 2
    channels = cot_ext.shape[3]
    running = jnp.zeros((cot_ext.shape[0] * height * width, weight.shape[0]), jnp.float32)
    for row_off in range(3):
        for col_off in range(3):
            window = cot_ext[:, 2 - row_off:2 - row_off + height, 2 - col_off:2 - col_off + width, :].reshape(-1, channels)
            running = running + lax.dot_general(window, weight[:, 3 * row_off + col_off, :], (((1,), (1,)), ((), ())), preferred_element_type=jnp.float32)
    return running.reshape(cot_ext.shape[0], height, width, weight.shape[0])


def weight_terms(extended, cotangent):
    height = cotangent.shape[1]
    width = cotangent.shape[2]
    channels = extended.shape[3]
    cot_flat = cotangent.reshape(-1, cotangent.shape[3])
    listing = []
    for row_off in range(3):
        for col_off in range(3):
            window = extended[:, row_off:row_off + height, col_off:col_off + width, :].reshape(-1, channels)
            listing.append(lax.dot_general(window, cot_flat, (((0,), (0,)), ((), ())), preferred_element_type=jnp.float32))
    return jnp.stack(listing, axis=1)


def forward_segment(first_in, second_in, weight):
    branch = conv_forward(jnp.maximum(extended_of(second_in), 0), weight)
    return second_in, (first_in.astype(jnp.float32) + branch).astype(jnp.bfloat16)


def backward_segment(out_first, out_second, cot_first, cot_second, weight):
    ext_rec = jnp.maximum(extended_of(out_first), 0)
    rebuilt = (out_second.astype(jnp.float32) - conv_forward(ext_rec, weight)).astype(jnp.bfloat16)
    through = conv_back(extended_of(cot_second), weight)
    cot_rebuilt = (cot_first.astype(jnp.float32) + jnp.where(out_first > 0, through, 0.0)).astype(jnp.bfloat16)
    return (rebuilt, out_first, cot_second, cot_rebuilt), weight_terms(ext_rec, cot_second)


def reference(fwd_in, bwd_in, fresh, top_cot, conv_weight):
    scale = (2.0 * PIXELS) ** -0.5
    first_pairs = []
    first_msgs = []
    first_grads = []
    for segment_pos in range(SEGMENTS):
        weight = conv_weight[segment_pos]
        first_pairs.append(forward_segment(to_images(fwd_in[0, segment_pos]), to_images(fwd_in[1, segment_pos]), weight))
        message, grad_term = backward_segment(to_images(bwd_in[0, segment_pos]), to_images(bwd_in[1, segment_pos]), to_images(bwd_in[2, segment_pos]), to_images(bwd_in[3, segment_pos]), weight)
        first_msgs.append(message)
        first_grads.append(grad_term)
    second_pairs = []
    second_msgs = []
    grads = []
    for segment_pos in range(SEGMENTS):
        weight = conv_weight[segment_pos]
        if segment_pos == 0:
            pair_in = (to_images(fresh[0]), to_images(fresh[1]))
        else:
            pair_in = first_pairs[segment_pos - 1]
        if segment_pos == SEGMENTS - 1:
            four_in = (first_pairs[segment_pos][0], first_pairs[segment_pos][1], to_images(top_cot[0]), to_images(top_cot[1]))
        else:
            four_in = first_msgs[segment_pos + 1]
        second_pairs.append(forward_segment(pair_in[0], pair_in[1], weight))
        message, grad_term = backward_segment(four_in[0], four_in[1], four_in[2], four_in[3], weight)
        second_msgs.append(message)
        grads.append((first_grads[segment_pos] + grad_term) * scale)
    fwd_out = jnp.stack([jnp.stack([to_tiles(pair[slot]) for pair in second_pairs]) for slot in range(2)])
    bwd_out = jnp.stack([jnp.stack([to_tiles(message[slot]) for message in second_msgs]) for slot in range(4)])
    return fwd_out, bwd_out, jnp.stack(grads)
```

```python
import functools

import jax
import jax.numpy as jnp
from jax import lax
from jax.experimental import pallas as pl
from jax.experimental.pallas import tpu as pltpu
from jax.sharding import PartitionSpec as P

BF16 = jnp.bfloat16
F32 = jnp.float32
VMEM = pl.BlockSpec(memory_space=pltpu.VMEM)
SMEM = pl.BlockSpec(memory_space=pltpu.SMEM)
TAPS = 9
PARITY, FIRST, LAST, PLACE = range(4)
MOST_DIRECT = 4


def call(kernel, out_shape, operands, flops, scratch=()):
    outs = jax.tree.leaves(out_shape)
    moved = sum(x.size * x.dtype.itemsize for x in operands[1:]) + sum(x.size * x.dtype.itemsize for x in outs)
    return pl.pallas_call(
        kernel,
        out_shape=out_shape,
        in_specs=[SMEM] + [VMEM] * (len(operands) - 1),
        out_specs=jax.tree.map(lambda _: VMEM, out_shape),
        scratch_shapes=list(scratch),
        compiler_params=pltpu.CompilerParams(vmem_limit_bytes=32 * 1024 * 1024),
        cost_estimate=pl.CostEstimate(flops=int(flops), bytes_accessed=int(moved), transcendentals=0),
    )(*operands)


def swapped(x, bit):
    return lax.ppermute(x, "dp", [(i, i ^ bit) for i in range(lax.axis_size("dp"))])


def passed_along(block, distance):
    devices = range(lax.axis_size("segment"))
    route = [(i - distance, i) for i in devices if i - distance in devices]
    return lax.ppermute(block, "segment", route)


def unfold(ext, tile, halo, parity, relu):
    height, width, channels = tile.shape
    blank = jnp.zeros_like(halo)
    above = jnp.where(parity == 1, halo, blank)
    below = jnp.where(parity == 0, halo, blank)
    rows = jnp.concatenate([above, tile.reshape(height * width, channels), below], axis=0)
    if relu:
        rows = jnp.maximum(rows, jnp.zeros_like(rows))
    amount = (height + 2) * width
    wide = rows.astype(F32)
    col = lax.rem(lax.broadcasted_iota(jnp.int32, wide.shape, 0), width)
    left = jnp.where(col == 0, 0.0, pltpu.roll(wide, 1, 0))
    right = jnp.where(col == width - 1, 0.0, pltpu.roll(wide, amount - 1, 0))
    ext[:, :channels] = left.astype(BF16)
    ext[:, channels : 2 * channels] = rows
    ext[:, 2 * channels :] = right.astype(BF16)


def windows(ext, width):
    amount = ext.shape[0] - 2 * width
    return jnp.concatenate([ext[a * width : a * width + amount, :] for a in range(3)], axis=1)


def conv(ext, weight, width):
    flat = weight[...].reshape(TAPS * weight.shape[1], weight.shape[2])
    return jnp.dot(windows(ext, width), flat, preferred_element_type=F32)


def conv_transposed(ext, weight, width):
    flat = jnp.concatenate([weight[TAPS - 1 - t] for t in range(TAPS)], axis=1)
    return lax.dot_general(windows(ext, width), flat, (((1,), (1,)), ((), ())), preferred_element_type=F32)


def edge(tile, parity):
    return jnp.where(parity == 0, tile[tile.shape[0] - 1], tile[0])


def edges_kernel(info, fwd_in, bwd_in, top_cot, out):
    parity = info[PARITY]
    out[0] = edge(fwd_in.at[1, 0, 0], parity)
    out[1] = edge(bwd_in.at[0, 0, 0], parity)
    out[2] = edge(bwd_in.at[3, 0, 0], parity)
    out[3] = edge(top_cot.at[1, 0], parity)


def grad_into(store, stream, ext, width):
    height, _, channels = stream.shape
    flat = jnp.maximum(stream, jnp.zeros_like(stream)).reshape(height * width, channels)
    turned = flat.astype(F32).T.astype(BF16)
    wide = windows(ext, width)
    outs = wide.shape[1] // TAPS
    for t in range(TAPS):
        other = TAPS - 1 - t
        store(t, jnp.dot(turned, wide[:, other * outs : (other + 1) * outs], preferred_element_type=F32))


def splitter(info, keep, give, add):
    def store(t, total):
        parts, _, rows, outs = keep.shape
        cut = total.reshape(parts, 2, rows, outs)
        mine = jnp.where(info[PARITY] == 0, cut[:, 0], cut[:, 1])
        theirs = jnp.where(info[PARITY] == 0, cut[:, 1], cut[:, 0])
        if add:
            mine = mine + keep[:, t]
            theirs = theirs + give[:, t].astype(F32)
        keep[:, t] = mine
        give[:, t] = theirs.astype(BF16)

    return store


def whole(total_ref, add):
    def store(t, total):
        total_ref[t] = total + total_ref[t] if add else total

    return store


def grad_one_kernel(info, halos, fwd_in, bwd_in, top_cot, *rest):
    *outs, ext = rest
    width = halos.shape[1]
    store = splitter(info, *outs, add=False) if len(outs) == 2 else whole(outs[0], add=False)
    again = splitter(info, *outs, add=True) if len(outs) == 2 else whole(outs[0], add=True)
    unfold(ext, bwd_in[3, 0, 0], halos[2], info[PARITY], False)
    grad_into(store, bwd_in[0, 0, 0], ext, width)

    @pl.when(info[LAST] == 1)
    def _():
        unfold(ext, top_cot[1, 0], halos[3], info[PARITY], False)
        grad_into(again, fwd_in[1, 0, 0], ext, width)


def grad_two_kernel(info, halos, message, *rest):
    *outs, ext = rest
    width = halos.shape[1]
    store = splitter(info, *outs, add=False) if len(outs) == 2 else whole(outs[0], add=False)
    unfold(ext, message[1], halos[1], info[PARITY], False)
    grad_into(store, message[0], ext, width)


def pair_sum_kernel(info, keep, got, own, *sends):
    place = info[PLACE]
    own[...] = keep[place] + got[place].astype(F32)
    for k, send in enumerate(sends):
        there = lax.bitwise_xor(place, k + 1)
        send[...] = (keep[there] + got[there].astype(F32)).astype(BF16)


def step_one_kernel(info, halos, fwd_in, bwd_in, *rest):
    *pieces, message, second, edges, weight, ext = rest
    width = halos.shape[1]
    parity = info[PARITY]
    if len(pieces) == 1:
        weight[...] = pieces[0][...]
    else:
        rows = pieces[0].shape[1]
        half = len(pieces) // 2
        for k in range(half):
            there = 2 * lax.bitwise_xor(info[PLACE], k)
            for piece, slot in ((pieces[k], there + parity), (pieces[half + k], there + 1 - parity)):
                weight[:, pl.ds(pl.multiple_of(slot * rows, rows), rows), :] = piece[...]
    shape = second.shape
    unfold(ext, bwd_in[0, 0, 0], halos[1], parity, True)
    message[0] = (bwd_in[1, 0, 0].astype(F32) - conv(ext, weight, width).reshape(shape)).astype(BF16)
    unfold(ext, bwd_in[3, 0, 0], halos[2], parity, False)
    through = conv_transposed(ext, weight, width).reshape(shape)
    kept = jnp.where(bwd_in[0, 0, 0].astype(F32) > 0, through, 0.0)
    message[1] = (bwd_in[2, 0, 0].astype(F32) + kept).astype(BF16)
    unfold(ext, fwd_in[1, 0, 0], halos[0], parity, True)
    second[...] = (fwd_in[0, 0, 0].astype(F32) + conv(ext, weight, width).reshape(shape)).astype(BF16)
    edges[0] = edge(message.at[0], parity)
    edges[1] = edge(message.at[1], parity)


def edges_two_kernel(info, second, message, fresh, fwd_in, top_cot, out):
    parity = info[PARITY]
    out[0] = jnp.where(info[FIRST] == 1, edge(fresh.at[1, 0], parity), edge(second, parity))
    out[1] = jnp.where(info[LAST] == 1, edge(fwd_in.at[1, 0, 0], parity), edge(message.at[0], parity))
    out[2] = jnp.where(info[LAST] == 1, edge(top_cot.at[1, 0], parity), edge(message.at[1], parity))


def forward_two_kernel(info, halos, early, second, fresh, weight, out, ext):
    width = halos.shape[1]
    first = info[FIRST] == 1
    stream = jnp.where(first, fresh[1, 0], second[...])
    unfold(ext, stream, halos[0], info[PARITY], True)
    other = jnp.where(first, fresh[0, 0], early[...])
    branch = conv(ext, weight, width).reshape(stream.shape)
    out[0, 0, 0] = stream
    out[1, 0, 0] = (other.astype(F32) + branch).astype(BF16)


def backward_two_kernel(info, halos, early, message, own_second, fwd_in, top_cot, weight, out, ext):
    width = halos.shape[1]
    last = info[LAST] == 1
    out_first = jnp.where(last, fwd_in[1, 0, 0], message[0])
    cot_second = jnp.where(last, top_cot[1, 0], message[1])
    out[1, 0, 0] = out_first
    out[2, 0, 0] = cot_second
    unfold(ext, out_first, halos[1], info[PARITY], True)
    out_second = jnp.where(last, own_second[...], early[0])
    branch = conv(ext, weight, width).reshape(out_first.shape)
    out[0, 0, 0] = (out_second.astype(F32) - branch).astype(BF16)
    unfold(ext, cot_second, halos[2], info[PARITY], False)
    through = conv_transposed(ext, weight, width).reshape(out_first.shape)
    cot_first = jnp.where(last, top_cot[0, 0], early[1])
    kept = jnp.where(out[1, 0, 0].astype(F32) > 0, through, 0.0)
    out[3, 0, 0] = (cot_first.astype(F32) + kept).astype(BF16)


def gather_sum_kernel(info, own, *rest):
    *parts, out = rest
    out[...] = functools.reduce(lambda x, y: x + y, [own[...]] + [p[...].astype(F32) for p in parts]).astype(BF16)


def finish_kernel(scale, info, own, *rest):
    *parts, out = rest
    out[...] = functools.reduce(lambda x, y: x + y, [own[...]] + [p[...].astype(F32) for p in parts]) * scale


def shards(fwd_in, bwd_in, fresh, top_cot, conv_weight):
    dp = lax.axis_size("dp")
    places = dp // 2
    dp_pos = lax.axis_index("dp")
    segment_pos = lax.axis_index("segment")
    height, width, channels = fwd_in.shape[3:]
    shard = conv_weight[0].transpose(1, 0, 2)
    rows = shard.shape[1]
    outs = shard.shape[2]
    direct = places <= MOST_DIRECT and rows % 16 == 0
    info = jnp.stack(
        [
            dp_pos % 2,
            (segment_pos == 0).astype(jnp.int32),
            (segment_pos == lax.axis_size("segment") - 1).astype(jnp.int32),
            dp_pos // 2,
        ]
    ).astype(jnp.int32)
    tile = jax.ShapeDtypeStruct((height, width, channels), BF16)
    tiles = lambda n: jax.ShapeDtypeStruct((n,) + tile.shape, BF16)
    line = lambda n: jax.ShapeDtypeStruct((n, width, channels), BF16)
    like = lambda x, dtype: jax.ShapeDtypeStruct(x.shape, dtype)
    ext = pltpu.VMEM(((height + 2) * width, 3 * channels), BF16)
    conv_flops = 2 * height * width * channels * TAPS * outs

    if direct:
        mine = [shard] + [swapped(shard, 2 * k) for k in range(1, places)]
        pieces = mine + [swapped(x, 1) for x in mine]
    else:
        pieces = [lax.all_gather(shard, "dp", axis=1, tiled=True)]

    early_fwd = passed_along(fwd_in[1, 0, 0], 1)
    early_back = passed_along(jnp.stack([bwd_in[0, 0, 0], bwd_in[3, 0, 0]]), -1)

    halos = swapped(call(edges_kernel, line(4), (info, fwd_in, bwd_in, top_cot), 0), 1)

    def scattered(kernel, operands, flops):
        if not direct:
            total = call(kernel, jax.ShapeDtypeStruct((TAPS, channels, outs), F32), operands, flops, [ext])
            return lax.psum_scatter(total, "dp", scatter_dimension=1, tiled=True), []
        split = (places, TAPS, rows, outs)
        keep, give = call(
            kernel,
            (jax.ShapeDtypeStruct(split, F32), jax.ShapeDtypeStruct(split, BF16)),
            operands,
            flops,
            [ext],
        )
        own, *sends = call(
            pair_sum_kernel,
            (like(shard, F32),) + (like(shard, BF16),) * (places - 1),
            (info, keep, swapped(give, 1)),
            0,
        )
        return own, [swapped(x, 2 * (k + 1)) for k, x in enumerate(sends)]

    own_one, parts_one = scattered(grad_one_kernel, (info, halos, fwd_in, bwd_in, top_cot), conv_flops)

    message, second, edges, weight = call(
        step_one_kernel,
        (tiles(2), tile, line(2), jax.ShapeDtypeStruct((TAPS, channels, outs), BF16)),
        (info, halos, fwd_in, bwd_in, *pieces),
        3 * conv_flops,
        [ext],
    )
    late_back = passed_along(message, -1)
    late_fwd = passed_along(second, 1)

    own_two, parts_two = scattered(grad_two_kernel, (info, swapped(edges, 1), message), conv_flops)
    below = call(gather_sum_kernel, like(shard, BF16), (info, own_two, *parts_two), 0)
    from_above = passed_along(below, -1)

    halos_two = swapped(
        call(edges_two_kernel, line(3), (info, late_fwd, late_back, fresh, fwd_in, top_cot), 0), 1
    )
    fwd_out = call(
        forward_two_kernel,
        like(fwd_in, BF16),
        (info, halos_two, early_fwd, late_fwd, fresh, weight),
        conv_flops,
        [ext],
    )
    bwd_out = call(
        backward_two_kernel,
        like(bwd_in, BF16),
        (info, halos_two, early_back, late_back, second, fwd_in, top_cot, weight),
        2 * conv_flops,
        [ext],
    )
    scale = (2.0 * dp * height * width) ** -0.5
    grad = call(
        functools.partial(finish_kernel, scale), like(shard, F32), (info, own_one, *parts_one, from_above), 0
    )
    return fwd_out, bwd_out, grad.transpose(1, 0, 2)[None]


def solution(mesh):
    in_specs = (
        P(None, "segment", "dp", None, None, None),
        P(None, "segment", "dp", None, None, None),
        P(None, "dp", None, None, None),
        P(None, "dp", None, None, None),
        P("segment", "dp", None, None),
    )
    out_specs = (
        P(None, "segment", "dp", None, None, None),
        P(None, "segment", "dp", None, None, None),
        P("segment", "dp", None, None),
    )
    return jax.shard_map(shards, mesh=mesh, in_specs=in_specs, out_specs=out_specs, check_vma=False)
```

```python
import functools

import jax
import jax.numpy as jnp
from jax import lax
from jax.experimental import pallas as pl
from jax.experimental.pallas import tpu as pltpu
from jax.sharding import PartitionSpec as P

BF16 = jnp.bfloat16
F32 = jnp.float32
VMEM = pl.BlockSpec(memory_space=pltpu.VMEM)
SMEM = pl.BlockSpec(memory_space=pltpu.SMEM)
TAPS = 9
PARITY, FIRST, LAST, PLACE = range(4)
X2, Y1, G2, X1, Y2, G1, FRESH, TOP, LINES = 0, 2, 4, 6, 7, 8, 9, 10, 11
MOST_DIRECT = 4
STEP_TWO = 1


def call(kernel, out_shape, operands, weight=0, scratch=()):
    return pl.pallas_call(
        kernel,
        out_shape=out_shape,
        in_specs=[SMEM] + [VMEM] * (len(operands) - 1),
        out_specs=jax.tree.map(lambda _: VMEM, out_shape),
        scratch_shapes=list(scratch),
        compiler_params=pltpu.CompilerParams(vmem_limit_bytes=32 * 1024 * 1024),
        cost_estimate=pl.CostEstimate(flops=int(weight), bytes_accessed=1, transcendentals=0),
    )(*operands)


def swapped(x, bit):
    return lax.ppermute(x, "dp", [(i, i ^ bit) for i in range(lax.axis_size("dp"))])


def passed_along(block, distance):
    devices = range(lax.axis_size("segment"))
    route = [(i - distance, i) for i in devices if i - distance in devices]
    return lax.ppermute(block, "segment", route)


def after(x, *others):
    return lax.optimization_barrier((x, *others))[0]


def flat(tile):
    return tile.reshape(-1, tile.shape[-1])


def unfold(ext, tile, near, beyond, parity, relu):
    width, channels = near.shape
    blank = jnp.zeros_like(near)
    around = [near] if beyond is None else [near, beyond]
    above = [jnp.where(parity == 1, line, blank) for line in around[::-1]]
    below = [jnp.where(parity == 0, line, blank) for line in around]
    rows = jnp.concatenate(above + [flat(tile)] + below, axis=0)
    if relu:
        rows = jnp.maximum(rows, jnp.zeros_like(rows))
    amount = rows.shape[0]
    wide = rows.astype(F32)
    col = lax.rem(lax.broadcasted_iota(jnp.int32, wide.shape, 0), width)
    left = jnp.where(col == 0, 0.0, pltpu.roll(wide, 1, 0))
    right = jnp.where(col == width - 1, 0.0, pltpu.roll(wide, amount - 1, 0))
    ext[:amount, :channels] = left.astype(BF16)
    ext[:amount, channels : 2 * channels] = rows
    ext[:amount, 2 * channels :] = right.astype(BF16)


def windows(ext, height, width):
    return jnp.concatenate([ext[a * width : (a + height) * width, :] for a in range(3)], axis=1)


def windows_and_near(ext, height, width, parity):
    parts = []
    for a in range(3):
        upper = ext[a * width : (a + 1) * width, :]
        lower = ext[(height + 1 + a) * width : (height + 2 + a) * width, :]
        inside = ext[(a + 1) * width : (a + 1 + height) * width, :]
        parts.append(jnp.concatenate([inside, jnp.where(parity == 0, lower, upper)], axis=0))
    return jnp.concatenate(parts, axis=1)


def conv(wide, weight):
    return jnp.dot(wide, weight[...].reshape(-1, weight.shape[2]), preferred_element_type=F32)


def conv_transposed(wide, weight):
    turned = jnp.concatenate([weight[TAPS - 1 - t] for t in range(TAPS)], axis=1)
    return lax.dot_general(wide, turned, (((1,), (1,)), ((), ())), preferred_element_type=F32)


def grad_into(store, stream, wide):
    lines = flat(stream)
    turned = jnp.maximum(lines, jnp.zeros_like(lines)).astype(F32).T.astype(BF16)
    outs = wide.shape[1] // TAPS
    for t in range(TAPS):
        other = TAPS - 1 - t
        store(t, jnp.dot(turned, wide[:, other * outs : (other + 1) * outs], preferred_element_type=F32))


def storing(info, outs, add):
    if len(outs) == 1:

        def store(t, total):
            outs[0][t] = total + outs[0][t] if add else total

        return store
    keep, give = outs

    def store_halves(t, total):
        parts, _, rows, channels = keep.shape
        cut = total.reshape(parts, 2, rows, channels)
        mine = jnp.where(info[PARITY] == 0, cut[:, 0], cut[:, 1])
        theirs = jnp.where(info[PARITY] == 0, cut[:, 1], cut[:, 0])
        if add:
            mine = mine + keep[:, t]
            theirs = theirs + give[:, t].astype(F32)
        keep[:, t] = mine
        give[:, t] = theirs.astype(BF16)

    return store_halves


def edges_kernel(info, fwd_in, bwd_in, fresh, top_cot, out):
    parity = info[PARITY]

    def put(slot, tile, amount):
        height = tile.shape[0]
        for i in range(amount):
            out[slot + i] = jnp.where(parity == 0, tile[height - 1 - i], tile[i])

    put(X2, fwd_in.at[1, 0, 0], 2)
    put(Y1, bwd_in.at[0, 0, 0], 2)
    put(G2, bwd_in.at[3, 0, 0], 2)
    put(X1, fwd_in.at[0, 0, 0], 1)
    put(Y2, bwd_in.at[1, 0, 0], 1)
    put(G1, bwd_in.at[2, 0, 0], 1)
    put(FRESH, fresh.at[1, 0], 1)
    put(TOP, top_cot.at[1, 0], 1)


def grad_one_kernel(info, lines, fwd_in, bwd_in, top_cot, *rest):
    *outs, ext = rest
    height, width = fwd_in.shape[3:5]
    unfold(ext, bwd_in[3, 0, 0], lines[G2], None, info[PARITY], False)
    grad_into(storing(info, outs, False), bwd_in[0, 0, 0], windows(ext, height, width))

    @pl.when(info[LAST] == 1)
    def _():
        unfold(ext, top_cot[1, 0], lines[TOP], None, info[PARITY], False)
        grad_into(storing(info, outs, True), fwd_in[1, 0, 0], windows(ext, height, width))


def pair_sum_kernel(info, keep, got, own, *sends):
    place = info[PLACE]
    own[...] = keep[place] + got[place].astype(F32)
    for k, send in enumerate(sends):
        there = lax.bitwise_xor(place, k + 1)
        send[...] = (keep[there] + got[there].astype(F32)).astype(BF16)


def step_one_kernel(info, lines, fwd_in, bwd_in, *rest):
    *pieces, message, second, weight, ext = rest
    height, width = fwd_in.shape[3:5]
    parity = info[PARITY]
    if len(pieces) == 1:
        weight[...] = pieces[0][...]
    else:
        rows = pieces[0].shape[1]
        half = len(pieces) // 2
        for k in range(half):
            there = 2 * lax.bitwise_xor(info[PLACE], k)
            for piece, slot in ((pieces[k], there + parity), (pieces[half + k], there + 1 - parity)):
                weight[:, pl.ds(pl.multiple_of(slot * rows, rows), rows), :] = piece[...]
    grown = lambda tile, line: jnp.concatenate([flat(tile), line], axis=0)
    first_out = bwd_in[0, 0, 0]
    unfold(ext, first_out, lines[Y1], lines[Y1 + 1], parity, True)
    branch = conv(windows_and_near(ext, height, width, parity), weight)
    rebuilt = grown(bwd_in[1, 0, 0], lines[Y2]).astype(F32) - branch
    message[0] = rebuilt.astype(BF16)
    unfold(ext, bwd_in[3, 0, 0], lines[G2], lines[G2 + 1], parity, False)
    through = conv_transposed(windows_and_near(ext, height, width, parity), weight)
    kept = jnp.where(grown(first_out, lines[Y1]).astype(F32) > 0, through, 0.0)
    message[1] = (grown(bwd_in[2, 0, 0], lines[G1]).astype(F32) + kept).astype(BF16)
    unfold(ext, fwd_in[1, 0, 0], lines[X2], lines[X2 + 1], parity, True)
    branch = conv(windows_and_near(ext, height, width, parity), weight)
    second[...] = (grown(fwd_in[0, 0, 0], lines[X1]).astype(F32) + branch).astype(BF16)


def grad_two_kernel(height, width, info, message, *rest):
    *outs, ext = rest
    amount = height * width
    unfold(ext, message[1, :amount], message[1, amount:], None, info[PARITY], False)
    grad_into(storing(info, outs, False), message[0, :amount], windows(ext, height, width))


def forward_two_kernel(info, lines, early, second, fresh, weight, out, ext):
    height, width = fresh.shape[2:4]
    amount = height * width
    shape = early.shape
    first = info[FIRST] == 1
    stream = jnp.where(first, flat(fresh[1, 0]), second[:amount])
    near = jnp.where(first, lines[FRESH], second[amount:])
    unfold(ext, stream, near, None, info[PARITY], True)
    out[0, 0, 0] = stream.reshape(shape)
    other = jnp.where(first, fresh[0, 0], early[...])
    branch = conv(windows(ext, height, width), weight).reshape(shape)
    out[1, 0, 0] = (other.astype(F32) + branch).astype(BF16)


def backward_two_kernel(info, lines, early, message, own_second, fwd_in, top_cot, weight, out, ext):
    height, width = top_cot.shape[2:4]
    amount = height * width
    shape = early.shape[1:]
    last = info[LAST] == 1
    out_first = jnp.where(last, flat(fwd_in[1, 0, 0]), message[0, :amount])
    near = jnp.where(last, lines[X2], message[0, amount:])
    out[1, 0, 0] = out_first.reshape(shape)
    unfold(ext, out_first, near, None, info[PARITY], True)
    out_second = jnp.where(last, own_second[:amount], flat(early[0])).reshape(shape)
    branch = conv(windows(ext, height, width), weight).reshape(shape)
    out[0, 0, 0] = (out_second.astype(F32) - branch).astype(BF16)
    cot_second = jnp.where(last, flat(top_cot[1, 0]), message[1, :amount])
    near = jnp.where(last, lines[TOP], message[1, amount:])
    out[2, 0, 0] = cot_second.reshape(shape)
    unfold(ext, cot_second, near, None, info[PARITY], False)
    through = conv_transposed(windows(ext, height, width), weight).reshape(shape)
    cot_first = jnp.where(last, top_cot[0, 0], early[1])
    kept = jnp.where(out[1, 0, 0].astype(F32) > 0, through, 0.0)
    out[3, 0, 0] = (cot_first.astype(F32) + kept).astype(BF16)


def summed(own, parts):
    return functools.reduce(lambda x, y: x + y, [own[...]] + [p[...].astype(F32) for p in parts])


def gather_sum_kernel(info, own, *rest):
    *parts, out = rest
    out[...] = summed(own, parts).astype(BF16)


def finish_kernel(scale, info, own, *rest):
    *parts, out = rest
    out[...] = summed(own, parts) * scale


def shards(fwd_in, bwd_in, fresh, top_cot, conv_weight):
    dp = lax.axis_size("dp")
    places = dp // 2
    dp_pos = lax.axis_index("dp")
    segment_pos = lax.axis_index("segment")
    height, width, channels = fwd_in.shape[3:]
    shard = conv_weight[0].transpose(1, 0, 2)
    rows = shard.shape[1]
    outs = shard.shape[2]
    direct = places <= MOST_DIRECT and rows % 16 == 0
    info = jnp.stack(
        [
            dp_pos % 2,
            (segment_pos == 0).astype(jnp.int32),
            (segment_pos == lax.axis_size("segment") - 1).astype(jnp.int32),
            dp_pos // 2,
        ]
    ).astype(jnp.int32)
    like = lambda x, dtype: jax.ShapeDtypeStruct(x.shape, dtype)
    taller = lambda *lead: jax.ShapeDtypeStruct(lead + ((height + 1) * width, channels), BF16)
    ext = pltpu.VMEM(((height + 4) * width, 3 * channels), BF16)
    conv_flops = 2 * height * width * channels * TAPS * outs

    if direct:
        mine = [shard] + [swapped(shard, 2 * k) for k in range(1, places)]
        pieces = mine + [swapped(x, 1) for x in mine]
    else:
        pieces = [lax.all_gather(shard, "dp", axis=1, tiled=True)]

    early_fwd = passed_along(fwd_in[1, 0, 0], 1)
    early_back = passed_along(jnp.stack([bwd_in[0, 0, 0], bwd_in[3, 0, 0]]), -1)

    lines = jax.ShapeDtypeStruct((LINES, width, channels), BF16)
    lines = swapped(call(edges_kernel, lines, (info, fwd_in, bwd_in, fresh, top_cot)), 1)

    def grads(kernel, operands):
        if not direct:
            return call(kernel, (jax.ShapeDtypeStruct((TAPS, channels, outs), F32),), operands, 1, [ext])
        split = (places, TAPS, rows, outs)
        shape = (jax.ShapeDtypeStruct(split, F32), jax.ShapeDtypeStruct(split, BF16))
        return call(kernel, shape, operands, 1, [ext])

    def scattered(keep, give=None):
        if not direct:
            return lax.psum_scatter(keep, "dp", scatter_dimension=1, tiled=True), []
        shape = (like(shard, F32),) + (like(shard, BF16),) * (places - 1)
        own, *sends = call(pair_sum_kernel, shape, (info, keep, swapped(give, 1)))
        return own, [swapped(x, 2 * (k + 1)) for k, x in enumerate(sends)]

    terms_one = grads(grad_one_kernel, (info, lines, fwd_in, bwd_in, top_cot))

    message, second, weight = call(
        step_one_kernel,
        (taller(2), taller(), jax.ShapeDtypeStruct((TAPS, channels, outs), BF16)),
        (after(info, early_fwd, early_back, terms_one[0]), lines, fwd_in, bwd_in, *pieces),
        1,
        [ext],
    )
    late_back = passed_along(message, -1)
    late_fwd = passed_along(second, 1)

    own_one, parts_one = scattered(*terms_one)
    own_two, parts_two = scattered(*grads(functools.partial(grad_two_kernel, height, width), (info, message)))
    below = call(gather_sum_kernel, like(shard, BF16), (info, own_two, *parts_two))
    from_above = passed_along(below, -1)

    fwd_out = call(
        forward_two_kernel,
        like(fwd_in, BF16),
        (info, lines, early_fwd, late_fwd, fresh, weight),
        STEP_TWO * conv_flops,
        [ext],
    )
    bwd_out = call(
        backward_two_kernel,
        like(bwd_in, BF16),
        (info, lines, early_back, late_back, second, fwd_in, top_cot, weight),
        STEP_TWO * conv_flops,
        [ext],
    )
    scale = (2.0 * dp * height * width) ** -0.5
    finish = functools.partial(finish_kernel, scale)
    grad = call(finish, like(shard, F32), (info, own_one, *parts_one, from_above))
    return fwd_out, bwd_out, grad.transpose(1, 0, 2)[None]


def solution(mesh):
    in_specs = (
        P(None, "segment", "dp", None, None, None),
        P(None, "segment", "dp", None, None, None),
        P(None, "dp", None, None, None),
        P(None, "dp", None, None, None),
        P("segment", "dp", None, None),
    )
    out_specs = (
        P(None, "segment", "dp", None, None, None),
        P(None, "segment", "dp", None, None, None),
        P("segment", "dp", None, None),
    )
    return jax.shard_map(shards, mesh=mesh, in_specs=in_specs, out_specs=out_specs, check_vma=False)
```

```python
import functools

import jax
import jax.numpy as jnp
from jax import lax
from jax.experimental import pallas as pl
from jax.experimental.pallas import tpu as pltpu
from jax.sharding import PartitionSpec as P

BF16 = jnp.bfloat16
F32 = jnp.float32
VMEM = pl.BlockSpec(memory_space=pltpu.VMEM)
SMEM = pl.BlockSpec(memory_space=pltpu.SMEM)
HBM = pl.BlockSpec(memory_space=pltpu.HBM)
TAPS = 9
PARITY, FIRST, LAST, PLACE = range(4)
X2, Y1, G2, X1, Y2, G1, FRESH, TOP, LINES = 0, 2, 4, 6, 7, 8, 9, 10, 11
MOST_DIRECT = 4
STEP_TWO = 1
COLLECT = 10
GRAD_ONE = 0


def call(kernel, out_shape, operands, weight=0, scratch=(), space=VMEM, limit=32):
    return pl.pallas_call(
        kernel,
        out_shape=out_shape,
        in_specs=[SMEM] + [space] * (len(operands) - 1),
        out_specs=jax.tree.map(lambda _: space, out_shape),
        scratch_shapes=list(scratch),
        compiler_params=pltpu.CompilerParams(vmem_limit_bytes=limit * 1024 * 1024),
        cost_estimate=pl.CostEstimate(flops=int(weight), bytes_accessed=1, transcendentals=0),
    )(*operands)


def swapped(x, bit):
    return lax.ppermute(x, "dp", [(i, i ^ bit) for i in range(lax.axis_size("dp"))])


def passed_along(block, distance):
    devices = range(lax.axis_size("segment"))
    route = [(i - distance, i) for i in devices if i - distance in devices]
    return lax.ppermute(block, "segment", route)


def after(x, *others):
    return lax.optimization_barrier((x, *others))[0]


def flat(tile):
    return tile.reshape(-1, tile.shape[-1])


def unfold(ext, tile, near, beyond, parity, relu):
    width, channels = near.shape
    blank = jnp.zeros_like(near)
    around = [near] if beyond is None else [near, beyond]
    above = [jnp.where(parity == 1, line, blank) for line in around[::-1]]
    below = [jnp.where(parity == 0, line, blank) for line in around]
    rows = jnp.concatenate(above + [flat(tile)] + below, axis=0)
    if relu:
        rows = jnp.maximum(rows, jnp.zeros_like(rows))
    amount = rows.shape[0]
    wide = rows.astype(F32)
    col = lax.rem(lax.broadcasted_iota(jnp.int32, wide.shape, 0), width)
    left = jnp.where(col == 0, 0.0, pltpu.roll(wide, 1, 0))
    right = jnp.where(col == width - 1, 0.0, pltpu.roll(wide, amount - 1, 0))
    ext[:amount, :channels] = left.astype(BF16)
    ext[:amount, channels : 2 * channels] = rows
    ext[:amount, 2 * channels :] = right.astype(BF16)


def windows(ext, height, width):
    return jnp.concatenate([ext[a * width : (a + height) * width, :] for a in range(3)], axis=1)


def windows_and_near(ext, height, width, parity):
    parts = []
    for a in range(3):
        upper = ext[a * width : (a + 1) * width, :]
        lower = ext[(height + 1 + a) * width : (height + 2 + a) * width, :]
        inside = ext[(a + 1) * width : (a + 1 + height) * width, :]
        parts.append(jnp.concatenate([inside, jnp.where(parity == 0, lower, upper)], axis=0))
    return jnp.concatenate(parts, axis=1)


def conv(wide, weight):
    return jnp.dot(wide, weight[...].reshape(-1, weight.shape[2]), preferred_element_type=F32)


def conv_transposed(wide, weight):
    turned = jnp.concatenate([weight[TAPS - 1 - t] for t in range(TAPS)], axis=1)
    return lax.dot_general(wide, turned, (((1,), (1,)), ((), ())), preferred_element_type=F32)


def grad_into(store, stream, wide):
    lines = flat(stream)
    turned = jnp.maximum(lines, jnp.zeros_like(lines)).astype(F32).T.astype(BF16)
    outs = wide.shape[1] // TAPS
    for t in range(TAPS):
        other = TAPS - 1 - t
        store(t, jnp.dot(turned, wide[:, other * outs : (other + 1) * outs], preferred_element_type=F32))


def storing(info, outs, add):
    if len(outs) == 1:

        def store(t, total):
            outs[0][t] = total + outs[0][t] if add else total

        return store
    keep, give = outs

    def store_halves(t, total):
        parts, _, rows, channels = keep.shape
        cut = total.reshape(parts, 2, rows, channels)
        mine = jnp.where(info[PARITY] == 0, cut[:, 0], cut[:, 1])
        theirs = jnp.where(info[PARITY] == 0, cut[:, 1], cut[:, 0])
        if add:
            mine = mine + keep[:, t]
            theirs = theirs + give[:, t].astype(F32)
        keep[:, t] = mine
        give[:, t] = theirs.astype(BF16)

    return store_halves


def collect_kernel(info, fwd_in, bwd_in, fresh, top_cot, lines, early_fwd, early_back, sems):
    parity = info[PARITY]
    pairs = [(bwd_in.at[0, 0, 0], early_back.at[0]), (bwd_in.at[3, 0, 0], early_back.at[1])]
    pairs.append((fwd_in.at[1, 0, 0], early_fwd))

    def put(slot, tile, amount):
        height = tile.shape[0]
        for i in range(amount):
            row = jnp.where(parity == 0, height - 1 - i, i)
            pairs.append((tile.at[row], lines.at[slot + i]))

    put(X2, fwd_in.at[1, 0, 0], 2)
    put(Y1, bwd_in.at[0, 0, 0], 2)
    put(G2, bwd_in.at[3, 0, 0], 2)
    put(X1, fwd_in.at[0, 0, 0], 1)
    put(Y2, bwd_in.at[1, 0, 0], 1)
    put(G1, bwd_in.at[2, 0, 0], 1)
    put(FRESH, fresh.at[1, 0], 1)
    put(TOP, top_cot.at[1, 0], 1)
    copies = [pltpu.make_async_copy(source, target, sems.at[i]) for i, (source, target) in enumerate(pairs)]
    for copy in copies:
        copy.start()
    for copy in copies:
        copy.wait()


def grad_one_kernel(info, lines, fwd_in, bwd_in, top_cot, *rest):
    *outs, ext = rest
    height, width = fwd_in.shape[3:5]
    unfold(ext, bwd_in[3, 0, 0], lines[G2], None, info[PARITY], False)
    grad_into(storing(info, outs, False), bwd_in[0, 0, 0], windows(ext, height, width))

    @pl.when(info[LAST] == 1)
    def _():
        unfold(ext, top_cot[1, 0], lines[TOP], None, info[PARITY], False)
        grad_into(storing(info, outs, True), fwd_in[1, 0, 0], windows(ext, height, width))


def pair_sum_kernel(info, keep, got, own, *sends):
    place = info[PLACE]
    own[...] = keep[place] + got[place].astype(F32)
    for k, send in enumerate(sends):
        there = lax.bitwise_xor(place, k + 1)
        send[...] = (keep[there] + got[there].astype(F32)).astype(BF16)


def fold_kernel(info, mine, got, out):
    out[...] = (mine[...].astype(F32) + got[...].astype(F32)).astype(BF16)


def grown(tile, line):
    return jnp.concatenate([flat(tile), line], axis=0)


def backward_one_kernel(info, lines, bwd_in, *rest):
    *pieces, message, weight, ext = rest
    height, width = bwd_in.shape[3:5]
    parity = info[PARITY]
    if len(pieces) == 1:
        weight[...] = pieces[0][...]
    else:
        rows = pieces[0].shape[1]
        half = len(pieces) // 2
        for k in range(half):
            there = 2 * lax.bitwise_xor(info[PLACE], k)
            for piece, slot in ((pieces[k], there + parity), (pieces[half + k], there + 1 - parity)):
                weight[:, pl.ds(pl.multiple_of(slot * rows, rows), rows), :] = piece[...]
    first_out = bwd_in[0, 0, 0]
    unfold(ext, first_out, lines[Y1], lines[Y1 + 1], parity, True)
    branch = conv(windows_and_near(ext, height, width, parity), weight)
    message[0] = (grown(bwd_in[1, 0, 0], lines[Y2]).astype(F32) - branch).astype(BF16)
    unfold(ext, bwd_in[3, 0, 0], lines[G2], lines[G2 + 1], parity, False)
    through = conv_transposed(windows_and_near(ext, height, width, parity), weight)
    kept = jnp.where(grown(first_out, lines[Y1]).astype(F32) > 0, through, 0.0)
    message[1] = (grown(bwd_in[2, 0, 0], lines[G1]).astype(F32) + kept).astype(BF16)


def forward_one_kernel(info, lines, fwd_in, weight, second, ext):
    height, width = fwd_in.shape[3:5]
    parity = info[PARITY]
    unfold(ext, fwd_in[1, 0, 0], lines[X2], lines[X2 + 1], parity, True)
    branch = conv(windows_and_near(ext, height, width, parity), weight)
    second[...] = (grown(fwd_in[0, 0, 0], lines[X1]).astype(F32) + branch).astype(BF16)


def grad_two_kernel(height, width, info, message, *rest):
    *outs, ext = rest
    amount = height * width
    unfold(ext, message[1, :amount], message[1, amount:], None, info[PARITY], False)
    grad_into(storing(info, outs, False), message[0, :amount], windows(ext, height, width))


def forward_two_kernel(info, lines, early, second, fresh, weight, out, ext):
    height, width = fresh.shape[2:4]
    amount = height * width
    shape = early.shape
    first = info[FIRST] == 1
    stream = jnp.where(first, flat(fresh[1, 0]), second[:amount])
    near = jnp.where(first, lines[FRESH], second[amount:])
    unfold(ext, stream, near, None, info[PARITY], True)
    out[0, 0, 0] = stream.reshape(shape)
    other = jnp.where(first, fresh[0, 0], early[...])
    branch = conv(windows(ext, height, width), weight).reshape(shape)
    out[1, 0, 0] = (other.astype(F32) + branch).astype(BF16)


def backward_two_kernel(info, lines, early, message, own_second, fwd_in, top_cot, weight, out, ext):
    height, width = top_cot.shape[2:4]
    amount = height * width
    shape = early.shape[1:]
    last = info[LAST] == 1
    out_first = jnp.where(last, flat(fwd_in[1, 0, 0]), message[0, :amount])
    near = jnp.where(last, lines[X2], message[0, amount:])
    out[1, 0, 0] = out_first.reshape(shape)
    unfold(ext, out_first, near, None, info[PARITY], True)
    out_second = jnp.where(last, own_second[:amount], flat(early[0])).reshape(shape)
    branch = conv(windows(ext, height, width), weight).reshape(shape)
    out[0, 0, 0] = (out_second.astype(F32) - branch).astype(BF16)
    cot_second = jnp.where(last, flat(top_cot[1, 0]), message[1, :amount])
    near = jnp.where(last, lines[TOP], message[1, amount:])
    out[2, 0, 0] = cot_second.reshape(shape)
    unfold(ext, cot_second, near, None, info[PARITY], False)
    through = conv_transposed(windows(ext, height, width), weight).reshape(shape)
    cot_first = jnp.where(last, top_cot[0, 0], early[1])
    kept = jnp.where(out[1, 0, 0].astype(F32) > 0, through, 0.0)
    out[3, 0, 0] = (cot_first.astype(F32) + kept).astype(BF16)


def summed(own, parts):
    return functools.reduce(lambda x, y: x + y, [own[...]] + [p[...].astype(F32) for p in parts])


def gather_sum_kernel(info, own, *rest):
    *parts, out = rest
    out[...] = summed(own, parts).astype(BF16)


def finish_kernel(scale, info, own, *rest):
    *parts, out = rest
    out[...] = summed(own, parts) * scale


def shards(fwd_in, bwd_in, fresh, top_cot, conv_weight):
    dp = lax.axis_size("dp")
    places = dp // 2
    dp_pos = lax.axis_index("dp")
    segment_pos = lax.axis_index("segment")
    height, width, channels = fwd_in.shape[3:]
    shard = conv_weight[0].transpose(1, 0, 2)
    rows = shard.shape[1]
    outs = shard.shape[2]
    direct = places <= MOST_DIRECT and rows % 16 == 0
    info = jnp.stack(
        [
            dp_pos % 2,
            (segment_pos == 0).astype(jnp.int32),
            (segment_pos == lax.axis_size("segment") - 1).astype(jnp.int32),
            dp_pos // 2,
        ]
    ).astype(jnp.int32)
    like = lambda x, dtype: jax.ShapeDtypeStruct(x.shape, dtype)
    taller = lambda *lead: jax.ShapeDtypeStruct(lead + ((height + 1) * width, channels), BF16)
    ext = pltpu.VMEM(((height + 4) * width, 3 * channels), BF16)
    conv_flops = 2 * height * width * channels * TAPS * outs

    if direct:
        mine = [shard]
        for k in range(1, places):
            low = k & -k
            mine.append(swapped(mine[k - low], 2 * low))

    tile = lambda *lead: jax.ShapeDtypeStruct(lead + (height, width, channels), BF16)
    lines, early_fwd, early_back = call(
        collect_kernel,
        (jax.ShapeDtypeStruct((LINES, width, channels), BF16), tile(), tile(2)),
        (info, fwd_in, bwd_in, fresh, top_cot),
        COLLECT * conv_flops,
        [pltpu.SemaphoreType.DMA((LINES + 3,))],
        HBM,
        60,
    )
    lines = swapped(lines, 1)
    early_fwd = passed_along(early_fwd, 1)
    early_back = passed_along(early_back, -1)

    def grads(kernel, operands, weight):
        if not direct:
            return call(kernel, (jax.ShapeDtypeStruct((TAPS, channels, outs), F32),), operands, weight, [ext])
        split = (places, TAPS, rows, outs)
        shape = (jax.ShapeDtypeStruct(split, F32), jax.ShapeDtypeStruct(split, BF16))
        return call(kernel, shape, operands, weight, [ext])

    def scattered(keep, give=None):
        if not direct:
            return lax.psum_scatter(keep, "dp", scatter_dimension=1, tiled=True), []
        shape = (like(shard, F32),) + (like(shard, BF16),) * (places - 1)
        own, *sends = call(pair_sum_kernel, shape, (info, keep, swapped(give, 1)))
        sends = dict(enumerate(sends, 1))
        parts = []
        for k in range(places - 1, 0, -1):
            low = k & -k
            got = swapped(sends[k], 2 * low)
            if k == low:
                parts.append(got)
                continue
            sends[k - low] = call(fold_kernel, like(shard, BF16), (info, sends[k - low], got))
            if low in sends and low != k - low:
                sends[low] = after(sends[low], sends[k - low])
        return own, parts

    terms_one = grads(grad_one_kernel, (info, lines, fwd_in, bwd_in, top_cot), GRAD_ONE * conv_flops)
    if direct:
        others = mine[:-1] + [after(mine[-1], terms_one[0])]
        pieces = mine + [swapped(x, 1) for x in others]
    else:
        pieces = [lax.all_gather(shard, "dp", axis=1, tiled=True)]
    own_one, parts_one = scattered(*terms_one)

    message, weight = call(
        backward_one_kernel,
        (taller(2), jax.ShapeDtypeStruct((TAPS, channels, outs), BF16)),
        (after(info, early_fwd, early_back), lines, bwd_in, *pieces),
        1,
        [ext],
    )
    late_back = passed_along(message, -1)

    terms_two = grads(functools.partial(grad_two_kernel, height, width), (info, message), 1)
    own_two, parts_two = scattered(*terms_two)
    below = call(gather_sum_kernel, like(shard, BF16), (info, own_two, *parts_two))
    from_above = passed_along(below, -1)

    second = call(
        forward_one_kernel,
        taller(),
        (after(info, terms_two[0]), lines, fwd_in, weight),
        1,
        [ext],
    )
    late_fwd = passed_along(second, 1)

    fwd_out = call(
        forward_two_kernel,
        like(fwd_in, BF16),
        (info, lines, early_fwd, late_fwd, fresh, weight),
        STEP_TWO * conv_flops,
        [ext],
    )
    bwd_out = call(
        backward_two_kernel,
        like(bwd_in, BF16),
        (info, lines, early_back, late_back, second, fwd_in, top_cot, weight),
        STEP_TWO * conv_flops,
        [ext],
    )
    scale = (2.0 * dp * height * width) ** -0.5
    finish = functools.partial(finish_kernel, scale)
    grad = call(finish, like(shard, F32), (info, own_one, *parts_one, from_above))
    return fwd_out, bwd_out, grad.transpose(1, 0, 2)[None]


def solution(mesh):
    in_specs = (
        P(None, "segment", "dp", None, None, None),
        P(None, "segment", "dp", None, None, None),
        P(None, "dp", None, None, None),
        P(None, "dp", None, None, None),
        P("segment", "dp", None, None),
    )
    out_specs = (
        P(None, "segment", "dp", None, None, None),
        P(None, "segment", "dp", None, None, None),
        P("segment", "dp", None, None),
    )
    return jax.shard_map(shards, mesh=mesh, in_specs=in_specs, out_specs=out_specs, check_vma=False)
```

```python
import functools

import jax
import jax.numpy as jnp
from jax import lax
from jax.experimental import pallas as pl
from jax.experimental.pallas import tpu as pltpu
from jax.sharding import PartitionSpec as P

BF16 = jnp.bfloat16
F32 = jnp.float32
VMEM = pl.BlockSpec(memory_space=pltpu.VMEM)
SMEM = pl.BlockSpec(memory_space=pltpu.SMEM)
TAPS = 9
PARITY, FIRST, LAST, PLACE, ODD = range(5)
X2, Y1, G2, X1, Y2, G1, FRESH, TOP, LINES = 0, 2, 4, 6, 7, 8, 9, 10, 11
DIRECT = (2, 4, 8)
STEP_TWO = 8
COLLECT = 0
GRAD_ONE = 0


def call(kernel, out_shape, operands, weight=0, scratch=()):
    name = getattr(kernel, "func", kernel).__name__
    return pl.pallas_call(
        kernel,
        name=name,
        out_shape=out_shape,
        in_specs=[SMEM] + [VMEM] * (len(operands) - 1),
        out_specs=jax.tree.map(lambda _: VMEM, out_shape),
        scratch_shapes=list(scratch),
        compiler_params=pltpu.CompilerParams(vmem_limit_bytes=32 * 1024 * 1024),
        cost_estimate=pl.CostEstimate(flops=int(weight), bytes_accessed=1, transcendentals=0),
    )(*operands)


def swapped(x, bit, name="halves"):
    with jax.named_scope(name):
        return lax.ppermute(x, "dp", [(i, i ^ bit) for i in range(lax.axis_size("dp"))])


def passed_along(block, distance, name):
    devices = range(lax.axis_size("segment"))
    routes = [[(i - distance, i) for i in devices if i - distance in devices and i % 2 == odd] for odd in (1, 0)]
    with jax.named_scope(name):
        return [lax.ppermute(block, "segment", route) for route in routes]


def after(x, *others):
    return lax.optimization_barrier((x, *others))[0]


def flat(tile):
    return tile.reshape(-1, tile.shape[-1])


def unfold(ext, tile, near, beyond, parity, relu):
    width, channels = near.shape
    blank = jnp.zeros_like(near)
    around = [near] if beyond is None else [near, beyond]
    above = [jnp.where(parity == 1, line, blank) for line in around[::-1]]
    below = [jnp.where(parity == 0, line, blank) for line in around]
    rows = jnp.concatenate(above + [flat(tile)] + below, axis=0)
    if relu:
        rows = jnp.maximum(rows, jnp.zeros_like(rows))
    amount = rows.shape[0]
    wide = rows.astype(F32)
    col = lax.rem(lax.broadcasted_iota(jnp.int32, wide.shape, 0), width)
    left = jnp.where(col == 0, 0.0, pltpu.roll(wide, 1, 0))
    right = jnp.where(col == width - 1, 0.0, pltpu.roll(wide, amount - 1, 0))
    ext[:amount, :channels] = left.astype(BF16)
    ext[:amount, channels : 2 * channels] = rows
    ext[:amount, 2 * channels :] = right.astype(BF16)


def windows(ext, height, width):
    return jnp.concatenate([ext[a * width : (a + height) * width, :] for a in range(3)], axis=1)


def windows_and_near(ext, height, width, parity):
    parts = []
    for a in range(3):
        upper = ext[a * width : (a + 1) * width, :]
        lower = ext[(height + 1 + a) * width : (height + 2 + a) * width, :]
        inside = ext[(a + 1) * width : (a + 1 + height) * width, :]
        parts.append(jnp.concatenate([inside, jnp.where(parity == 0, lower, upper)], axis=0))
    return jnp.concatenate(parts, axis=1)


def conv(wide, weight):
    return jnp.dot(wide, weight[...].reshape(-1, weight.shape[2]), preferred_element_type=F32)


def conv_transposed(wide, weight):
    turned = jnp.concatenate([weight[TAPS - 1 - t] for t in range(TAPS)], axis=1)
    return lax.dot_general(wide, turned, (((1,), (1,)), ((), ())), preferred_element_type=F32)


def grad_into(store, stream, wide):
    lines = flat(stream)
    turned = jnp.maximum(lines, jnp.zeros_like(lines)).astype(F32).T.astype(BF16)
    outs = wide.shape[1] // TAPS
    for t in range(TAPS):
        other = TAPS - 1 - t
        store(t, jnp.dot(turned, wide[:, other * outs : (other + 1) * outs], preferred_element_type=F32))


def storing(info, outs, add):
    if len(outs) == 1:

        def store(t, total):
            outs[0][t] = total + outs[0][t] if add else total

        return store
    keep, give = outs

    def store_halves(t, total):
        parts, _, rows, channels = keep.shape
        cut = total.reshape(parts, 2, rows, channels)
        mine = jnp.where(info[PARITY] == 0, cut[:, 0], cut[:, 1])
        theirs = jnp.where(info[PARITY] == 0, cut[:, 1], cut[:, 0])
        if add:
            mine = mine + keep[:, t]
            theirs = theirs + give[:, t].astype(F32)
        keep[:, t] = mine
        give[:, t] = theirs.astype(BF16)

    return store_halves


def arrived(info, pair, index):
    return jnp.where(info[ODD] == 1, pair[0][index], pair[1][index])


def collect_kernel(info, fwd_in, bwd_in, fresh, top_cot, lines, early_fwd, early_back):
    parity = info[PARITY]

    def put(slot, tile, amount):
        height = tile.shape[0]
        for i in range(amount):
            lines[slot + i] = jnp.where(parity == 0, tile[height - 1 - i], tile[i])

    put(X2, fwd_in.at[1, 0, 0], 2)
    put(Y1, bwd_in.at[0, 0, 0], 2)
    put(G2, bwd_in.at[3, 0, 0], 2)
    put(X1, fwd_in.at[0, 0, 0], 1)
    put(Y2, bwd_in.at[1, 0, 0], 1)
    put(G1, bwd_in.at[2, 0, 0], 1)
    put(FRESH, fresh.at[1, 0], 1)
    put(TOP, top_cot.at[1, 0], 1)
    early_back[0] = bwd_in[0, 0, 0]
    early_back[1] = bwd_in[3, 0, 0]
    early_fwd[...] = fwd_in[1, 0, 0]


def grad_one_kernel(info, lines, fwd_in, bwd_in, top_cot, *rest):
    *outs, ext = rest
    height, width = fwd_in.shape[3:5]
    unfold(ext, bwd_in[3, 0, 0], lines[G2], None, info[PARITY], False)
    grad_into(storing(info, outs, False), bwd_in[0, 0, 0], windows(ext, height, width))

    @pl.when(info[LAST] == 1)
    def _():
        unfold(ext, top_cot[1, 0], lines[TOP], None, info[PARITY], False)
        grad_into(storing(info, outs, True), fwd_in[1, 0, 0], windows(ext, height, width))


def pair_sum_kernel(info, keep, got, stay, send):
    place = info[PLACE]
    for k in range(stay.shape[0]):
        here, there = lax.bitwise_xor(place, 2 * k), lax.bitwise_xor(place, 2 * k + 1)
        stay[k] = keep[here] + got[here].astype(F32)
        send[k] = (keep[there] + got[there].astype(F32)).astype(BF16)


def fold_kernel(info, held, got, stay, send):
    for k in range(stay.shape[0]):
        stay[k] = held[2 * k] + got[2 * k].astype(F32)
        send[k] = (held[2 * k + 1] + got[2 * k + 1].astype(F32)).astype(BF16)


def grown(tile, line):
    return jnp.concatenate([flat(tile), line], axis=0)


def step_one_kernel(info, lines, fwd_in, bwd_in, *rest):
    *pieces, message, second, weight, ext = rest
    height, width = bwd_in.shape[3:5]
    parity = info[PARITY]
    if len(pieces) == 1:
        weight[...] = pieces[0][...]
    else:
        rows = pieces[0].shape[1]
        half = len(pieces) // 2
        for k in range(half):
            there = 2 * lax.bitwise_xor(info[PLACE], k)
            for piece, slot in ((pieces[k], there + parity), (pieces[half + k], there + 1 - parity)):
                weight[:, pl.ds(pl.multiple_of(slot * rows, rows), rows), :] = piece[...]
    first_out = bwd_in[0, 0, 0]
    unfold(ext, first_out, lines[Y1], lines[Y1 + 1], parity, True)
    branch = conv(windows_and_near(ext, height, width, parity), weight)
    message[0] = (grown(bwd_in[1, 0, 0], lines[Y2]).astype(F32) - branch).astype(BF16)
    unfold(ext, bwd_in[3, 0, 0], lines[G2], lines[G2 + 1], parity, False)
    through = conv_transposed(windows_and_near(ext, height, width, parity), weight)
    kept = jnp.where(grown(first_out, lines[Y1]).astype(F32) > 0, through, 0.0)
    message[1] = (grown(bwd_in[2, 0, 0], lines[G1]).astype(F32) + kept).astype(BF16)
    unfold(ext, fwd_in[1, 0, 0], lines[X2], lines[X2 + 1], parity, True)
    branch = conv(windows_and_near(ext, height, width, parity), weight)
    second[...] = (grown(fwd_in[0, 0, 0], lines[X1]).astype(F32) + branch).astype(BF16)


def grad_two_kernel(height, width, info, message, *rest):
    *outs, ext = rest
    amount = height * width
    unfold(ext, message[1, :amount], message[1, amount:], None, info[PARITY], False)
    grad_into(storing(info, outs, False), message[0, :amount], windows(ext, height, width))


def forward_two_kernel(info, lines, *rest):
    early, second, (fresh, weight, out, ext) = rest[:2], rest[2:4], rest[4:]
    height, width, channels = fresh.shape[2:]
    amount = height * width
    shape = (height, width, channels)
    first = info[FIRST] == 1
    stream = jnp.where(first, flat(fresh[1, 0]), arrived(info, second, pl.ds(0, amount)))
    near = jnp.where(first, lines[FRESH], arrived(info, second, pl.ds(amount, width)))
    unfold(ext, stream, near, None, info[PARITY], True)
    out[0, 0, 0] = stream.reshape(shape)
    other = jnp.where(first, fresh[0, 0], arrived(info, early, ...))
    branch = conv(windows(ext, height, width), weight).reshape(shape)
    out[1, 0, 0] = (other.astype(F32) + branch).astype(BF16)


def backward_two_kernel(info, lines, *rest):
    early, message, (own_second, fwd_in, top_cot, weight, out, ext) = rest[:2], rest[2:4], rest[4:]
    height, width, channels = top_cot.shape[2:]
    amount = height * width
    shape = (height, width, channels)
    last = info[LAST] == 1
    tile, line = pl.ds(0, amount), pl.ds(amount, width)
    out_first = jnp.where(last, flat(fwd_in[1, 0, 0]), arrived(info, message, (0, tile)))
    near = jnp.where(last, lines[X2], arrived(info, message, (0, line)))
    out[1, 0, 0] = out_first.reshape(shape)
    unfold(ext, out_first, near, None, info[PARITY], True)
    out_second = jnp.where(last, own_second[:amount].reshape(shape), arrived(info, early, 0))
    branch = conv(windows(ext, height, width), weight).reshape(shape)
    out[0, 0, 0] = (out_second.astype(F32) - branch).astype(BF16)
    cot_second = jnp.where(last, flat(top_cot[1, 0]), arrived(info, message, (1, tile)))
    near = jnp.where(last, lines[TOP], arrived(info, message, (1, line)))
    out[2, 0, 0] = cot_second.reshape(shape)
    unfold(ext, cot_second, near, None, info[PARITY], False)
    through = conv_transposed(windows(ext, height, width), weight).reshape(shape)
    cot_first = jnp.where(last, top_cot[0, 0], arrived(info, early, 1))
    kept = jnp.where(out[1, 0, 0].astype(F32) > 0, through, 0.0)
    out[3, 0, 0] = (cot_first.astype(F32) + kept).astype(BF16)


def summed(own, parts):
    return functools.reduce(lambda x, y: x + y, [own[...]] + [p[...].astype(F32) for p in parts])


def gather_sum_kernel(info, own, *rest):
    *parts, out = rest
    out[...] = summed(own, parts).astype(BF16)


def finish_kernel(scale, info, own, *rest):
    *parts, out = rest
    out[...] = summed(own, parts) * scale


def shards(fwd_in, bwd_in, fresh, top_cot, conv_weight):
    dp = lax.axis_size("dp")
    places = dp // 2
    dp_pos = lax.axis_index("dp")
    segment_pos = lax.axis_index("segment")
    height, width, channels = fwd_in.shape[3:]
    shard = conv_weight[0].transpose(1, 0, 2)
    rows = shard.shape[1]
    outs = shard.shape[2]
    direct = places in DIRECT and rows % 16 == 0
    info = jnp.stack(
        [
            dp_pos % 2,
            (segment_pos == 0).astype(jnp.int32),
            (segment_pos == lax.axis_size("segment") - 1).astype(jnp.int32),
            dp_pos // 2,
            segment_pos % 2,
        ]
    ).astype(jnp.int32)
    like = lambda x, dtype: jax.ShapeDtypeStruct(x.shape, dtype)
    taller = lambda *lead: jax.ShapeDtypeStruct(lead + ((height + 1) * width, channels), BF16)
    ext = pltpu.VMEM(((height + 4) * width, 3 * channels), BF16)
    conv_flops = 2 * height * width * channels * TAPS * outs

    if direct:
        mine = [shard]
        for k in range(1, places):
            low = k & -k
            source = mine[k - low] if low == k else after(mine[k - low], mine[low])
            mine.append(swapped(source, 2 * low, "weight_z%d" % k))

    tile = lambda *lead: jax.ShapeDtypeStruct(lead + (height, width, channels), BF16)
    lines, early_fwd, early_back = call(
        collect_kernel,
        (jax.ShapeDtypeStruct((LINES, width, channels), BF16), tile(), tile(2)),
        (info, fwd_in, bwd_in, fresh, top_cot),
        COLLECT * conv_flops,
    )
    lines = swapped(lines, 1, "lines")
    early_back = passed_along(early_back, -1, "early_back")

    def grads(kernel, operands, weight):
        if not direct:
            return call(kernel, (jax.ShapeDtypeStruct((TAPS, channels, outs), F32),), operands, weight, [ext])
        split = (places, TAPS, rows, outs)
        shape = (jax.ShapeDtypeStruct(split, F32), jax.ShapeDtypeStruct(split, BF16))
        return call(kernel, shape, operands, weight, [ext])

    def scattered(name, keep, give=None, hold=()):
        if not direct:
            return lax.psum_scatter(keep, "dp", scatter_dimension=1, tiled=True), []
        amount = places // 2
        shape = lambda dtype: jax.ShapeDtypeStruct((amount,) + shard.shape, dtype)
        got = swapped(give, 1, name)
        stay, send = call(pair_sum_kernel, (shape(F32), shape(BF16)), (after(info, *hold[:1]), keep, got))
        bit = 2
        while amount > 1:
            got = swapped(send, bit, name + "_near")
            amount, bit = amount // 2, 2 * bit
            stay, send = call(fold_kernel, (shape(F32), shape(BF16)), (after(info, *hold[1:]), stay, got))
        return stay[0], [swapped(send, bit, name + "_far")[0]]

    terms_one = grads(grad_one_kernel, (info, lines, fwd_in, bwd_in, top_cot), GRAD_ONE * conv_flops)
    early_fwd = passed_along(after(early_fwd, terms_one[0]), 1, "early_fwd")
    if direct:
        others = mine[:-1] + [after(mine[-1], terms_one[0])]
        pieces = mine + [swapped(x, 1, "weight_core%d" % k) for k, x in enumerate(others)]
    else:
        pieces = [lax.all_gather(shard, "dp", axis=1, tiled=True)]

    message, second, weight = call(
        step_one_kernel,
        (taller(2), taller(), jax.ShapeDtypeStruct((TAPS, channels, outs), BF16)),
        (after(info, *early_back), lines, fwd_in, bwd_in, *pieces),
        1,
        [ext],
    )
    late_back = passed_along(message, -1, "late_back")
    late_fwd = passed_along(second, 1, "late_fwd")

    terms_two = grads(functools.partial(grad_two_kernel, height, width), (after(info, *early_fwd), message), 1)
    own_two, parts_two = scattered("term_two", *terms_two)
    below = call(gather_sum_kernel, like(shard, BF16), (info, own_two, *parts_two))
    from_above = passed_along(below, -1, "below")
    own_one, parts_one = scattered("term_one", *terms_one, hold=(own_two, below))

    fwd_out = call(
        forward_two_kernel,
        like(fwd_in, BF16),
        (info, lines, *early_fwd, *late_fwd, fresh, weight),
        STEP_TWO * conv_flops,
        [ext],
    )
    bwd_out = call(
        backward_two_kernel,
        like(bwd_in, BF16),
        (info, lines, *early_back, *late_back, second, fwd_in, top_cot, weight),
        STEP_TWO * conv_flops,
        [ext],
    )
    scale = (2.0 * dp * height * width) ** -0.5
    finish = functools.partial(finish_kernel, scale)
    grad = call(finish, like(shard, F32), (info, own_one, *parts_one, *from_above))
    return fwd_out, bwd_out, grad.transpose(1, 0, 2)[None]


def solution(mesh):
    in_specs = (
        P(None, "segment", "dp", None, None, None),
        P(None, "segment", "dp", None, None, None),
        P(None, "dp", None, None, None),
        P(None, "dp", None, None, None),
        P("segment", "dp", None, None),
    )
    out_specs = (
        P(None, "segment", "dp", None, None, None),
        P(None, "segment", "dp", None, None, None),
        P("segment", "dp", None, None),
    )
    return jax.shard_map(shards, mesh=mesh, in_specs=in_specs, out_specs=out_specs, check_vma=False)
```

```python
import functools

import jax
import jax.numpy as jnp
from jax import lax
from jax.experimental import pallas as pl
from jax.experimental.pallas import tpu as pltpu
from jax.sharding import PartitionSpec as P

BF16 = jnp.bfloat16
F32 = jnp.float32
VMEM = pl.BlockSpec(memory_space=pltpu.VMEM)
SMEM = pl.BlockSpec(memory_space=pltpu.SMEM)
TAPS = 9
PARITY, FIRST, LAST, PLACE = range(4)
X2, Y1, G2, X1, Y2, G1, FRESH, TOP, LINES = 0, 2, 4, 6, 7, 8, 9, 10, 11
DIRECT = (2, 4, 8)
STEP_TWO = 3
COLLECT = 0
GRAD_ONE = 0


def call(kernel, out_shape, operands, weight=0, scratch=()):
    name = getattr(kernel, "func", kernel).__name__
    return pl.pallas_call(
        kernel,
        name=name,
        out_shape=out_shape,
        in_specs=[SMEM] + [VMEM] * (len(operands) - 1),
        out_specs=jax.tree.map(lambda _: VMEM, out_shape),
        scratch_shapes=list(scratch),
        compiler_params=pltpu.CompilerParams(vmem_limit_bytes=32 * 1024 * 1024),
        cost_estimate=pl.CostEstimate(flops=int(weight), bytes_accessed=1, transcendentals=0),
    )(*operands)


def swapped(x, bit, name="halves"):
    with jax.named_scope(name):
        return lax.ppermute(x, "dp", [(i, i ^ bit) for i in range(lax.axis_size("dp"))])


def passed_along(block, distance, name):
    devices = range(lax.axis_size("segment"))
    route = [(i - distance, i) for i in devices if i - distance in devices]
    with jax.named_scope(name):
        return lax.ppermute(block, "segment", route)


def after(x, *others):
    return lax.optimization_barrier((x, *others))[0]


def flat(tile):
    return tile.reshape(-1, tile.shape[-1])


def unfold(ext, tile, near, beyond, parity, relu):
    width, channels = near.shape
    blank = jnp.zeros_like(near)
    around = [near] if beyond is None else [near, beyond]
    above = [jnp.where(parity == 1, line, blank) for line in around[::-1]]
    below = [jnp.where(parity == 0, line, blank) for line in around]
    rows = jnp.concatenate(above + [flat(tile)] + below, axis=0)
    if relu:
        rows = jnp.maximum(rows, jnp.zeros_like(rows))
    amount = rows.shape[0]
    wide = rows.astype(F32)
    col = lax.rem(lax.broadcasted_iota(jnp.int32, wide.shape, 0), width)
    left = jnp.where(col == 0, 0.0, pltpu.roll(wide, 1, 0))
    right = jnp.where(col == width - 1, 0.0, pltpu.roll(wide, amount - 1, 0))
    ext[:amount, :channels] = left.astype(BF16)
    ext[:amount, channels : 2 * channels] = rows
    ext[:amount, 2 * channels :] = right.astype(BF16)


def windows(ext, height, width):
    return jnp.concatenate([ext[a * width : (a + height) * width, :] for a in range(3)], axis=1)


def windows_and_near(ext, height, width, parity):
    parts = []
    for a in range(3):
        upper = ext[a * width : (a + 1) * width, :]
        lower = ext[(height + 1 + a) * width : (height + 2 + a) * width, :]
        inside = ext[(a + 1) * width : (a + 1 + height) * width, :]
        parts.append(jnp.concatenate([inside, jnp.where(parity == 0, lower, upper)], axis=0))
    return jnp.concatenate(parts, axis=1)


def conv(wide, weight):
    return jnp.dot(wide, weight[...].reshape(-1, weight.shape[2]), preferred_element_type=F32)


def conv_transposed(wide, weight):
    turned = jnp.concatenate([weight[TAPS - 1 - t] for t in range(TAPS)], axis=1)
    return lax.dot_general(wide, turned, (((1,), (1,)), ((), ())), preferred_element_type=F32)


def grad_into(store, stream, wide):
    lines = flat(stream)
    turned = jnp.maximum(lines, jnp.zeros_like(lines)).astype(F32).T.astype(BF16)
    outs = wide.shape[1] // TAPS
    for t in range(TAPS):
        other = TAPS - 1 - t
        store(t, jnp.dot(turned, wide[:, other * outs : (other + 1) * outs], preferred_element_type=F32))


def storing(info, outs, add):
    if len(outs) == 1:

        def store(t, total):
            outs[0][t] = total + outs[0][t] if add else total

        return store
    keep, give = outs

    def store_halves(t, total):
        parts, _, rows, channels = keep.shape
        cut = total.reshape(parts, 2, rows, channels)
        mine = jnp.where(info[PARITY] == 0, cut[:, 0], cut[:, 1])
        theirs = jnp.where(info[PARITY] == 0, cut[:, 1], cut[:, 0])
        if add:
            mine = mine + keep[:, t]
            theirs = theirs + give[:, t].astype(F32)
        keep[:, t] = mine
        give[:, t] = theirs.astype(BF16)

    return store_halves


def collect_kernel(info, fwd_in, bwd_in, fresh, top_cot, lines, early_fwd, early_back):
    parity = info[PARITY]

    def put(slot, tile, amount):
        height = tile.shape[0]
        for i in range(amount):
            lines[slot + i] = jnp.where(parity == 0, tile[height - 1 - i], tile[i])

    put(X2, fwd_in.at[1, 0, 0], 2)
    put(Y1, bwd_in.at[0, 0, 0], 2)
    put(G2, bwd_in.at[3, 0, 0], 2)
    put(X1, fwd_in.at[0, 0, 0], 1)
    put(Y2, bwd_in.at[1, 0, 0], 1)
    put(G1, bwd_in.at[2, 0, 0], 1)
    put(FRESH, fresh.at[1, 0], 1)
    put(TOP, top_cot.at[1, 0], 1)
    early_back[0] = bwd_in[0, 0, 0]
    early_back[1] = bwd_in[3, 0, 0]
    early_fwd[...] = fwd_in[1, 0, 0]


def grad_one_kernel(info, lines, fwd_in, bwd_in, top_cot, *rest):
    *outs, ext = rest
    height, width = fwd_in.shape[3:5]
    unfold(ext, bwd_in[3, 0, 0], lines[G2], None, info[PARITY], False)
    grad_into(storing(info, outs, False), bwd_in[0, 0, 0], windows(ext, height, width))

    @pl.when(info[LAST] == 1)
    def _():
        unfold(ext, top_cot[1, 0], lines[TOP], None, info[PARITY], False)
        grad_into(storing(info, outs, True), fwd_in[1, 0, 0], windows(ext, height, width))


def pair_sum_kernel(info, keep, got, stay, send):
    place = info[PLACE]
    for k in range(stay.shape[0]):
        here, there = lax.bitwise_xor(place, 2 * k), lax.bitwise_xor(place, 2 * k + 1)
        stay[k] = keep[here] + got[here].astype(F32)
        send[k] = (keep[there] + got[there].astype(F32)).astype(BF16)


def fold_kernel(info, held, got, stay, send):
    for k in range(stay.shape[0]):
        stay[k] = held[2 * k] + got[2 * k].astype(F32)
        send[k] = (held[2 * k + 1] + got[2 * k + 1].astype(F32)).astype(BF16)


def grown(tile, line):
    return jnp.concatenate([flat(tile), line], axis=0)


def step_one_kernel(info, lines, fwd_in, bwd_in, *rest):
    *pieces, message, second, weight, ext = rest
    height, width = bwd_in.shape[3:5]
    parity = info[PARITY]
    if len(pieces) == 1:
        weight[...] = pieces[0][...]
    else:
        rows = pieces[0].shape[1]
        half = len(pieces) // 2
        for k in range(half):
            there = 2 * lax.bitwise_xor(info[PLACE], k)
            for piece, slot in ((pieces[k], there + parity), (pieces[half + k], there + 1 - parity)):
                weight[:, pl.ds(pl.multiple_of(slot * rows, rows), rows), :] = piece[...]
    first_out = bwd_in[0, 0, 0]
    unfold(ext, first_out, lines[Y1], lines[Y1 + 1], parity, True)
    branch = conv(windows_and_near(ext, height, width, parity), weight)
    message[0] = (grown(bwd_in[1, 0, 0], lines[Y2]).astype(F32) - branch).astype(BF16)
    unfold(ext, bwd_in[3, 0, 0], lines[G2], lines[G2 + 1], parity, False)
    through = conv_transposed(windows_and_near(ext, height, width, parity), weight)
    kept = jnp.where(grown(first_out, lines[Y1]).astype(F32) > 0, through, 0.0)
    message[1] = (grown(bwd_in[2, 0, 0], lines[G1]).astype(F32) + kept).astype(BF16)
    unfold(ext, fwd_in[1, 0, 0], lines[X2], lines[X2 + 1], parity, True)
    branch = conv(windows_and_near(ext, height, width, parity), weight)
    second[...] = (grown(fwd_in[0, 0, 0], lines[X1]).astype(F32) + branch).astype(BF16)


def grad_two_kernel(height, width, info, message, *rest):
    *outs, ext = rest
    amount = height * width
    unfold(ext, message[1, :amount], message[1, amount:], None, info[PARITY], False)
    grad_into(storing(info, outs, False), message[0, :amount], windows(ext, height, width))


def forward_two_kernel(info, lines, early, second, fresh, weight, out, ext):
    height, width = fresh.shape[2:4]
    amount = height * width
    shape = early.shape
    first = info[FIRST] == 1
    stream = jnp.where(first, flat(fresh[1, 0]), second[:amount])
    near = jnp.where(first, lines[FRESH], second[amount:])
    unfold(ext, stream, near, None, info[PARITY], True)
    out[0, 0, 0] = stream.reshape(shape)
    other = jnp.where(first, fresh[0, 0], early[...])
    branch = conv(windows(ext, height, width), weight).reshape(shape)
    out[1, 0, 0] = (other.astype(F32) + branch).astype(BF16)


def backward_two_kernel(info, lines, early, message, own_second, fwd_in, top_cot, weight, out, ext):
    height, width = top_cot.shape[2:4]
    amount = height * width
    shape = early.shape[1:]
    last = info[LAST] == 1
    out_first = jnp.where(last, flat(fwd_in[1, 0, 0]), message[0, :amount])
    near = jnp.where(last, lines[X2], message[0, amount:])
    out[1, 0, 0] = out_first.reshape(shape)
    unfold(ext, out_first, near, None, info[PARITY], True)
    out_second = jnp.where(last, own_second[:amount], flat(early[0])).reshape(shape)
    branch = conv(windows(ext, height, width), weight).reshape(shape)
    out[0, 0, 0] = (out_second.astype(F32) - branch).astype(BF16)
    cot_second = jnp.where(last, flat(top_cot[1, 0]), message[1, :amount])
    near = jnp.where(last, lines[TOP], message[1, amount:])
    out[2, 0, 0] = cot_second.reshape(shape)
    unfold(ext, cot_second, near, None, info[PARITY], False)
    through = conv_transposed(windows(ext, height, width), weight).reshape(shape)
    cot_first = jnp.where(last, top_cot[0, 0], early[1])
    kept = jnp.where(out[1, 0, 0].astype(F32) > 0, through, 0.0)
    out[3, 0, 0] = (cot_first.astype(F32) + kept).astype(BF16)


def summed(own, parts):
    return functools.reduce(lambda x, y: x + y, [own[...]] + [p[...].astype(F32) for p in parts])


def gather_sum_kernel(info, own, *rest):
    *parts, out = rest
    out[...] = summed(own, parts).astype(BF16)


def finish_kernel(scale, info, own, *rest):
    *parts, out = rest
    out[...] = summed(own, parts) * scale


def shards(fwd_in, bwd_in, fresh, top_cot, conv_weight):
    dp = lax.axis_size("dp")
    places = dp // 2
    dp_pos = lax.axis_index("dp")
    segment_pos = lax.axis_index("segment")
    height, width, channels = fwd_in.shape[3:]
    shard = conv_weight[0].transpose(1, 0, 2)
    rows = shard.shape[1]
    outs = shard.shape[2]
    direct = places in DIRECT and rows % 16 == 0
    info = jnp.stack(
        [
            dp_pos % 2,
            (segment_pos == 0).astype(jnp.int32),
            (segment_pos == lax.axis_size("segment") - 1).astype(jnp.int32),
            dp_pos // 2,
        ]
    ).astype(jnp.int32)
    like = lambda x, dtype: jax.ShapeDtypeStruct(x.shape, dtype)
    taller = lambda *lead: jax.ShapeDtypeStruct(lead + ((height + 1) * width, channels), BF16)
    ext = pltpu.VMEM(((height + 4) * width, 3 * channels), BF16)
    conv_flops = 2 * height * width * channels * TAPS * outs

    if direct:
        mine = [shard]
        for k in range(1, places):
            low = k & -k
            source = mine[k - low] if low == k else after(mine[k - low], mine[low])
            mine.append(swapped(source, 2 * low, "weight_z%d" % k))

    tile = lambda *lead: jax.ShapeDtypeStruct(lead + (height, width, channels), BF16)
    lines, early_fwd, early_back = call(
        collect_kernel,
        (jax.ShapeDtypeStruct((LINES, width, channels), BF16), tile(), tile(2)),
        (info, fwd_in, bwd_in, fresh, top_cot),
        COLLECT * conv_flops,
    )
    lines = swapped(lines, 1, "lines")
    early_back = passed_along(early_back, -1, "early_back")

    def grads(kernel, operands, weight):
        if not direct:
            return call(kernel, (jax.ShapeDtypeStruct((TAPS, channels, outs), F32),), operands, weight, [ext])
        split = (places, TAPS, rows, outs)
        shape = (jax.ShapeDtypeStruct(split, F32), jax.ShapeDtypeStruct(split, BF16))
        return call(kernel, shape, operands, weight, [ext])

    def scattered(name, keep, give=None, hold=()):
        if not direct:
            return lax.psum_scatter(keep, "dp", scatter_dimension=1, tiled=True), []
        amount = places // 2
        shape = lambda dtype: jax.ShapeDtypeStruct((amount,) + shard.shape, dtype)
        got = swapped(give, 1, name)
        stay, send = call(pair_sum_kernel, (shape(F32), shape(BF16)), (after(info, *hold[:1]), keep, got))
        bit = 2
        while amount > 1:
            got = swapped(send, bit, name + "_near")
            amount, bit = amount // 2, 2 * bit
            stay, send = call(fold_kernel, (shape(F32), shape(BF16)), (after(info, *hold[1:]), stay, got))
        return stay[0], [swapped(send, bit, name + "_far")[0]]

    terms_one = grads(grad_one_kernel, (info, lines, fwd_in, bwd_in, top_cot), GRAD_ONE * conv_flops)
    if direct:
        others = mine[:-1] + [after(mine[-1], terms_one[0])]
        pieces = mine + [swapped(x, 1, "weight_core%d" % k) for k, x in enumerate(others)]
        early_fwd = after(early_fwd, pieces[-2])
    else:
        pieces = [lax.all_gather(shard, "dp", axis=1, tiled=True)]

    early_fwd = passed_along(early_fwd, 1, "early_fwd")

    message, second, weight = call(
        step_one_kernel,
        (taller(2), taller(), jax.ShapeDtypeStruct((TAPS, channels, outs), BF16)),
        (after(info, early_back), lines, fwd_in, bwd_in, *pieces),
        1,
        [ext],
    )
    late_back = passed_along(message, -1, "late_back")
    late_fwd = passed_along(second, 1, "late_fwd")

    terms_two = grads(functools.partial(grad_two_kernel, height, width), (after(info, early_fwd), message), 1)
    own_one, parts_one = scattered("term_one", *terms_one)
    own_two, parts_two = scattered("term_two", *terms_two)
    below = call(gather_sum_kernel, like(shard, BF16), (info, own_two, *parts_two))
    from_above = passed_along(below, -1, "below")

    fwd_out = call(
        forward_two_kernel,
        like(fwd_in, BF16),
        (info, lines, early_fwd, late_fwd, fresh, weight),
        STEP_TWO * conv_flops,
        [ext],
    )
    bwd_out = call(
        backward_two_kernel,
        like(bwd_in, BF16),
        (info, lines, early_back, late_back, second, fwd_in, top_cot, weight),
        STEP_TWO * conv_flops,
        [ext],
    )
    scale = (2.0 * dp * height * width) ** -0.5
    finish = functools.partial(finish_kernel, scale)
    grad = call(finish, like(shard, F32), (info, own_one, *parts_one, from_above))
    return fwd_out, bwd_out, grad.transpose(1, 0, 2)[None]


def solution(mesh):
    in_specs = (
        P(None, "segment", "dp", None, None, None),
        P(None, "segment", "dp", None, None, None),
        P(None, "dp", None, None, None),
        P(None, "dp", None, None, None),
        P("segment", "dp", None, None),
    )
    out_specs = (
        P(None, "segment", "dp", None, None, None),
        P(None, "segment", "dp", None, None, None),
        P("segment", "dp", None, None),
    )
    return jax.shard_map(shards, mesh=mesh, in_specs=in_specs, out_specs=out_specs, check_vma=False)
```

```python
import functools

import jax
import jax.numpy as jnp
from jax import lax
from jax.experimental import pallas as pl
from jax.experimental.pallas import tpu as pltpu
from jax.sharding import PartitionSpec as P

BF16 = jnp.bfloat16
F32 = jnp.float32
VMEM = pl.BlockSpec(memory_space=pltpu.VMEM)
SMEM = pl.BlockSpec(memory_space=pltpu.SMEM)
TAPS = 9
PARITY, FIRST, LAST, PLACE = range(4)
X2, Y1, G2, X1, Y2, G1, FRESH, TOP, LINES = 0, 2, 4, 6, 7, 8, 9, 10, 11
DIRECT = (2, 4, 8)
STEP_TWO = 3
COLLECT = 0
GRAD_ONE = 3


def call(kernel, out_shape, operands, weight=0, scratch=(), limit=32):
    name = getattr(kernel, "func", kernel).__name__
    return pl.pallas_call(
        kernel,
        name=name,
        out_shape=out_shape,
        in_specs=[SMEM] + [VMEM] * (len(operands) - 1),
        out_specs=jax.tree.map(lambda _: VMEM, out_shape),
        scratch_shapes=list(scratch),
        compiler_params=pltpu.CompilerParams(vmem_limit_bytes=limit * 1024 * 1024),
        cost_estimate=pl.CostEstimate(flops=int(weight), bytes_accessed=1, transcendentals=0),
    )(*operands)


def swapped(x, bit, name="halves"):
    with jax.named_scope(name):
        return lax.ppermute(x, "dp", [(i, i ^ bit) for i in range(lax.axis_size("dp"))])


def passed_along(block, distance, name):
    devices = range(lax.axis_size("segment"))
    route = [(i - distance, i) for i in devices if i - distance in devices]
    with jax.named_scope(name):
        return lax.ppermute(block, "segment", route)


def after(x, *others):
    return lax.optimization_barrier((x, *others))[0]


def flat(tile):
    return tile.reshape(-1, tile.shape[-1])


def unfold(ext, tile, near, beyond, parity, relu):
    width, channels = near.shape
    blank = jnp.zeros_like(near)
    around = [near] if beyond is None else [near, beyond]
    above = [jnp.where(parity == 1, line, blank) for line in around[::-1]]
    below = [jnp.where(parity == 0, line, blank) for line in around]
    rows = jnp.concatenate(above + [flat(tile)] + below, axis=0)
    if relu:
        rows = jnp.maximum(rows, jnp.zeros_like(rows))
    amount = rows.shape[0]
    wide = rows.astype(F32)
    col = lax.rem(lax.broadcasted_iota(jnp.int32, wide.shape, 0), width)
    left = jnp.where(col == 0, 0.0, pltpu.roll(wide, 1, 0))
    right = jnp.where(col == width - 1, 0.0, pltpu.roll(wide, amount - 1, 0))
    ext[:amount, :channels] = left.astype(BF16)
    ext[:amount, channels : 2 * channels] = rows
    ext[:amount, 2 * channels :] = right.astype(BF16)


def windows(ext, height, width):
    return jnp.concatenate([ext[a * width : (a + height) * width, :] for a in range(3)], axis=1)


def windows_and_near(ext, height, width, parity):
    parts = []
    for a in range(3):
        upper = ext[a * width : (a + 1) * width, :]
        lower = ext[(height + 1 + a) * width : (height + 2 + a) * width, :]
        inside = ext[(a + 1) * width : (a + 1 + height) * width, :]
        parts.append(jnp.concatenate([inside, jnp.where(parity == 0, lower, upper)], axis=0))
    return jnp.concatenate(parts, axis=1)


def conv(wide, weight):
    return jnp.dot(wide, weight[...].reshape(-1, weight.shape[2]), preferred_element_type=F32)


def conv_transposed(wide, weight):
    turned = jnp.concatenate([weight[TAPS - 1 - t] for t in range(TAPS)], axis=1)
    return lax.dot_general(wide, turned, (((1,), (1,)), ((), ())), preferred_element_type=F32)


def grad_into(store, stream, wide):
    lines = flat(stream)
    turned = jnp.maximum(lines, jnp.zeros_like(lines)).astype(F32).T.astype(BF16)
    outs = wide.shape[1] // TAPS
    for t in range(TAPS):
        other = TAPS - 1 - t
        store(t, jnp.dot(turned, wide[:, other * outs : (other + 1) * outs], preferred_element_type=F32))


def storing(info, outs, add):
    if len(outs) == 1:

        def store(t, total):
            outs[0][t] = total + outs[0][t] if add else total

        return store
    keep, give = outs

    def store_halves(t, total):
        parts, _, rows, channels = keep.shape
        cut = total.reshape(parts, 2, rows, channels)
        mine = jnp.where(info[PARITY] == 0, cut[:, 0], cut[:, 1])
        theirs = jnp.where(info[PARITY] == 0, cut[:, 1], cut[:, 0])
        if add:
            mine = mine + keep[:, t]
            theirs = theirs + give[:, t].astype(F32)
        keep[:, t] = mine
        give[:, t] = theirs.astype(BF16)

    return store_halves


def collect_kernel(info, fwd_in, bwd_in, fresh, top_cot, lines, early_fwd, early_back):
    parity = info[PARITY]

    def put(slot, tile, amount):
        height = tile.shape[0]
        for i in range(amount):
            lines[slot + i] = jnp.where(parity == 0, tile[height - 1 - i], tile[i])

    put(X2, fwd_in.at[1, 0, 0], 2)
    put(Y1, bwd_in.at[0, 0, 0], 2)
    put(G2, bwd_in.at[3, 0, 0], 2)
    put(X1, fwd_in.at[0, 0, 0], 1)
    put(Y2, bwd_in.at[1, 0, 0], 1)
    put(G1, bwd_in.at[2, 0, 0], 1)
    put(FRESH, fresh.at[1, 0], 1)
    put(TOP, top_cot.at[1, 0], 1)
    early_back[0] = bwd_in[0, 0, 0]
    early_back[1] = bwd_in[3, 0, 0]
    early_fwd[...] = fwd_in[1, 0, 0]


def grad_one_kernel(info, lines, fwd_in, bwd_in, top_cot, *rest):
    *outs, ext = rest
    height, width = fwd_in.shape[3:5]
    unfold(ext, bwd_in[3, 0, 0], lines[G2], None, info[PARITY], False)
    grad_into(storing(info, outs, False), bwd_in[0, 0, 0], windows(ext, height, width))

    @pl.when(info[LAST] == 1)
    def _():
        unfold(ext, top_cot[1, 0], lines[TOP], None, info[PARITY], False)
        grad_into(storing(info, outs, True), fwd_in[1, 0, 0], windows(ext, height, width))


def pair_sum_kernel(info, keep, got, stay, send):
    place = info[PLACE]
    for k in range(stay.shape[0]):
        here, there = lax.bitwise_xor(place, 2 * k), lax.bitwise_xor(place, 2 * k + 1)
        stay[k] = keep[here] + got[here].astype(F32)
        send[k] = (keep[there] + got[there].astype(F32)).astype(BF16)


def fold_kernel(info, held, got, stay, send):
    for k in range(stay.shape[0]):
        stay[k] = held[2 * k] + got[2 * k].astype(F32)
        send[k] = (held[2 * k + 1] + got[2 * k + 1].astype(F32)).astype(BF16)


def grown(tile, line):
    return jnp.concatenate([flat(tile), line], axis=0)


def step_one_kernel(info, lines, fwd_in, bwd_in, *rest):
    *pieces, message, second, weight, ext = rest
    height, width = bwd_in.shape[3:5]
    parity = info[PARITY]
    if len(pieces) == 1:
        weight[...] = pieces[0][...]
    else:
        rows = pieces[0].shape[1]
        half = len(pieces) // 2
        for k in range(half):
            there = 2 * lax.bitwise_xor(info[PLACE], k)
            for piece, slot in ((pieces[k], there + parity), (pieces[half + k], there + 1 - parity)):
                weight[:, pl.ds(pl.multiple_of(slot * rows, rows), rows), :] = piece[...]
    first_out = bwd_in[0, 0, 0]
    unfold(ext, first_out, lines[Y1], lines[Y1 + 1], parity, True)
    branch = conv(windows_and_near(ext, height, width, parity), weight)
    message[0] = (grown(bwd_in[1, 0, 0], lines[Y2]).astype(F32) - branch).astype(BF16)
    unfold(ext, bwd_in[3, 0, 0], lines[G2], lines[G2 + 1], parity, False)
    through = conv_transposed(windows_and_near(ext, height, width, parity), weight)
    kept = jnp.where(grown(first_out, lines[Y1]).astype(F32) > 0, through, 0.0)
    message[1] = (grown(bwd_in[2, 0, 0], lines[G1]).astype(F32) + kept).astype(BF16)
    unfold(ext, fwd_in[1, 0, 0], lines[X2], lines[X2 + 1], parity, True)
    branch = conv(windows_and_near(ext, height, width, parity), weight)
    second[...] = (grown(fwd_in[0, 0, 0], lines[X1]).astype(F32) + branch).astype(BF16)


def grad_two_kernel(height, width, info, message, *rest):
    *outs, ext = rest
    amount = height * width
    unfold(ext, message[1, :amount], message[1, amount:], None, info[PARITY], False)
    grad_into(storing(info, outs, False), message[0, :amount], windows(ext, height, width))


def forward_two_kernel(info, lines, early, second, fresh, weight, out, ext):
    height, width = fresh.shape[2:4]
    amount = height * width
    shape = early.shape
    first = info[FIRST] == 1
    stream = jnp.where(first, flat(fresh[1, 0]), second[:amount])
    near = jnp.where(first, lines[FRESH], second[amount:])
    unfold(ext, stream, near, None, info[PARITY], True)
    out[0, 0, 0] = stream.reshape(shape)
    other = jnp.where(first, fresh[0, 0], early[...])
    branch = conv(windows(ext, height, width), weight).reshape(shape)
    out[1, 0, 0] = (other.astype(F32) + branch).astype(BF16)


def backward_two_kernel(info, lines, early, message, own_second, fwd_in, top_cot, weight, out, ext):
    height, width = top_cot.shape[2:4]
    amount = height * width
    shape = early.shape[1:]
    last = info[LAST] == 1
    out_first = jnp.where(last, flat(fwd_in[1, 0, 0]), message[0, :amount])
    near = jnp.where(last, lines[X2], message[0, amount:])
    out[1, 0, 0] = out_first.reshape(shape)
    unfold(ext, out_first, near, None, info[PARITY], True)
    out_second = jnp.where(last, own_second[:amount], flat(early[0])).reshape(shape)
    branch = conv(windows(ext, height, width), weight).reshape(shape)
    out[0, 0, 0] = (out_second.astype(F32) - branch).astype(BF16)
    cot_second = jnp.where(last, flat(top_cot[1, 0]), message[1, :amount])
    near = jnp.where(last, lines[TOP], message[1, amount:])
    out[2, 0, 0] = cot_second.reshape(shape)
    unfold(ext, cot_second, near, None, info[PARITY], False)
    through = conv_transposed(windows(ext, height, width), weight).reshape(shape)
    cot_first = jnp.where(last, top_cot[0, 0], early[1])
    kept = jnp.where(out[1, 0, 0].astype(F32) > 0, through, 0.0)
    out[3, 0, 0] = (cot_first.astype(F32) + kept).astype(BF16)


def summed(own, parts):
    return functools.reduce(lambda x, y: x + y, [own[...]] + [p[...].astype(F32) for p in parts])


def gather_sum_kernel(info, own, *rest):
    *parts, out = rest
    out[...] = summed(own, parts).astype(BF16)


def finish_kernel(scale, info, own, *rest):
    *parts, out = rest
    out[...] = summed(own, parts) * scale


def shards(fwd_in, bwd_in, fresh, top_cot, conv_weight):
    dp = lax.axis_size("dp")
    places = dp // 2
    dp_pos = lax.axis_index("dp")
    segment_pos = lax.axis_index("segment")
    height, width, channels = fwd_in.shape[3:]
    shard = conv_weight[0].transpose(1, 0, 2)
    rows = shard.shape[1]
    outs = shard.shape[2]
    direct = places in DIRECT and rows % 16 == 0
    info = jnp.stack(
        [
            dp_pos % 2,
            (segment_pos == 0).astype(jnp.int32),
            (segment_pos == lax.axis_size("segment") - 1).astype(jnp.int32),
            dp_pos // 2,
        ]
    ).astype(jnp.int32)
    like = lambda x, dtype: jax.ShapeDtypeStruct(x.shape, dtype)
    taller = lambda *lead: jax.ShapeDtypeStruct(lead + ((height + 1) * width, channels), BF16)
    ext = pltpu.VMEM(((height + 4) * width, 3 * channels), BF16)
    conv_flops = 2 * height * width * channels * TAPS * outs

    if direct:
        mine = [shard]
        for k in range(1, places):
            low = k & -k
            mine.append(swapped(mine[k - low], 2 * low, "weight_z%d" % k))

    tile = lambda *lead: jax.ShapeDtypeStruct(lead + (height, width, channels), BF16)
    lines, early_fwd, early_back = call(
        collect_kernel,
        (jax.ShapeDtypeStruct((LINES, width, channels), BF16), tile(), tile(2)),
        (info, fwd_in, bwd_in, fresh, top_cot),
        COLLECT * conv_flops,
        limit=60,
    )
    lines = swapped(lines, 1, "lines")
    early_back = passed_along(early_back, -1, "early_back")

    def grads(kernel, operands, weight):
        if not direct:
            return call(kernel, (jax.ShapeDtypeStruct((TAPS, channels, outs), F32),), operands, weight, [ext])
        split = (places, TAPS, rows, outs)
        shape = (jax.ShapeDtypeStruct(split, F32), jax.ShapeDtypeStruct(split, BF16))
        return call(kernel, shape, operands, weight, [ext])

    def scattered(name, keep, give=None, hold=()):
        if not direct:
            return lax.psum_scatter(keep, "dp", scatter_dimension=1, tiled=True), []
        amount = places // 2
        shape = lambda dtype: jax.ShapeDtypeStruct((amount,) + shard.shape, dtype)
        got = swapped(give, 1, name)
        stay, send = call(pair_sum_kernel, (shape(F32), shape(BF16)), (after(info, *hold[:1]), keep, got))
        bit = 2
        while amount > 1:
            got = swapped(send, bit, name + "_near")
            amount, bit = amount // 2, 2 * bit
            stay, send = call(fold_kernel, (shape(F32), shape(BF16)), (after(info, *hold[1:]), stay, got))
        return stay[0], [swapped(send, bit, name + "_far")[0]]

    terms_one = grads(grad_one_kernel, (info, lines, fwd_in, bwd_in, top_cot), GRAD_ONE * conv_flops)
    if direct:
        others = mine[:-1] + [after(mine[-1], terms_one[0])]
        pieces = mine + [swapped(x, 1, "weight_core%d" % k) for k, x in enumerate(others)]
        early_fwd = after(early_fwd, pieces[-2])
    else:
        pieces = [lax.all_gather(shard, "dp", axis=1, tiled=True)]

    early_fwd = passed_along(early_fwd, 1, "early_fwd")

    message, second, weight = call(
        step_one_kernel,
        (taller(2), taller(), jax.ShapeDtypeStruct((TAPS, channels, outs), BF16)),
        (after(info, early_back), lines, fwd_in, bwd_in, *pieces),
        1,
        [ext],
    )
    late_back = passed_along(message, -1, "late_back")
    late_fwd = passed_along(second, 1, "late_fwd")

    terms_two = grads(functools.partial(grad_two_kernel, height, width), (after(info, early_fwd), message), 1)
    own_one, parts_one = scattered("term_one", *terms_one)
    own_two, parts_two = scattered("term_two", *terms_two)
    below = call(gather_sum_kernel, like(shard, BF16), (info, own_two, *parts_two))
    from_above = passed_along(below, -1, "below")

    fwd_out = call(
        forward_two_kernel,
        like(fwd_in, BF16),
        (info, lines, early_fwd, late_fwd, fresh, weight),
        STEP_TWO * conv_flops,
        [ext],
    )
    bwd_out = call(
        backward_two_kernel,
        like(bwd_in, BF16),
        (info, lines, early_back, late_back, second, fwd_in, top_cot, weight),
        STEP_TWO * conv_flops,
        [ext],
    )
    scale = (2.0 * dp * height * width) ** -0.5
    finish = functools.partial(finish_kernel, scale)
    grad = call(finish, like(shard, F32), (info, own_one, *parts_one, from_above))
    return fwd_out, bwd_out, grad.transpose(1, 0, 2)[None]


def solution(mesh):
    in_specs = (
        P(None, "segment", "dp", None, None, None),
        P(None, "segment", "dp", None, None, None),
        P(None, "dp", None, None, None),
        P(None, "dp", None, None, None),
        P("segment", "dp", None, None),
    )
    out_specs = (
        P(None, "segment", "dp", None, None, None),
        P(None, "segment", "dp", None, None, None),
        P("segment", "dp", None, None),
    )
    return jax.shard_map(shards, mesh=mesh, in_specs=in_specs, out_specs=out_specs, check_vma=False)
```

```python
import functools

import jax
import jax.numpy as jnp
from jax import lax
from jax.experimental import pallas as pl
from jax.experimental.pallas import tpu as pltpu
from jax.sharding import PartitionSpec as P

BF16 = jnp.bfloat16
F32 = jnp.float32
VMEM = pl.BlockSpec(memory_space=pltpu.VMEM)
SMEM = pl.BlockSpec(memory_space=pltpu.SMEM)
TAPS = 9
PARITY, FIRST, LAST, PLACE, ODD = range(5)
X2, Y1, G2, X1, Y2, G1, FRESH, TOP, LINES = 0, 2, 4, 6, 7, 8, 9, 10, 11
DIRECT = (2, 4, 8)
STEP_TWO = 3
COLLECT = 0
GRAD_ONE = 0


def call(kernel, out_shape, operands, weight=0, scratch=(), limit=32):
    name = getattr(kernel, "func", kernel).__name__
    return pl.pallas_call(
        kernel,
        name=name,
        out_shape=out_shape,
        in_specs=[SMEM] + [VMEM] * (len(operands) - 1),
        out_specs=jax.tree.map(lambda _: VMEM, out_shape),
        scratch_shapes=list(scratch),
        compiler_params=pltpu.CompilerParams(vmem_limit_bytes=limit * 1024 * 1024),
        cost_estimate=pl.CostEstimate(flops=int(weight), bytes_accessed=1, transcendentals=0),
    )(*operands)


def swapped(x, bit, name="halves"):
    with jax.named_scope(name):
        return lax.ppermute(x, "dp", [(i, i ^ bit) for i in range(lax.axis_size("dp"))])


def moved(block, name, target):
    devices = range(lax.axis_size("segment"))
    with jax.named_scope(name):
        return lax.ppermute(block, "segment", [(i, target(i)) for i in devices if target(i) in devices])


def passed_along(block, distance, name):
    return moved(block, name, lambda i: i + distance)


def after(x, *others):
    return lax.optimization_barrier((x, *others))[0]


def flat(tile):
    return tile.reshape(-1, tile.shape[-1])


def unfold(ext, tile, near, beyond, parity, relu):
    width, channels = near.shape
    blank = jnp.zeros_like(near)
    around = [near] if beyond is None else [near, beyond]
    above = [jnp.where(parity == 1, line, blank) for line in around[::-1]]
    below = [jnp.where(parity == 0, line, blank) for line in around]
    rows = jnp.concatenate(above + [flat(tile)] + below, axis=0)
    if relu:
        rows = jnp.maximum(rows, jnp.zeros_like(rows))
    amount = rows.shape[0]
    wide = rows.astype(F32)
    col = lax.rem(lax.broadcasted_iota(jnp.int32, wide.shape, 0), width)
    left = jnp.where(col == 0, 0.0, pltpu.roll(wide, 1, 0))
    right = jnp.where(col == width - 1, 0.0, pltpu.roll(wide, amount - 1, 0))
    ext[:amount, :channels] = left.astype(BF16)
    ext[:amount, channels : 2 * channels] = rows
    ext[:amount, 2 * channels :] = right.astype(BF16)


def windows(ext, height, width):
    return jnp.concatenate([ext[a * width : (a + height) * width, :] for a in range(3)], axis=1)


def windows_and_near(ext, height, width, parity):
    parts = []
    for a in range(3):
        upper = ext[a * width : (a + 1) * width, :]
        lower = ext[(height + 1 + a) * width : (height + 2 + a) * width, :]
        inside = ext[(a + 1) * width : (a + 1 + height) * width, :]
        parts.append(jnp.concatenate([inside, jnp.where(parity == 0, lower, upper)], axis=0))
    return jnp.concatenate(parts, axis=1)


def conv(wide, weight):
    return jnp.dot(wide, weight[...].reshape(-1, weight.shape[2]), preferred_element_type=F32)


def conv_transposed(wide, weight):
    turned = jnp.concatenate([weight[TAPS - 1 - t] for t in range(TAPS)], axis=1)
    return lax.dot_general(wide, turned, (((1,), (1,)), ((), ())), preferred_element_type=F32)


def grad_into(store, stream, wide):
    lines = flat(stream)
    turned = jnp.maximum(lines, jnp.zeros_like(lines)).astype(F32).T.astype(BF16)
    outs = wide.shape[1] // TAPS
    for t in range(TAPS):
        other = TAPS - 1 - t
        store(t, jnp.dot(turned, wide[:, other * outs : (other + 1) * outs], preferred_element_type=F32))


def storing(info, outs, add):
    if len(outs) == 1:

        def store(t, total):
            outs[0][t] = total + outs[0][t] if add else total

        return store
    keep, give = outs

    def store_halves(t, total):
        parts, _, rows, channels = keep.shape
        cut = total.reshape(parts, 2, rows, channels)
        mine = jnp.where(info[PARITY] == 0, cut[:, 0], cut[:, 1])
        theirs = jnp.where(info[PARITY] == 0, cut[:, 1], cut[:, 0])
        if add:
            mine = mine + keep[:, t]
            theirs = theirs + give[:, t].astype(F32)
        keep[:, t] = mine
        give[:, t] = theirs.astype(BF16)

    return store_halves


def collect_kernel(info, fwd_in, bwd_in, fresh, top_cot, lines, back, cross, around):
    parity = info[PARITY]

    def put(slot, tile, amount):
        height = tile.shape[0]
        for i in range(amount):
            lines[slot + i] = jnp.where(parity == 0, tile[height - 1 - i], tile[i])

    put(X2, fwd_in.at[1, 0, 0], 2)
    put(Y1, bwd_in.at[0, 0, 0], 2)
    put(G2, bwd_in.at[3, 0, 0], 2)
    put(X1, fwd_in.at[0, 0, 0], 1)
    put(Y2, bwd_in.at[1, 0, 0], 1)
    put(G1, bwd_in.at[2, 0, 0], 1)
    put(FRESH, fresh.at[1, 0], 1)
    put(TOP, top_cot.at[1, 0], 1)
    odd = info[ODD] == 1
    back[...] = bwd_in[0, 0, 0]
    cross[...] = jnp.where(odd, bwd_in[3, 0, 0], fwd_in[1, 0, 0])
    around[...] = jnp.where(odd, fwd_in[1, 0, 0], bwd_in[3, 0, 0])


def grad_one_kernel(info, lines, fwd_in, bwd_in, top_cot, *rest):
    *outs, ext = rest
    height, width = fwd_in.shape[3:5]
    unfold(ext, bwd_in[3, 0, 0], lines[G2], None, info[PARITY], False)
    grad_into(storing(info, outs, False), bwd_in[0, 0, 0], windows(ext, height, width))

    @pl.when(info[LAST] == 1)
    def _():
        unfold(ext, top_cot[1, 0], lines[TOP], None, info[PARITY], False)
        grad_into(storing(info, outs, True), fwd_in[1, 0, 0], windows(ext, height, width))


def pair_sum_kernel(info, keep, got, stay, send):
    place = info[PLACE]
    for k in range(stay.shape[0]):
        here, there = lax.bitwise_xor(place, 2 * k), lax.bitwise_xor(place, 2 * k + 1)
        stay[k] = keep[here] + got[here].astype(F32)
        send[k] = (keep[there] + got[there].astype(F32)).astype(BF16)


def fold_kernel(info, held, got, stay, send):
    for k in range(stay.shape[0]):
        stay[k] = held[2 * k] + got[2 * k].astype(F32)
        send[k] = (held[2 * k + 1] + got[2 * k + 1].astype(F32)).astype(BF16)


def grown(tile, line):
    return jnp.concatenate([flat(tile), line], axis=0)


def step_one_kernel(info, lines, fwd_in, bwd_in, *rest):
    *pieces, message, second, weight, ext = rest
    height, width = bwd_in.shape[3:5]
    parity = info[PARITY]
    if len(pieces) == 1:
        weight[...] = pieces[0][...]
    else:
        rows = pieces[0].shape[1]
        half = len(pieces) // 2
        for k in range(half):
            there = 2 * lax.bitwise_xor(info[PLACE], k)
            for piece, slot in ((pieces[k], there + parity), (pieces[half + k], there + 1 - parity)):
                weight[:, pl.ds(pl.multiple_of(slot * rows, rows), rows), :] = piece[...]
    first_out = bwd_in[0, 0, 0]
    unfold(ext, first_out, lines[Y1], lines[Y1 + 1], parity, True)
    branch = conv(windows_and_near(ext, height, width, parity), weight)
    message[0] = (grown(bwd_in[1, 0, 0], lines[Y2]).astype(F32) - branch).astype(BF16)
    unfold(ext, bwd_in[3, 0, 0], lines[G2], lines[G2 + 1], parity, False)
    through = conv_transposed(windows_and_near(ext, height, width, parity), weight)
    kept = jnp.where(grown(first_out, lines[Y1]).astype(F32) > 0, through, 0.0)
    message[1] = (grown(bwd_in[2, 0, 0], lines[G1]).astype(F32) + kept).astype(BF16)
    unfold(ext, fwd_in[1, 0, 0], lines[X2], lines[X2 + 1], parity, True)
    branch = conv(windows_and_near(ext, height, width, parity), weight)
    second[...] = (grown(fwd_in[0, 0, 0], lines[X1]).astype(F32) + branch).astype(BF16)


def grad_two_kernel(height, width, info, message, *rest):
    *outs, ext = rest
    amount = height * width
    unfold(ext, message[1, :amount], message[1, amount:], None, info[PARITY], False)
    grad_into(storing(info, outs, False), message[0, :amount], windows(ext, height, width))


def forward_two_kernel(info, lines, cross, around, second, fresh, weight, out, ext):
    height, width = fresh.shape[2:4]
    amount = height * width
    shape = cross.shape
    first = info[FIRST] == 1
    stream = jnp.where(first, flat(fresh[1, 0]), second[:amount])
    near = jnp.where(first, lines[FRESH], second[amount:])
    unfold(ext, stream, near, None, info[PARITY], True)
    out[0, 0, 0] = stream.reshape(shape)
    early = jnp.where(info[ODD] == 1, cross[...], around[...])
    other = jnp.where(first, fresh[0, 0], early)
    branch = conv(windows(ext, height, width), weight).reshape(shape)
    out[1, 0, 0] = (other.astype(F32) + branch).astype(BF16)


def backward_two_kernel(info, lines, back, cross, around, message, own_second, fwd_in, top_cot, weight, out, ext):
    height, width = top_cot.shape[2:4]
    amount = height * width
    shape = back.shape
    last = info[LAST] == 1
    out_first = jnp.where(last, flat(fwd_in[1, 0, 0]), message[0, :amount])
    near = jnp.where(last, lines[X2], message[0, amount:])
    out[1, 0, 0] = out_first.reshape(shape)
    unfold(ext, out_first, near, None, info[PARITY], True)
    out_second = jnp.where(last, own_second[:amount], flat(back[...])).reshape(shape)
    branch = conv(windows(ext, height, width), weight).reshape(shape)
    out[0, 0, 0] = (out_second.astype(F32) - branch).astype(BF16)
    cot_second = jnp.where(last, flat(top_cot[1, 0]), message[1, :amount])
    near = jnp.where(last, lines[TOP], message[1, amount:])
    out[2, 0, 0] = cot_second.reshape(shape)
    unfold(ext, cot_second, near, None, info[PARITY], False)
    through = conv_transposed(windows(ext, height, width), weight).reshape(shape)
    early = jnp.where(info[ODD] == 1, around[...], cross[...])
    cot_first = jnp.where(last, top_cot[0, 0], early)
    kept = jnp.where(out[1, 0, 0].astype(F32) > 0, through, 0.0)
    out[3, 0, 0] = (cot_first.astype(F32) + kept).astype(BF16)


def summed(own, parts):
    return functools.reduce(lambda x, y: x + y, [own[...]] + [p[...].astype(F32) for p in parts])


def gather_sum_kernel(info, own, *rest):
    *parts, out = rest
    out[...] = summed(own, parts).astype(BF16)


def finish_kernel(scale, info, own, *rest):
    *parts, out = rest
    out[...] = summed(own, parts) * scale


def shards(fwd_in, bwd_in, fresh, top_cot, conv_weight):
    dp = lax.axis_size("dp")
    places = dp // 2
    dp_pos = lax.axis_index("dp")
    segment_pos = lax.axis_index("segment")
    height, width, channels = fwd_in.shape[3:]
    shard = conv_weight[0].transpose(1, 0, 2)
    rows = shard.shape[1]
    outs = shard.shape[2]
    direct = places in DIRECT and rows % 16 == 0
    info = jnp.stack(
        [
            dp_pos % 2,
            (segment_pos == 0).astype(jnp.int32),
            (segment_pos == lax.axis_size("segment") - 1).astype(jnp.int32),
            dp_pos // 2,
            segment_pos % 2,
        ]
    ).astype(jnp.int32)
    like = lambda x, dtype: jax.ShapeDtypeStruct(x.shape, dtype)
    taller = lambda *lead: jax.ShapeDtypeStruct(lead + ((height + 1) * width, channels), BF16)
    ext = pltpu.VMEM(((height + 4) * width, 3 * channels), BF16)
    conv_flops = 2 * height * width * channels * TAPS * outs

    if direct:
        mine = [shard]
        for k in range(1, places):
            low = k & -k
            mine.append(swapped(mine[k - low], 2 * low, "weight_z%d" % k))

    tile = lambda *lead: jax.ShapeDtypeStruct(lead + (height, width, channels), BF16)
    lines, back, cross, around = call(
        collect_kernel,
        (jax.ShapeDtypeStruct((LINES, width, channels), BF16), tile(), tile(), tile()),
        (info, fwd_in, bwd_in, fresh, top_cot),
        COLLECT * conv_flops,
        limit=60,
    )
    lines = swapped(lines, 1, "lines")
    back = passed_along(back, -1, "back")
    around = moved(around, "around_first", lambda i: i + 2 if i % 2 else i - 2)

    def grads(kernel, operands, weight):
        if not direct:
            return call(kernel, (jax.ShapeDtypeStruct((TAPS, channels, outs), F32),), operands, weight, [ext])
        split = (places, TAPS, rows, outs)
        shape = (jax.ShapeDtypeStruct(split, F32), jax.ShapeDtypeStruct(split, BF16))
        return call(kernel, shape, operands, weight, [ext])

    def scattered(name, keep, give=None, hold=()):
        if not direct:
            return lax.psum_scatter(keep, "dp", scatter_dimension=1, tiled=True), []
        amount = places // 2
        shape = lambda dtype: jax.ShapeDtypeStruct((amount,) + shard.shape, dtype)
        got = swapped(give, 1, name)
        stay, send = call(pair_sum_kernel, (shape(F32), shape(BF16)), (after(info, *hold[:1]), keep, got))
        bit = 2
        while amount > 1:
            got = swapped(send, bit, name + "_near")
            amount, bit = amount // 2, 2 * bit
            stay, send = call(fold_kernel, (shape(F32), shape(BF16)), (after(info, *hold[1:]), stay, got))
        return stay[0], [swapped(send, bit, name + "_far")[0]]

    terms_one = grads(grad_one_kernel, (after(info, back), lines, fwd_in, bwd_in, top_cot), GRAD_ONE * conv_flops)
    if direct:
        others = mine[:-1] + [after(mine[-1], terms_one[0])]
        others[1] = after(others[1], mine[-1])
        pieces = mine + [swapped(x, 1, "weight_core%d" % k) for k, x in enumerate(others)]
        cross = after(cross, pieces[-2])
    else:
        pieces = [lax.all_gather(shard, "dp", axis=1, tiled=True)]

    cross = moved(cross, "cross", lambda i: i ^ 1)

    message, second, weight = call(
        step_one_kernel,
        (taller(2), taller(), jax.ShapeDtypeStruct((TAPS, channels, outs), BF16)),
        (after(info, around, cross), lines, fwd_in, bwd_in, *pieces),
        1,
        [ext],
    )
    late_back = passed_along(message, -1, "late_back")
    late_fwd = passed_along(second, 1, "late_fwd")
    last = lax.axis_size("segment") - 1
    turn = lambda i: i ^ 1 if (i >= 2 if i % 2 else i <= last - 2) else -1
    around = moved(after(around, message), "around_second", turn)

    terms_two = grads(functools.partial(grad_two_kernel, height, width), (info, message), 1)
    own_one, parts_one = scattered("term_one", *terms_one)
    own_two, parts_two = scattered("term_two", *terms_two)
    below = call(gather_sum_kernel, like(shard, BF16), (info, own_two, *parts_two))
    from_above = passed_along(below, -1, "below")

    fwd_out = call(
        forward_two_kernel,
        like(fwd_in, BF16),
        (info, lines, cross, around, late_fwd, fresh, weight),
        STEP_TWO * conv_flops,
        [ext],
    )
    bwd_out = call(
        backward_two_kernel,
        like(bwd_in, BF16),
        (info, lines, back, cross, around, late_back, second, fwd_in, top_cot, weight),
        STEP_TWO * conv_flops,
        [ext],
    )
    scale = (2.0 * dp * height * width) ** -0.5
    finish = functools.partial(finish_kernel, scale)
    grad = call(finish, like(shard, F32), (info, own_one, *parts_one, from_above))
    return fwd_out, bwd_out, grad.transpose(1, 0, 2)[None]


def solution(mesh):
    in_specs = (
        P(None, "segment", "dp", None, None, None),
        P(None, "segment", "dp", None, None, None),
        P(None, "dp", None, None, None),
        P(None, "dp", None, None, None),
        P("segment", "dp", None, None),
    )
    out_specs = (
        P(None, "segment", "dp", None, None, None),
        P(None, "segment", "dp", None, None, None),
        P("segment", "dp", None, None),
    )
    return jax.shard_map(shards, mesh=mesh, in_specs=in_specs, out_specs=out_specs, check_vma=False)
```

```python
import functools

import jax
import jax.numpy as jnp
from jax import lax
from jax.experimental import pallas as pl
from jax.experimental.pallas import tpu as pltpu
from jax.sharding import PartitionSpec as P

BF16 = jnp.bfloat16
F32 = jnp.float32
VMEM = pl.BlockSpec(memory_space=pltpu.VMEM)
SMEM = pl.BlockSpec(memory_space=pltpu.SMEM)
TAPS = 9
PARITY, FIRST, LAST, PLACE, ODD = range(5)
X2, Y1, G2, X1, Y2, G1, FRESH, TOP, LINES = 0, 2, 4, 6, 7, 8, 9, 10, 11
DIRECT = (2, 4, 8)
STEP_TWO = 3
STEP_ONE = 5
COLLECT = 0
GRAD_ONE = 0


def call(kernel, out_shape, operands, weight=0, scratch=(), limit=32):
    name = getattr(kernel, "func", kernel).__name__
    return pl.pallas_call(
        kernel,
        name=name,
        out_shape=out_shape,
        in_specs=[SMEM] + [VMEM] * (len(operands) - 1),
        out_specs=jax.tree.map(lambda _: VMEM, out_shape),
        scratch_shapes=list(scratch),
        compiler_params=pltpu.CompilerParams(vmem_limit_bytes=limit * 1024 * 1024),
        cost_estimate=pl.CostEstimate(flops=int(weight), bytes_accessed=1, transcendentals=0),
    )(*operands)


def swapped(x, bit, name="halves"):
    with jax.named_scope(name):
        return lax.ppermute(x, "dp", [(i, i ^ bit) for i in range(lax.axis_size("dp"))])


def moved(block, name, target):
    devices = range(lax.axis_size("segment"))
    with jax.named_scope(name):
        return lax.ppermute(block, "segment", [(i, target(i)) for i in devices if target(i) in devices])


def passed_along(block, distance, name):
    return moved(block, name, lambda i: i + distance)


def after(x, *others):
    return lax.optimization_barrier((x, *others))[0]


def flat(tile):
    return tile.reshape(-1, tile.shape[-1])


def unfold(ext, tile, near, beyond, parity, relu):
    width, channels = near.shape
    blank = jnp.zeros_like(near)
    around = [near] if beyond is None else [near, beyond]
    above = [jnp.where(parity == 1, line, blank) for line in around[::-1]]
    below = [jnp.where(parity == 0, line, blank) for line in around]
    rows = jnp.concatenate(above + [flat(tile)] + below, axis=0)
    if relu:
        rows = jnp.maximum(rows, jnp.zeros_like(rows))
    amount = rows.shape[0]
    wide = rows.astype(F32)
    col = lax.rem(lax.broadcasted_iota(jnp.int32, wide.shape, 0), width)
    left = jnp.where(col == 0, 0.0, pltpu.roll(wide, 1, 0))
    right = jnp.where(col == width - 1, 0.0, pltpu.roll(wide, amount - 1, 0))
    ext[:amount, :channels] = left.astype(BF16)
    ext[:amount, channels : 2 * channels] = rows
    ext[:amount, 2 * channels :] = right.astype(BF16)


def windows(ext, height, width):
    return jnp.concatenate([ext[a * width : (a + height) * width, :] for a in range(3)], axis=1)


def windows_and_near(ext, height, width, parity):
    parts = []
    for a in range(3):
        upper = ext[a * width : (a + 1) * width, :]
        lower = ext[(height + 1 + a) * width : (height + 2 + a) * width, :]
        inside = ext[(a + 1) * width : (a + 1 + height) * width, :]
        parts.append(jnp.concatenate([inside, jnp.where(parity == 0, lower, upper)], axis=0))
    return jnp.concatenate(parts, axis=1)


def conv(wide, weight):
    return jnp.dot(wide, weight[...].reshape(-1, weight.shape[2]), preferred_element_type=F32)


def conv_transposed(wide, weight):
    turned = jnp.concatenate([weight[TAPS - 1 - t] for t in range(TAPS)], axis=1)
    return lax.dot_general(wide, turned, (((1,), (1,)), ((), ())), preferred_element_type=F32)


def grad_into(store, stream, wide):
    lines = flat(stream)
    turned = jnp.maximum(lines, jnp.zeros_like(lines)).astype(F32).T.astype(BF16)
    outs = wide.shape[1] // TAPS
    for t in range(TAPS):
        other = TAPS - 1 - t
        store(t, jnp.dot(turned, wide[:, other * outs : (other + 1) * outs], preferred_element_type=F32))


def storing(info, outs, add):
    if len(outs) == 1:

        def store(t, total):
            outs[0][t] = total + outs[0][t] if add else total

        return store
    keep, give = outs

    def store_halves(t, total):
        parts, _, rows, channels = keep.shape
        cut = total.reshape(parts, 2, rows, channels)
        mine = jnp.where(info[PARITY] == 0, cut[:, 0], cut[:, 1])
        theirs = jnp.where(info[PARITY] == 0, cut[:, 1], cut[:, 0])
        if add:
            mine = mine + keep[:, t]
            theirs = theirs + give[:, t].astype(F32)
        keep[:, t] = mine
        give[:, t] = theirs.astype(BF16)

    return store_halves


def collect_kernel(info, fwd_in, bwd_in, fresh, top_cot, lines, back, cross, around):
    parity = info[PARITY]

    def put(slot, tile, amount):
        height = tile.shape[0]
        for i in range(amount):
            lines[slot + i] = jnp.where(parity == 0, tile[height - 1 - i], tile[i])

    put(X2, fwd_in.at[1, 0, 0], 2)
    put(Y1, bwd_in.at[0, 0, 0], 2)
    put(G2, bwd_in.at[3, 0, 0], 2)
    put(X1, fwd_in.at[0, 0, 0], 1)
    put(Y2, bwd_in.at[1, 0, 0], 1)
    put(G1, bwd_in.at[2, 0, 0], 1)
    put(FRESH, fresh.at[1, 0], 1)
    put(TOP, top_cot.at[1, 0], 1)
    odd = info[ODD] == 1
    back[...] = bwd_in[0, 0, 0]
    cross[...] = jnp.where(odd, bwd_in[3, 0, 0], fwd_in[1, 0, 0])
    around[...] = jnp.where(odd, fwd_in[1, 0, 0], bwd_in[3, 0, 0])


def grad_one_kernel(info, lines, fwd_in, bwd_in, top_cot, *rest):
    *outs, ext = rest
    height, width = fwd_in.shape[3:5]
    unfold(ext, bwd_in[3, 0, 0], lines[G2], None, info[PARITY], False)
    grad_into(storing(info, outs, False), bwd_in[0, 0, 0], windows(ext, height, width))

    @pl.when(info[LAST] == 1)
    def _():
        unfold(ext, top_cot[1, 0], lines[TOP], None, info[PARITY], False)
        grad_into(storing(info, outs, True), fwd_in[1, 0, 0], windows(ext, height, width))


def pair_sum_kernel(info, keep, got, stay, send):
    place = info[PLACE]
    for k in range(stay.shape[0]):
        here, there = lax.bitwise_xor(place, 2 * k), lax.bitwise_xor(place, 2 * k + 1)
        stay[k] = keep[here] + got[here].astype(F32)
        send[k] = (keep[there] + got[there].astype(F32)).astype(BF16)


def fold_kernel(info, held, got, stay, send):
    for k in range(stay.shape[0]):
        stay[k] = held[2 * k] + got[2 * k].astype(F32)
        send[k] = (held[2 * k + 1] + got[2 * k + 1].astype(F32)).astype(BF16)


def grown(tile, line):
    return jnp.concatenate([flat(tile), line], axis=0)


def step_one_kernel(info, lines, fwd_in, bwd_in, *rest):
    *pieces, message, second, weight, ext = rest
    height, width = bwd_in.shape[3:5]
    parity = info[PARITY]
    if len(pieces) == 1:
        weight[...] = pieces[0][...]
    else:
        rows = pieces[0].shape[1]
        half = len(pieces) // 2
        for k in range(half):
            there = 2 * lax.bitwise_xor(info[PLACE], k)
            for piece, slot in ((pieces[k], there + parity), (pieces[half + k], there + 1 - parity)):
                weight[:, pl.ds(pl.multiple_of(slot * rows, rows), rows), :] = piece[...]
    first_out = bwd_in[0, 0, 0]
    unfold(ext, first_out, lines[Y1], lines[Y1 + 1], parity, True)
    branch = conv(windows_and_near(ext, height, width, parity), weight)
    message[0] = (grown(bwd_in[1, 0, 0], lines[Y2]).astype(F32) - branch).astype(BF16)
    unfold(ext, bwd_in[3, 0, 0], lines[G2], lines[G2 + 1], parity, False)
    through = conv_transposed(windows_and_near(ext, height, width, parity), weight)
    kept = jnp.where(grown(first_out, lines[Y1]).astype(F32) > 0, through, 0.0)
    message[1] = (grown(bwd_in[2, 0, 0], lines[G1]).astype(F32) + kept).astype(BF16)
    unfold(ext, fwd_in[1, 0, 0], lines[X2], lines[X2 + 1], parity, True)
    branch = conv(windows_and_near(ext, height, width, parity), weight)
    second[...] = (grown(fwd_in[0, 0, 0], lines[X1]).astype(F32) + branch).astype(BF16)


def grad_two_kernel(height, width, info, message, *rest):
    *outs, ext = rest
    amount = height * width
    unfold(ext, message[1, :amount], message[1, amount:], None, info[PARITY], False)
    grad_into(storing(info, outs, False), message[0, :amount], windows(ext, height, width))


def forward_two_kernel(info, lines, cross, around, second, fresh, weight, out, ext):
    height, width = fresh.shape[2:4]
    amount = height * width
    shape = cross.shape
    first = info[FIRST] == 1
    stream = jnp.where(first, flat(fresh[1, 0]), second[:amount])
    near = jnp.where(first, lines[FRESH], second[amount:])
    unfold(ext, stream, near, None, info[PARITY], True)
    out[0, 0, 0] = stream.reshape(shape)
    early = jnp.where(info[ODD] == 1, cross[...], around[...])
    other = jnp.where(first, fresh[0, 0], early)
    branch = conv(windows(ext, height, width), weight).reshape(shape)
    out[1, 0, 0] = (other.astype(F32) + branch).astype(BF16)


def backward_two_kernel(info, lines, back, cross, around, message, own_second, fwd_in, top_cot, weight, out, ext):
    height, width = top_cot.shape[2:4]
    amount = height * width
    shape = back.shape
    last = info[LAST] == 1
    out_first = jnp.where(last, flat(fwd_in[1, 0, 0]), message[0, :amount])
    near = jnp.where(last, lines[X2], message[0, amount:])
    out[1, 0, 0] = out_first.reshape(shape)
    unfold(ext, out_first, near, None, info[PARITY], True)
    out_second = jnp.where(last, own_second[:amount], flat(back[...])).reshape(shape)
    branch = conv(windows(ext, height, width), weight).reshape(shape)
    out[0, 0, 0] = (out_second.astype(F32) - branch).astype(BF16)
    cot_second = jnp.where(last, flat(top_cot[1, 0]), message[1, :amount])
    near = jnp.where(last, lines[TOP], message[1, amount:])
    out[2, 0, 0] = cot_second.reshape(shape)
    unfold(ext, cot_second, near, None, info[PARITY], False)
    through = conv_transposed(windows(ext, height, width), weight).reshape(shape)
    early = jnp.where(info[ODD] == 1, around[...], cross[...])
    cot_first = jnp.where(last, top_cot[0, 0], early)
    kept = jnp.where(out[1, 0, 0].astype(F32) > 0, through, 0.0)
    out[3, 0, 0] = (cot_first.astype(F32) + kept).astype(BF16)


def summed(own, parts):
    return functools.reduce(lambda x, y: x + y, [own[...]] + [p[...].astype(F32) for p in parts])


def gather_sum_kernel(info, own, *rest):
    *parts, out = rest
    out[...] = summed(own, parts).astype(BF16)


def finish_kernel(scale, info, own, *rest):
    *parts, out = rest
    out[...] = summed(own, parts) * scale


def shards(fwd_in, bwd_in, fresh, top_cot, conv_weight):
    dp = lax.axis_size("dp")
    places = dp // 2
    dp_pos = lax.axis_index("dp")
    segment_pos = lax.axis_index("segment")
    height, width, channels = fwd_in.shape[3:]
    shard = conv_weight[0].transpose(1, 0, 2)
    rows = shard.shape[1]
    outs = shard.shape[2]
    direct = places in DIRECT and rows % 16 == 0
    info = jnp.stack(
        [
            dp_pos % 2,
            (segment_pos == 0).astype(jnp.int32),
            (segment_pos == lax.axis_size("segment") - 1).astype(jnp.int32),
            dp_pos // 2,
            segment_pos % 2,
        ]
    ).astype(jnp.int32)
    like = lambda x, dtype: jax.ShapeDtypeStruct(x.shape, dtype)
    taller = lambda *lead: jax.ShapeDtypeStruct(lead + ((height + 1) * width, channels), BF16)
    ext = pltpu.VMEM(((height + 4) * width, 3 * channels), BF16)
    conv_flops = 2 * height * width * channels * TAPS * outs

    if direct:
        mine = [shard]
        for k in range(1, places):
            low = k & -k
            mine.append(swapped(mine[k - low], 2 * low, "weight_z%d" % k))

    tile = lambda *lead: jax.ShapeDtypeStruct(lead + (height, width, channels), BF16)
    lines, back, cross, around = call(
        collect_kernel,
        (jax.ShapeDtypeStruct((LINES, width, channels), BF16), tile(), tile(), tile()),
        (info, fwd_in, bwd_in, fresh, top_cot),
        COLLECT * conv_flops,
        limit=60,
    )
    if direct:
        lines = after(lines, *mine[1:-1])
    lines = swapped(lines, 1, "lines")
    back = passed_along(back, -1, "back")
    around = moved(around, "around_first", lambda i: i + 2 if i % 2 else i - 2)

    def grads(kernel, operands, weight):
        if not direct:
            return call(kernel, (jax.ShapeDtypeStruct((TAPS, channels, outs), F32),), operands, weight, [ext])
        split = (places, TAPS, rows, outs)
        shape = (jax.ShapeDtypeStruct(split, F32), jax.ShapeDtypeStruct(split, BF16))
        return call(kernel, shape, operands, weight, [ext])

    def reduced(name, keep, give=None, hold=()):
        if not direct:
            return lax.psum_scatter(keep, "dp", scatter_dimension=1, tiled=True), None
        shape = lambda dtype: jax.ShapeDtypeStruct((places // 2,) + shard.shape, dtype)
        return call(pair_sum_kernel, (shape(F32), shape(BF16)), (after(info, *hold), keep, swapped(give, 1, name)))

    def scattered(name, stay, send, hold=()):
        if not direct:
            return stay, []
        amount, bit = places // 2, 2
        while amount > 1:
            got = swapped(send, bit, name + "_near")
            amount, bit = amount // 2, 2 * bit
            shape = lambda dtype: jax.ShapeDtypeStruct((amount,) + shard.shape, dtype)
            stay, send = call(fold_kernel, (shape(F32), shape(BF16)), (after(info, *hold), stay, got))
        return stay[0], [swapped(send, bit, name + "_far")[0]]

    terms_one = grads(grad_one_kernel, (after(info, back), lines, fwd_in, bwd_in, top_cot), GRAD_ONE * conv_flops)
    cross = moved(after(cross, lines), "cross", lambda i: i ^ 1)
    sums_one = reduced("term_one", *terms_one, hold=(cross,))
    if direct:
        others = mine[:-1] + [after(mine[-1], terms_one[0])]
        pieces = mine + [swapped(x, 1, "weight_core%d" % k) for k, x in enumerate(others)]
    else:
        pieces = [lax.all_gather(shard, "dp", axis=1, tiled=True)]

    message, second, weight = call(
        step_one_kernel,
        (taller(2), taller(), jax.ShapeDtypeStruct((TAPS, channels, outs), BF16)),
        (after(info, around), lines, fwd_in, bwd_in, *pieces),
        STEP_ONE * conv_flops,
        [ext],
    )
    late_back = passed_along(message, -1, "late_back")
    late_fwd = passed_along(second, 1, "late_fwd")
    last = lax.axis_size("segment") - 1
    turn = lambda i: i ^ 1 if (i >= 2 if i % 2 else i <= last - 2) else -1
    around = moved(after(around, message), "around_second", turn)

    own_one, parts_one = scattered("term_one", *sums_one)
    terms_two = grads(functools.partial(grad_two_kernel, height, width), (after(info, own_one), message), 1)
    sums_two = reduced("term_two", *terms_two, hold=())
    own_two, parts_two = scattered("term_two", *sums_two, hold=parts_one)
    below = call(gather_sum_kernel, like(shard, BF16), (info, own_two, *parts_two))
    from_above = passed_along(below, -1, "below")

    fwd_out = call(
        forward_two_kernel,
        like(fwd_in, BF16),
        (after(info, below), lines, cross, around, late_fwd, fresh, weight),
        STEP_TWO * conv_flops,
        [ext],
    )
    bwd_out = call(
        backward_two_kernel,
        like(bwd_in, BF16),
        (info, lines, back, cross, around, late_back, second, fwd_in, top_cot, weight),
        STEP_TWO * conv_flops,
        [ext],
    )
    scale = (2.0 * dp * height * width) ** -0.5
    finish = functools.partial(finish_kernel, scale)
    grad = call(finish, like(shard, F32), (info, own_one, *parts_one, from_above))
    return fwd_out, bwd_out, grad.transpose(1, 0, 2)[None]


def solution(mesh):
    in_specs = (
        P(None, "segment", "dp", None, None, None),
        P(None, "segment", "dp", None, None, None),
        P(None, "dp", None, None, None),
        P(None, "dp", None, None, None),
        P("segment", "dp", None, None),
    )
    out_specs = (
        P(None, "segment", "dp", None, None, None),
        P(None, "segment", "dp", None, None, None),
        P("segment", "dp", None, None),
    )
    return jax.shard_map(shards, mesh=mesh, in_specs=in_specs, out_specs=out_specs, check_vma=False)
```

```python
import functools

import jax
import jax.numpy as jnp
from jax import lax
from jax.experimental import pallas as pl
from jax.experimental.pallas import tpu as pltpu
from jax.sharding import PartitionSpec as P

BF16 = jnp.bfloat16
F32 = jnp.float32
VMEM = pl.BlockSpec(memory_space=pltpu.VMEM)
SMEM = pl.BlockSpec(memory_space=pltpu.SMEM)
TAPS = 9
PARITY, FIRST, LAST, PLACE, ODD = range(5)
X2, Y1, G2, X1, Y2, G1, FRESH, TOP, LINES = 0, 2, 4, 6, 7, 8, 9, 10, 11
DIRECT = (2, 4, 8)
STEP_TWO = 3
COLLECT = 0
GRAD_ONE = 0


def call(kernel, out_shape, operands, weight=0, scratch=(), limit=32):
    name = getattr(kernel, "func", kernel).__name__
    return pl.pallas_call(
        kernel,
        name=name,
        out_shape=out_shape,
        in_specs=[SMEM] + [VMEM] * (len(operands) - 1),
        out_specs=jax.tree.map(lambda _: VMEM, out_shape),
        scratch_shapes=list(scratch),
        compiler_params=pltpu.CompilerParams(vmem_limit_bytes=limit * 1024 * 1024),
        cost_estimate=pl.CostEstimate(flops=int(weight), bytes_accessed=1, transcendentals=0),
    )(*operands)


def swapped(x, bit, name="halves"):
    with jax.named_scope(name):
        return lax.ppermute(x, "dp", [(i, i ^ bit) for i in range(lax.axis_size("dp"))])


def moved(block, name, target):
    devices = range(lax.axis_size("segment"))
    with jax.named_scope(name):
        return lax.ppermute(block, "segment", [(i, target(i)) for i in devices if target(i) in devices])


def passed_along(block, distance, name):
    return moved(block, name, lambda i: i + distance)


def after(x, *others):
    return lax.optimization_barrier((x, *others))[0]


def flat(tile):
    return tile.reshape(-1, tile.shape[-1])


def unfold(ext, tile, near, beyond, parity, relu):
    width, channels = near.shape
    blank = jnp.zeros_like(near)
    around = [near] if beyond is None else [near, beyond]
    above = [jnp.where(parity == 1, line, blank) for line in around[::-1]]
    below = [jnp.where(parity == 0, line, blank) for line in around]
    rows = jnp.concatenate(above + [flat(tile)] + below, axis=0)
    if relu:
        rows = jnp.maximum(rows, jnp.zeros_like(rows))
    amount = rows.shape[0]
    wide = rows.astype(F32)
    col = lax.rem(lax.broadcasted_iota(jnp.int32, wide.shape, 0), width)
    left = jnp.where(col == 0, 0.0, pltpu.roll(wide, 1, 0))
    right = jnp.where(col == width - 1, 0.0, pltpu.roll(wide, amount - 1, 0))
    ext[:amount, :channels] = left.astype(BF16)
    ext[:amount, channels : 2 * channels] = rows
    ext[:amount, 2 * channels :] = right.astype(BF16)


def windows(ext, height, width):
    return jnp.concatenate([ext[a * width : (a + height) * width, :] for a in range(3)], axis=1)


def windows_and_near(ext, height, width, parity):
    parts = []
    for a in range(3):
        upper = ext[a * width : (a + 1) * width, :]
        lower = ext[(height + 1 + a) * width : (height + 2 + a) * width, :]
        inside = ext[(a + 1) * width : (a + 1 + height) * width, :]
        parts.append(jnp.concatenate([inside, jnp.where(parity == 0, lower, upper)], axis=0))
    return jnp.concatenate(parts, axis=1)


def conv(wide, weight):
    return jnp.dot(wide, weight[...].reshape(-1, weight.shape[2]), preferred_element_type=F32)


def conv_transposed(wide, weight):
    turned = jnp.concatenate([weight[TAPS - 1 - t] for t in range(TAPS)], axis=1)
    return lax.dot_general(wide, turned, (((1,), (1,)), ((), ())), preferred_element_type=F32)


def grad_into(store, stream, wide):
    lines = flat(stream)
    turned = jnp.maximum(lines, jnp.zeros_like(lines)).astype(F32).T.astype(BF16)
    outs = wide.shape[1] // TAPS
    for t in range(TAPS):
        other = TAPS - 1 - t
        store(t, jnp.dot(turned, wide[:, other * outs : (other + 1) * outs], preferred_element_type=F32))


def storing(info, outs, add):
    if len(outs) == 1:

        def store(t, total):
            outs[0][t] = total + outs[0][t] if add else total

        return store
    keep, give = outs

    def store_halves(t, total):
        parts, _, rows, channels = keep.shape
        cut = total.reshape(parts, 2, rows, channels)
        mine = jnp.where(info[PARITY] == 0, cut[:, 0], cut[:, 1])
        theirs = jnp.where(info[PARITY] == 0, cut[:, 1], cut[:, 0])
        if add:
            mine = mine + keep[:, t]
            theirs = theirs + give[:, t].astype(F32)
        keep[:, t] = mine
        give[:, t] = theirs.astype(BF16)

    return store_halves


def collect_kernel(info, fwd_in, bwd_in, fresh, top_cot, lines, back, cross, around):
    parity = info[PARITY]

    def put(slot, tile, amount):
        height = tile.shape[0]
        for i in range(amount):
            lines[slot + i] = jnp.where(parity == 0, tile[height - 1 - i], tile[i])

    put(X2, fwd_in.at[1, 0, 0], 2)
    put(Y1, bwd_in.at[0, 0, 0], 2)
    put(G2, bwd_in.at[3, 0, 0], 2)
    put(X1, fwd_in.at[0, 0, 0], 1)
    put(Y2, bwd_in.at[1, 0, 0], 1)
    put(G1, bwd_in.at[2, 0, 0], 1)
    put(FRESH, fresh.at[1, 0], 1)
    put(TOP, top_cot.at[1, 0], 1)
    odd = info[ODD] == 1
    back[...] = bwd_in[0, 0, 0]
    cross[...] = jnp.where(odd, bwd_in[3, 0, 0], fwd_in[1, 0, 0])
    around[...] = jnp.where(odd, fwd_in[1, 0, 0], bwd_in[3, 0, 0])


def grad_one_kernel(info, lines, fwd_in, bwd_in, top_cot, *rest):
    *outs, ext = rest
    height, width = fwd_in.shape[3:5]
    unfold(ext, bwd_in[3, 0, 0], lines[G2], None, info[PARITY], False)
    grad_into(storing(info, outs, False), bwd_in[0, 0, 0], windows(ext, height, width))

    @pl.when(info[LAST] == 1)
    def _():
        unfold(ext, top_cot[1, 0], lines[TOP], None, info[PARITY], False)
        grad_into(storing(info, outs, True), fwd_in[1, 0, 0], windows(ext, height, width))


def pair_sum_kernel(info, keep, got, stay, send):
    place = info[PLACE]
    for k in range(stay.shape[0]):
        here, there = lax.bitwise_xor(place, 2 * k), lax.bitwise_xor(place, 2 * k + 1)
        stay[k] = keep[here] + got[here].astype(F32)
        send[k] = (keep[there] + got[there].astype(F32)).astype(BF16)


def fold_kernel(info, held, got, stay, send):
    for k in range(stay.shape[0]):
        stay[k] = held[2 * k] + got[2 * k].astype(F32)
        send[k] = (held[2 * k + 1] + got[2 * k + 1].astype(F32)).astype(BF16)


def grown(tile, line):
    return jnp.concatenate([flat(tile), line], axis=0)


def step_one_kernel(info, lines, fwd_in, bwd_in, *rest):
    *pieces, message, second, weight, ext = rest
    height, width = bwd_in.shape[3:5]
    parity = info[PARITY]
    if len(pieces) == 1:
        weight[...] = pieces[0][...]
    else:
        rows = pieces[0].shape[1]
        half = len(pieces) // 2
        for k in range(half):
            there = 2 * lax.bitwise_xor(info[PLACE], k)
            for piece, slot in ((pieces[k], there + parity), (pieces[half + k], there + 1 - parity)):
                weight[:, pl.ds(pl.multiple_of(slot * rows, rows), rows), :] = piece[...]
    first_out = bwd_in[0, 0, 0]
    unfold(ext, first_out, lines[Y1], lines[Y1 + 1], parity, True)
    branch = conv(windows_and_near(ext, height, width, parity), weight)
    message[0] = (grown(bwd_in[1, 0, 0], lines[Y2]).astype(F32) - branch).astype(BF16)
    unfold(ext, bwd_in[3, 0, 0], lines[G2], lines[G2 + 1], parity, False)
    through = conv_transposed(windows_and_near(ext, height, width, parity), weight)
    kept = jnp.where(grown(first_out, lines[Y1]).astype(F32) > 0, through, 0.0)
    message[1] = (grown(bwd_in[2, 0, 0], lines[G1]).astype(F32) + kept).astype(BF16)
    unfold(ext, fwd_in[1, 0, 0], lines[X2], lines[X2 + 1], parity, True)
    branch = conv(windows_and_near(ext, height, width, parity), weight)
    second[...] = (grown(fwd_in[0, 0, 0], lines[X1]).astype(F32) + branch).astype(BF16)


def grad_two_kernel(height, width, info, message, *rest):
    *outs, ext = rest
    amount = height * width
    unfold(ext, message[1, :amount], message[1, amount:], None, info[PARITY], False)
    grad_into(storing(info, outs, False), message[0, :amount], windows(ext, height, width))


def forward_two_kernel(info, lines, cross, around, second, fresh, weight, out, ext):
    height, width = fresh.shape[2:4]
    amount = height * width
    shape = cross.shape
    first = info[FIRST] == 1
    stream = jnp.where(first, flat(fresh[1, 0]), second[:amount])
    near = jnp.where(first, lines[FRESH], second[amount:])
    unfold(ext, stream, near, None, info[PARITY], True)
    out[0, 0, 0] = stream.reshape(shape)
    early = jnp.where(info[ODD] == 1, cross[...], around[...])
    other = jnp.where(first, fresh[0, 0], early)
    branch = conv(windows(ext, height, width), weight).reshape(shape)
    out[1, 0, 0] = (other.astype(F32) + branch).astype(BF16)


def backward_two_kernel(info, lines, back, cross, around, message, own_second, fwd_in, top_cot, weight, out, ext):
    height, width = top_cot.shape[2:4]
    amount = height * width
    shape = back.shape
    last = info[LAST] == 1
    out_first = jnp.where(last, flat(fwd_in[1, 0, 0]), message[0, :amount])
    near = jnp.where(last, lines[X2], message[0, amount:])
    out[1, 0, 0] = out_first.reshape(shape)
    unfold(ext, out_first, near, None, info[PARITY], True)
    out_second = jnp.where(last, own_second[:amount], flat(back[...])).reshape(shape)
    branch = conv(windows(ext, height, width), weight).reshape(shape)
    out[0, 0, 0] = (out_second.astype(F32) - branch).astype(BF16)
    cot_second = jnp.where(last, flat(top_cot[1, 0]), message[1, :amount])
    near = jnp.where(last, lines[TOP], message[1, amount:])
    out[2, 0, 0] = cot_second.reshape(shape)
    unfold(ext, cot_second, near, None, info[PARITY], False)
    through = conv_transposed(windows(ext, height, width), weight).reshape(shape)
    early = jnp.where(info[ODD] == 1, around[...], cross[...])
    cot_first = jnp.where(last, top_cot[0, 0], early)
    kept = jnp.where(out[1, 0, 0].astype(F32) > 0, through, 0.0)
    out[3, 0, 0] = (cot_first.astype(F32) + kept).astype(BF16)


def summed(own, parts):
    return functools.reduce(lambda x, y: x + y, [own[...]] + [p[...].astype(F32) for p in parts])


def gather_sum_kernel(info, own, *rest):
    *parts, out = rest
    out[...] = summed(own, parts).astype(BF16)


def finish_kernel(scale, info, own, *rest):
    *parts, out = rest
    out[...] = summed(own, parts) * scale


def shards(fwd_in, bwd_in, fresh, top_cot, conv_weight):
    dp = lax.axis_size("dp")
    places = dp // 2
    dp_pos = lax.axis_index("dp")
    segment_pos = lax.axis_index("segment")
    height, width, channels = fwd_in.shape[3:]
    shard = conv_weight[0].transpose(1, 0, 2)
    rows = shard.shape[1]
    outs = shard.shape[2]
    direct = places in DIRECT and rows % 16 == 0
    info = jnp.stack(
        [
            dp_pos % 2,
            (segment_pos == 0).astype(jnp.int32),
            (segment_pos == lax.axis_size("segment") - 1).astype(jnp.int32),
            dp_pos // 2,
            segment_pos % 2,
        ]
    ).astype(jnp.int32)
    like = lambda x, dtype: jax.ShapeDtypeStruct(x.shape, dtype)
    taller = lambda *lead: jax.ShapeDtypeStruct(lead + ((height + 1) * width, channels), BF16)
    ext = pltpu.VMEM(((height + 4) * width, 3 * channels), BF16)
    conv_flops = 2 * height * width * channels * TAPS * outs

    if direct:
        mine = [shard]
        for k in range(1, places):
            low = k & -k
            mine.append(swapped(mine[k - low], 2 * low, "weight_z%d" % k))

    tile = lambda *lead: jax.ShapeDtypeStruct(lead + (height, width, channels), BF16)
    lines, back, cross, around = call(
        collect_kernel,
        (jax.ShapeDtypeStruct((LINES, width, channels), BF16), tile(), tile(), tile()),
        (info, fwd_in, bwd_in, fresh, top_cot),
        COLLECT * conv_flops,
        limit=60,
    )
    if direct:
        lines = after(lines, *mine[1:-1])
    lines = swapped(lines, 1, "lines")
    back = passed_along(back, -1, "back")
    around = moved(around, "around_first", lambda i: i + 2 if i % 2 else i - 2)

    def grads(kernel, operands, weight):
        if not direct:
            return call(kernel, (jax.ShapeDtypeStruct((TAPS, channels, outs), F32),), operands, weight, [ext])
        split = (places, TAPS, rows, outs)
        shape = (jax.ShapeDtypeStruct(split, F32), jax.ShapeDtypeStruct(split, BF16))
        return call(kernel, shape, operands, weight, [ext])

    def scattered(name, keep, give=None, hold=()):
        if not direct:
            return lax.psum_scatter(keep, "dp", scatter_dimension=1, tiled=True), []
        amount = places // 2
        shape = lambda dtype: jax.ShapeDtypeStruct((amount,) + shard.shape, dtype)
        got = swapped(give, 1, name)
        stay, send = call(pair_sum_kernel, (shape(F32), shape(BF16)), (after(info, *hold[:1]), keep, got))
        bit = 2
        while amount > 1:
            got = swapped(send, bit, name + "_near")
            amount, bit = amount // 2, 2 * bit
            stay, send = call(fold_kernel, (shape(F32), shape(BF16)), (after(info, *hold[1:]), stay, got))
        return stay[0], [swapped(send, bit, name + "_far")[0]]

    terms_one = grads(grad_one_kernel, (after(info, back), lines, fwd_in, bwd_in, top_cot), GRAD_ONE * conv_flops)
    if direct:
        others = mine[:-1] + [after(mine[-1], terms_one[0])]
        pieces = mine + [swapped(x, 1, "weight_core%d" % k) for k, x in enumerate(others)]
        cross = after(cross, pieces[-2])
    else:
        pieces = [lax.all_gather(shard, "dp", axis=1, tiled=True)]

    cross = moved(cross, "cross", lambda i: i ^ 1)

    message, second, weight = call(
        step_one_kernel,
        (taller(2), taller(), jax.ShapeDtypeStruct((TAPS, channels, outs), BF16)),
        (after(info, around), lines, fwd_in, bwd_in, *pieces),
        1,
        [ext],
    )
    late_back = passed_along(message, -1, "late_back")
    late_fwd = passed_along(second, 1, "late_fwd")
    last = lax.axis_size("segment") - 1
    turn = lambda i: i ^ 1 if (i >= 2 if i % 2 else i <= last - 2) else -1
    around = moved(after(around, message), "around_second", turn)

    terms_two = grads(functools.partial(grad_two_kernel, height, width), (after(info, cross), message), 1)
    own_one, parts_one = scattered("term_one", *terms_one)
    own_two, parts_two = scattered("term_two", *terms_two)
    below = call(gather_sum_kernel, like(shard, BF16), (info, own_two, *parts_two))
    from_above = passed_along(below, -1, "below")

    fwd_out = call(
        forward_two_kernel,
        like(fwd_in, BF16),
        (info, lines, cross, around, late_fwd, fresh, weight),
        STEP_TWO * conv_flops,
        [ext],
    )
    bwd_out = call(
        backward_two_kernel,
        like(bwd_in, BF16),
        (info, lines, back, cross, around, late_back, second, fwd_in, top_cot, weight),
        STEP_TWO * conv_flops,
        [ext],
    )
    scale = (2.0 * dp * height * width) ** -0.5
    finish = functools.partial(finish_kernel, scale)
    grad = call(finish, like(shard, F32), (info, own_one, *parts_one, from_above))
    return fwd_out, bwd_out, grad.transpose(1, 0, 2)[None]


def solution(mesh):
    in_specs = (
        P(None, "segment", "dp", None, None, None),
        P(None, "segment", "dp", None, None, None),
        P(None, "dp", None, None, None),
        P(None, "dp", None, None, None),
        P("segment", "dp", None, None),
    )
    out_specs = (
        P(None, "segment", "dp", None, None, None),
        P(None, "segment", "dp", None, None, None),
        P("segment", "dp", None, None),
    )
    return jax.shard_map(shards, mesh=mesh, in_specs=in_specs, out_specs=out_specs, check_vma=False)
```

```python
import functools

import jax
import jax.numpy as jnp
from jax import lax
from jax.experimental import pallas as pl
from jax.experimental.pallas import tpu as pltpu
from jax.sharding import PartitionSpec as P

BF16 = jnp.bfloat16
F32 = jnp.float32
VMEM = pl.BlockSpec(memory_space=pltpu.VMEM)
SMEM = pl.BlockSpec(memory_space=pltpu.SMEM)
TAPS = 9
PARITY, FIRST, LAST, PLACE, ODD = range(5)
X2, Y1, G2, X1, Y2, G1, FRESH, TOP, LINES = 0, 2, 4, 6, 7, 8, 9, 10, 11
DIRECT = (2, 4, 8)
STEP_TWO = 2
COLLECT = 0
GRAD_ONE = 0


def call(kernel, out_shape, operands, weight=0, scratch=(), limit=32):
    name = getattr(kernel, "func", kernel).__name__
    return pl.pallas_call(
        kernel,
        name=name,
        out_shape=out_shape,
        in_specs=[SMEM] + [VMEM] * (len(operands) - 1),
        out_specs=jax.tree.map(lambda _: VMEM, out_shape),
        scratch_shapes=list(scratch),
        compiler_params=pltpu.CompilerParams(vmem_limit_bytes=limit * 1024 * 1024),
        cost_estimate=pl.CostEstimate(flops=int(weight), bytes_accessed=1, transcendentals=0),
    )(*operands)


def swapped(x, bit, name="halves"):
    with jax.named_scope(name):
        return lax.ppermute(x, "dp", [(i, i ^ bit) for i in range(lax.axis_size("dp"))])


def moved(block, name, target):
    devices = range(lax.axis_size("segment"))
    with jax.named_scope(name):
        return lax.ppermute(block, "segment", [(i, target(i)) for i in devices if target(i) in devices])


def passed_along(block, distance, name):
    return moved(block, name, lambda i: i + distance)


def after(x, *others):
    return lax.optimization_barrier((x, *others))[0]


def flat(tile):
    return tile.reshape(-1, tile.shape[-1])


def unfold(ext, tile, near, beyond, parity, relu):
    width, channels = near.shape
    blank = jnp.zeros_like(near)
    around = [near] if beyond is None else [near, beyond]
    above = [jnp.where(parity == 1, line, blank) for line in around[::-1]]
    below = [jnp.where(parity == 0, line, blank) for line in around]
    rows = jnp.concatenate(above + [flat(tile)] + below, axis=0)
    if relu:
        rows = jnp.maximum(rows, jnp.zeros_like(rows))
    amount = rows.shape[0]
    wide = rows.astype(F32)
    col = lax.rem(lax.broadcasted_iota(jnp.int32, wide.shape, 0), width)
    left = jnp.where(col == 0, 0.0, pltpu.roll(wide, 1, 0))
    right = jnp.where(col == width - 1, 0.0, pltpu.roll(wide, amount - 1, 0))
    ext[:amount, :channels] = left.astype(BF16)
    ext[:amount, channels : 2 * channels] = rows
    ext[:amount, 2 * channels :] = right.astype(BF16)


def windows(ext, height, width):
    return jnp.concatenate([ext[a * width : (a + height) * width, :] for a in range(3)], axis=1)


def windows_and_near(ext, height, width, parity):
    parts = []
    for a in range(3):
        upper = ext[a * width : (a + 1) * width, :]
        lower = ext[(height + 1 + a) * width : (height + 2 + a) * width, :]
        inside = ext[(a + 1) * width : (a + 1 + height) * width, :]
        parts.append(jnp.concatenate([inside, jnp.where(parity == 0, lower, upper)], axis=0))
    return jnp.concatenate(parts, axis=1)


def conv(wide, weight):
    return jnp.dot(wide, weight[...].reshape(-1, weight.shape[2]), preferred_element_type=F32)


def conv_transposed(wide, weight):
    turned = jnp.concatenate([weight[TAPS - 1 - t] for t in range(TAPS)], axis=1)
    return lax.dot_general(wide, turned, (((1,), (1,)), ((), ())), preferred_element_type=F32)


def grad_into(store, stream, wide):
    lines = flat(stream)
    turned = jnp.maximum(lines, jnp.zeros_like(lines)).astype(F32).T.astype(BF16)
    outs = wide.shape[1] // TAPS
    for t in range(TAPS):
        other = TAPS - 1 - t
        store(t, jnp.dot(turned, wide[:, other * outs : (other + 1) * outs], preferred_element_type=F32))


def storing(info, outs, add):
    if len(outs) == 1:

        def store(t, total):
            outs[0][t] = total + outs[0][t] if add else total

        return store
    keep, give = outs

    def store_halves(t, total):
        parts, _, rows, channels = keep.shape
        cut = total.reshape(parts, 2, rows, channels)
        mine = jnp.where(info[PARITY] == 0, cut[:, 0], cut[:, 1])
        theirs = jnp.where(info[PARITY] == 0, cut[:, 1], cut[:, 0])
        if add:
            mine = mine + keep[:, t]
            theirs = theirs + give[:, t].astype(F32)
        keep[:, t] = mine
        give[:, t] = theirs.astype(BF16)

    return store_halves


def collect_kernel(info, fwd_in, bwd_in, fresh, top_cot, lines, back, cross, around):
    parity = info[PARITY]

    def put(slot, tile, amount):
        height = tile.shape[0]
        for i in range(amount):
            lines[slot + i] = jnp.where(parity == 0, tile[height - 1 - i], tile[i])

    put(X2, fwd_in.at[1, 0, 0], 2)
    put(Y1, bwd_in.at[0, 0, 0], 2)
    put(G2, bwd_in.at[3, 0, 0], 2)
    put(X1, fwd_in.at[0, 0, 0], 1)
    put(Y2, bwd_in.at[1, 0, 0], 1)
    put(G1, bwd_in.at[2, 0, 0], 1)
    put(FRESH, fresh.at[1, 0], 1)
    put(TOP, top_cot.at[1, 0], 1)
    odd = info[ODD] == 1
    back[...] = bwd_in[0, 0, 0]
    cross[...] = jnp.where(odd, bwd_in[3, 0, 0], fwd_in[1, 0, 0])
    around[...] = jnp.where(odd, fwd_in[1, 0, 0], bwd_in[3, 0, 0])


def grad_one_kernel(info, lines, fwd_in, bwd_in, top_cot, *rest):
    *outs, ext = rest
    height, width = fwd_in.shape[3:5]
    unfold(ext, bwd_in[3, 0, 0], lines[G2], None, info[PARITY], False)
    grad_into(storing(info, outs, False), bwd_in[0, 0, 0], windows(ext, height, width))

    @pl.when(info[LAST] == 1)
    def _():
        unfold(ext, top_cot[1, 0], lines[TOP], None, info[PARITY], False)
        grad_into(storing(info, outs, True), fwd_in[1, 0, 0], windows(ext, height, width))


def pair_sum_kernel(info, keep, got, stay, send):
    place = info[PLACE]
    for k in range(stay.shape[0]):
        here, there = lax.bitwise_xor(place, 2 * k), lax.bitwise_xor(place, 2 * k + 1)
        stay[k] = keep[here] + got[here].astype(F32)
        send[k] = (keep[there] + got[there].astype(F32)).astype(BF16)


def fold_kernel(info, held, got, stay, send):
    for k in range(stay.shape[0]):
        stay[k] = held[2 * k] + got[2 * k].astype(F32)
        send[k] = (held[2 * k + 1] + got[2 * k + 1].astype(F32)).astype(BF16)


def grown(tile, line):
    return jnp.concatenate([flat(tile), line], axis=0)


def step_one_kernel(info, lines, fwd_in, bwd_in, *rest):
    *pieces, message, second, weight, ext = rest
    height, width = bwd_in.shape[3:5]
    parity = info[PARITY]
    if len(pieces) == 1:
        weight[...] = pieces[0][...]
    else:
        rows = pieces[0].shape[1]
        half = len(pieces) // 2
        for k in range(half):
            there = 2 * lax.bitwise_xor(info[PLACE], k)
            for piece, slot in ((pieces[k], there + parity), (pieces[half + k], there + 1 - parity)):
                weight[:, pl.ds(pl.multiple_of(slot * rows, rows), rows), :] = piece[...]
    first_out = bwd_in[0, 0, 0]
    unfold(ext, first_out, lines[Y1], lines[Y1 + 1], parity, True)
    branch = conv(windows_and_near(ext, height, width, parity), weight)
    message[0] = (grown(bwd_in[1, 0, 0], lines[Y2]).astype(F32) - branch).astype(BF16)
    unfold(ext, bwd_in[3, 0, 0], lines[G2], lines[G2 + 1], parity, False)
    through = conv_transposed(windows_and_near(ext, height, width, parity), weight)
    kept = jnp.where(grown(first_out, lines[Y1]).astype(F32) > 0, through, 0.0)
    message[1] = (grown(bwd_in[2, 0, 0], lines[G1]).astype(F32) + kept).astype(BF16)
    unfold(ext, fwd_in[1, 0, 0], lines[X2], lines[X2 + 1], parity, True)
    branch = conv(windows_and_near(ext, height, width, parity), weight)
    second[...] = (grown(fwd_in[0, 0, 0], lines[X1]).astype(F32) + branch).astype(BF16)


def grad_two_kernel(height, width, info, message, *rest):
    *outs, ext = rest
    amount = height * width
    unfold(ext, message[1, :amount], message[1, amount:], None, info[PARITY], False)
    grad_into(storing(info, outs, False), message[0, :amount], windows(ext, height, width))


def forward_two_kernel(info, lines, cross, around, second, fresh, weight, out, ext):
    height, width = fresh.shape[2:4]
    amount = height * width
    shape = cross.shape
    first = info[FIRST] == 1
    stream = jnp.where(first, flat(fresh[1, 0]), second[:amount])
    near = jnp.where(first, lines[FRESH], second[amount:])
    unfold(ext, stream, near, None, info[PARITY], True)
    out[0, 0, 0] = stream.reshape(shape)
    early = jnp.where(info[ODD] == 1, cross[...], around[...])
    other = jnp.where(first, fresh[0, 0], early)
    branch = conv(windows(ext, height, width), weight).reshape(shape)
    out[1, 0, 0] = (other.astype(F32) + branch).astype(BF16)


def backward_two_kernel(info, lines, back, cross, around, message, own_second, fwd_in, top_cot, weight, out, ext):
    height, width = top_cot.shape[2:4]
    amount = height * width
    shape = back.shape
    last = info[LAST] == 1
    out_first = jnp.where(last, flat(fwd_in[1, 0, 0]), message[0, :amount])
    near = jnp.where(last, lines[X2], message[0, amount:])
    out[1, 0, 0] = out_first.reshape(shape)
    unfold(ext, out_first, near, None, info[PARITY], True)
    out_second = jnp.where(last, own_second[:amount], flat(back[...])).reshape(shape)
    branch = conv(windows(ext, height, width), weight).reshape(shape)
    out[0, 0, 0] = (out_second.astype(F32) - branch).astype(BF16)
    cot_second = jnp.where(last, flat(top_cot[1, 0]), message[1, :amount])
    near = jnp.where(last, lines[TOP], message[1, amount:])
    out[2, 0, 0] = cot_second.reshape(shape)
    unfold(ext, cot_second, near, None, info[PARITY], False)
    through = conv_transposed(windows(ext, height, width), weight).reshape(shape)
    early = jnp.where(info[ODD] == 1, around[...], cross[...])
    cot_first = jnp.where(last, top_cot[0, 0], early)
    kept = jnp.where(out[1, 0, 0].astype(F32) > 0, through, 0.0)
    out[3, 0, 0] = (cot_first.astype(F32) + kept).astype(BF16)


def summed(own, parts):
    return functools.reduce(lambda x, y: x + y, [own[...]] + [p[...].astype(F32) for p in parts])


def gather_sum_kernel(info, own, *rest):
    *parts, out = rest
    out[...] = summed(own, parts).astype(BF16)


def finish_kernel(scale, info, own, *rest):
    *parts, out = rest
    out[...] = summed(own, parts) * scale


def shards(fwd_in, bwd_in, fresh, top_cot, conv_weight):
    dp = lax.axis_size("dp")
    places = dp // 2
    dp_pos = lax.axis_index("dp")
    segment_pos = lax.axis_index("segment")
    height, width, channels = fwd_in.shape[3:]
    shard = conv_weight[0].transpose(1, 0, 2)
    rows = shard.shape[1]
    outs = shard.shape[2]
    direct = places in DIRECT and rows % 16 == 0
    info = jnp.stack(
        [
            dp_pos % 2,
            (segment_pos == 0).astype(jnp.int32),
            (segment_pos == lax.axis_size("segment") - 1).astype(jnp.int32),
            dp_pos // 2,
            segment_pos % 2,
        ]
    ).astype(jnp.int32)
    like = lambda x, dtype: jax.ShapeDtypeStruct(x.shape, dtype)
    taller = lambda *lead: jax.ShapeDtypeStruct(lead + ((height + 1) * width, channels), BF16)
    ext = pltpu.VMEM(((height + 4) * width, 3 * channels), BF16)
    conv_flops = 2 * height * width * channels * TAPS * outs

    if direct:
        mine = [shard]
        for k in range(1, places):
            low = k & -k
            mine.append(swapped(mine[k - low], 2 * low, "weight_z%d" % k))

    tile = lambda *lead: jax.ShapeDtypeStruct(lead + (height, width, channels), BF16)
    lines, back, cross, around = call(
        collect_kernel,
        (jax.ShapeDtypeStruct((LINES, width, channels), BF16), tile(), tile(), tile()),
        (info, fwd_in, bwd_in, fresh, top_cot),
        COLLECT * conv_flops,
        limit=60,
    )
    if direct:
        lines = after(lines, *mine[1:-1])
    lines = swapped(lines, 1, "lines")
    back = passed_along(back, -1, "back")
    around = moved(around, "around_first", lambda i: i + 2 if i % 2 else i - 2)

    def grads(kernel, operands, weight):
        if not direct:
            return call(kernel, (jax.ShapeDtypeStruct((TAPS, channels, outs), F32),), operands, weight, [ext])
        split = (places, TAPS, rows, outs)
        shape = (jax.ShapeDtypeStruct(split, F32), jax.ShapeDtypeStruct(split, BF16))
        return call(kernel, shape, operands, weight, [ext])

    def scattered(name, keep, give=None, hold=()):
        if not direct:
            return lax.psum_scatter(keep, "dp", scatter_dimension=1, tiled=True), []
        amount = places // 2
        shape = lambda dtype: jax.ShapeDtypeStruct((amount,) + shard.shape, dtype)
        got = swapped(give, 1, name)
        stay, send = call(pair_sum_kernel, (shape(F32), shape(BF16)), (after(info, *hold[:1]), keep, got))
        bit = 2
        while amount > 1:
            got = swapped(send, bit, name + "_near")
            amount, bit = amount // 2, 2 * bit
            stay, send = call(fold_kernel, (shape(F32), shape(BF16)), (after(info, *hold[1:]), stay, got))
        return stay[0], [swapped(send, bit, name + "_far")[0]]

    terms_one = grads(grad_one_kernel, (after(info, back), lines, fwd_in, bwd_in, top_cot), GRAD_ONE * conv_flops)
    if direct:
        others = mine[:-1] + [after(mine[-1], terms_one[0])]
        pieces = mine + [swapped(x, 1, "weight_core%d" % k) for k, x in enumerate(others)]
        cross = after(cross, pieces[-2])
    else:
        pieces = [lax.all_gather(shard, "dp", axis=1, tiled=True)]

    cross = moved(cross, "cross", lambda i: i ^ 1)

    message, second, weight = call(
        step_one_kernel,
        (taller(2), taller(), jax.ShapeDtypeStruct((TAPS, channels, outs), BF16)),
        (info, lines, fwd_in, bwd_in, *pieces),
        1,
        [ext],
    )
    late_back = passed_along(message, -1, "late_back")
    late_fwd = passed_along(second, 1, "late_fwd")
    last = lax.axis_size("segment") - 1
    first_hop = around
    turn = lambda i: i ^ 1 if (i >= 2 if i % 2 else i <= last - 2) else -1
    around = moved(after(around, message), "around_second", turn)

    terms_two = grads(functools.partial(grad_two_kernel, height, width), (after(info, cross, first_hop), message), 1)
    own_one, parts_one = scattered("term_one", *terms_one)
    own_two, parts_two = scattered("term_two", *terms_two)
    below = call(gather_sum_kernel, like(shard, BF16), (info, own_two, *parts_two))
    from_above = passed_along(below, -1, "below")

    fwd_out = call(
        forward_two_kernel,
        like(fwd_in, BF16),
        (info, lines, cross, around, late_fwd, fresh, weight),
        STEP_TWO * conv_flops,
        [ext],
    )
    bwd_out = call(
        backward_two_kernel,
        like(bwd_in, BF16),
        (info, lines, back, cross, around, late_back, second, fwd_in, top_cot, weight),
        STEP_TWO * conv_flops,
        [ext],
    )
    scale = (2.0 * dp * height * width) ** -0.5
    finish = functools.partial(finish_kernel, scale)
    grad = call(finish, like(shard, F32), (info, own_one, *parts_one, from_above))
    return fwd_out, bwd_out, grad.transpose(1, 0, 2)[None]


def solution(mesh):
    in_specs = (
        P(None, "segment", "dp", None, None, None),
        P(None, "segment", "dp", None, None, None),
        P(None, "dp", None, None, None),
        P(None, "dp", None, None, None),
        P("segment", "dp", None, None),
    )
    out_specs = (
        P(None, "segment", "dp", None, None, None),
        P(None, "segment", "dp", None, None, None),
        P("segment", "dp", None, None),
    )
    return jax.shard_map(shards, mesh=mesh, in_specs=in_specs, out_specs=out_specs, check_vma=False)
```

```python
import functools

import jax
import jax.numpy as jnp
from jax import lax
from jax.experimental import pallas as pl
from jax.experimental.pallas import tpu as pltpu
from jax.sharding import PartitionSpec as P

BF16 = jnp.bfloat16
F32 = jnp.float32
VMEM = pl.BlockSpec(memory_space=pltpu.VMEM)
SMEM = pl.BlockSpec(memory_space=pltpu.SMEM)
TAPS = 9
PARITY, FIRST, LAST, PLACE, ODD = range(5)
X2, Y1, G2, X1, Y2, G1, FRESH, TOP, LINES = 0, 2, 4, 6, 7, 8, 9, 10, 11
DIRECT = (2, 4, 8)
STEP_TWO = 2
COLLECT = 0
GRAD_ONE = 0


def call(kernel, out_shape, operands, weight=0, scratch=(), limit=32):
    name = getattr(kernel, "func", kernel).__name__
    return pl.pallas_call(
        kernel,
        name=name,
        out_shape=out_shape,
        in_specs=[SMEM] + [VMEM] * (len(operands) - 1),
        out_specs=jax.tree.map(lambda _: VMEM, out_shape),
        scratch_shapes=list(scratch),
        compiler_params=pltpu.CompilerParams(vmem_limit_bytes=limit * 1024 * 1024),
        cost_estimate=pl.CostEstimate(flops=int(weight), bytes_accessed=1, transcendentals=0),
    )(*operands)


def swapped(x, bit, name="halves"):
    with jax.named_scope(name):
        return lax.ppermute(x, "dp", [(i, i ^ bit) for i in range(lax.axis_size("dp"))])


def moved(block, name, target):
    devices = range(lax.axis_size("segment"))
    with jax.named_scope(name):
        return lax.ppermute(block, "segment", [(i, target(i)) for i in devices if target(i) in devices])


def passed_along(block, distance, name):
    return moved(block, name, lambda i: i + distance)


def after(x, *others):
    return lax.optimization_barrier((x, *others))[0]


def flat(tile):
    return tile.reshape(-1, tile.shape[-1])


def unfold(ext, tile, near, beyond, parity, relu):
    width, channels = near.shape
    blank = jnp.zeros_like(near)
    around = [near] if beyond is None else [near, beyond]
    above = [jnp.where(parity == 1, line, blank) for line in around[::-1]]
    below = [jnp.where(parity == 0, line, blank) for line in around]
    rows = jnp.concatenate(above + [flat(tile)] + below, axis=0)
    if relu:
        rows = jnp.maximum(rows, jnp.zeros_like(rows))
    amount = rows.shape[0]
    wide = rows.astype(F32)
    col = lax.rem(lax.broadcasted_iota(jnp.int32, wide.shape, 0), width)
    left = jnp.where(col == 0, 0.0, pltpu.roll(wide, 1, 0))
    right = jnp.where(col == width - 1, 0.0, pltpu.roll(wide, amount - 1, 0))
    ext[:amount, :channels] = left.astype(BF16)
    ext[:amount, channels : 2 * channels] = rows
    ext[:amount, 2 * channels :] = right.astype(BF16)


def windows(ext, height, width):
    return jnp.concatenate([ext[a * width : (a + height) * width, :] for a in range(3)], axis=1)


def windows_and_near(ext, height, width, parity):
    parts = []
    for a in range(3):
        upper = ext[a * width : (a + 1) * width, :]
        lower = ext[(height + 1 + a) * width : (height + 2 + a) * width, :]
        inside = ext[(a + 1) * width : (a + 1 + height) * width, :]
        parts.append(jnp.concatenate([inside, jnp.where(parity == 0, lower, upper)], axis=0))
    return jnp.concatenate(parts, axis=1)


def conv(wide, weight):
    return jnp.dot(wide, weight[...].reshape(-1, weight.shape[2]), preferred_element_type=F32)


def conv_transposed(wide, weight):
    turned = jnp.concatenate([weight[TAPS - 1 - t] for t in range(TAPS)], axis=1)
    return lax.dot_general(wide, turned, (((1,), (1,)), ((), ())), preferred_element_type=F32)


def grad_into(store, stream, wide):
    lines = flat(stream)
    turned = jnp.maximum(lines, jnp.zeros_like(lines)).astype(F32).T.astype(BF16)
    outs = wide.shape[1] // TAPS
    for t in range(TAPS):
        other = TAPS - 1 - t
        store(t, jnp.dot(turned, wide[:, other * outs : (other + 1) * outs], preferred_element_type=F32))


def storing(info, outs, add):
    if len(outs) == 1:

        def store(t, total):
            outs[0][t] = total + outs[0][t] if add else total

        return store
    keep, give = outs

    def store_halves(t, total):
        parts, _, rows, channels = keep.shape
        cut = total.reshape(parts, 2, rows, channels)
        mine = jnp.where(info[PARITY] == 0, cut[:, 0], cut[:, 1])
        theirs = jnp.where(info[PARITY] == 0, cut[:, 1], cut[:, 0])
        if add:
            mine = mine + keep[:, t]
            theirs = theirs + give[:, t].astype(F32)
        keep[:, t] = mine
        give[:, t] = theirs.astype(BF16)

    return store_halves


def collect_kernel(info, fwd_in, bwd_in, fresh, top_cot, lines, back, cross, around):
    parity = info[PARITY]

    def put(slot, tile, amount):
        height = tile.shape[0]
        for i in range(amount):
            lines[slot + i] = jnp.where(parity == 0, tile[height - 1 - i], tile[i])

    put(X2, fwd_in.at[1, 0, 0], 2)
    put(Y1, bwd_in.at[0, 0, 0], 2)
    put(G2, bwd_in.at[3, 0, 0], 2)
    put(X1, fwd_in.at[0, 0, 0], 1)
    put(Y2, bwd_in.at[1, 0, 0], 1)
    put(G1, bwd_in.at[2, 0, 0], 1)
    put(FRESH, fresh.at[1, 0], 1)
    put(TOP, top_cot.at[1, 0], 1)
    odd = info[ODD] == 1
    back[...] = bwd_in[0, 0, 0]
    cross[...] = jnp.where(odd, bwd_in[3, 0, 0], fwd_in[1, 0, 0])
    around[...] = jnp.where(odd, fwd_in[1, 0, 0], bwd_in[3, 0, 0])


def grad_one_kernel(info, lines, fwd_in, bwd_in, top_cot, *rest):
    *outs, ext = rest
    height, width = fwd_in.shape[3:5]
    unfold(ext, bwd_in[3, 0, 0], lines[G2], None, info[PARITY], False)
    grad_into(storing(info, outs, False), bwd_in[0, 0, 0], windows(ext, height, width))

    @pl.when(info[LAST] == 1)
    def _():
        unfold(ext, top_cot[1, 0], lines[TOP], None, info[PARITY], False)
        grad_into(storing(info, outs, True), fwd_in[1, 0, 0], windows(ext, height, width))


def pair_sum_kernel(info, keep, got, stay, send):
    place = info[PLACE]
    for k in range(stay.shape[0]):
        here, there = lax.bitwise_xor(place, 2 * k), lax.bitwise_xor(place, 2 * k + 1)
        stay[k] = keep[here] + got[here].astype(F32)
        send[k] = (keep[there] + got[there].astype(F32)).astype(BF16)


def fold_kernel(info, held, got, stay, send):
    for k in range(stay.shape[0]):
        stay[k] = held[2 * k] + got[2 * k].astype(F32)
        send[k] = (held[2 * k + 1] + got[2 * k + 1].astype(F32)).astype(BF16)


def grown(tile, line):
    return jnp.concatenate([flat(tile), line], axis=0)


def step_one_kernel(info, lines, fwd_in, bwd_in, *rest):
    *pieces, message, second, weight, ext = rest
    height, width = bwd_in.shape[3:5]
    parity = info[PARITY]
    if len(pieces) == 1:
        weight[...] = pieces[0][...]
    else:
        rows = pieces[0].shape[1]
        half = len(pieces) // 2
        for k in range(half):
            there = 2 * lax.bitwise_xor(info[PLACE], k)
            for piece, slot in ((pieces[k], there + parity), (pieces[half + k], there + 1 - parity)):
                weight[:, pl.ds(pl.multiple_of(slot * rows, rows), rows), :] = piece[...]
    first_out = bwd_in[0, 0, 0]
    unfold(ext, first_out, lines[Y1], lines[Y1 + 1], parity, True)
    branch = conv(windows_and_near(ext, height, width, parity), weight)
    message[0] = (grown(bwd_in[1, 0, 0], lines[Y2]).astype(F32) - branch).astype(BF16)
    unfold(ext, bwd_in[3, 0, 0], lines[G2], lines[G2 + 1], parity, False)
    through = conv_transposed(windows_and_near(ext, height, width, parity), weight)
    kept = jnp.where(grown(first_out, lines[Y1]).astype(F32) > 0, through, 0.0)
    message[1] = (grown(bwd_in[2, 0, 0], lines[G1]).astype(F32) + kept).astype(BF16)
    unfold(ext, fwd_in[1, 0, 0], lines[X2], lines[X2 + 1], parity, True)
    branch = conv(windows_and_near(ext, height, width, parity), weight)
    second[...] = (grown(fwd_in[0, 0, 0], lines[X1]).astype(F32) + branch).astype(BF16)


def grad_two_kernel(height, width, info, message, *rest):
    *outs, ext = rest
    amount = height * width
    unfold(ext, message[1, :amount], message[1, amount:], None, info[PARITY], False)
    grad_into(storing(info, outs, False), message[0, :amount], windows(ext, height, width))


def forward_two_kernel(info, lines, cross, around, second, fresh, weight, out, ext):
    height, width = fresh.shape[2:4]
    amount = height * width
    shape = cross.shape
    first = info[FIRST] == 1
    stream = jnp.where(first, flat(fresh[1, 0]), second[:amount])
    near = jnp.where(first, lines[FRESH], second[amount:])
    unfold(ext, stream, near, None, info[PARITY], True)
    out[0, 0, 0] = stream.reshape(shape)
    early = jnp.where(info[ODD] == 1, cross[...], around[...])
    other = jnp.where(first, fresh[0, 0], early)
    branch = conv(windows(ext, height, width), weight).reshape(shape)
    out[1, 0, 0] = (other.astype(F32) + branch).astype(BF16)


def backward_two_kernel(info, lines, back, cross, around, message, own_second, fwd_in, top_cot, weight, out, ext):
    height, width = top_cot.shape[2:4]
    amount = height * width
    shape = back.shape
    last = info[LAST] == 1
    out_first = jnp.where(last, flat(fwd_in[1, 0, 0]), message[0, :amount])
    near = jnp.where(last, lines[X2], message[0, amount:])
    out[1, 0, 0] = out_first.reshape(shape)
    unfold(ext, out_first, near, None, info[PARITY], True)
    out_second = jnp.where(last, own_second[:amount], flat(back[...])).reshape(shape)
    branch = conv(windows(ext, height, width), weight).reshape(shape)
    out[0, 0, 0] = (out_second.astype(F32) - branch).astype(BF16)
    cot_second = jnp.where(last, flat(top_cot[1, 0]), message[1, :amount])
    near = jnp.where(last, lines[TOP], message[1, amount:])
    out[2, 0, 0] = cot_second.reshape(shape)
    unfold(ext, cot_second, near, None, info[PARITY], False)
    through = conv_transposed(windows(ext, height, width), weight).reshape(shape)
    early = jnp.where(info[ODD] == 1, around[...], cross[...])
    cot_first = jnp.where(last, top_cot[0, 0], early)
    kept = jnp.where(out[1, 0, 0].astype(F32) > 0, through, 0.0)
    out[3, 0, 0] = (cot_first.astype(F32) + kept).astype(BF16)


def summed(own, parts):
    return functools.reduce(lambda x, y: x + y, [own[...]] + [p[...].astype(F32) for p in parts])


def gather_sum_kernel(info, own, *rest):
    *parts, out = rest
    out[...] = summed(own, parts).astype(BF16)


def finish_kernel(scale, info, own, *rest):
    *parts, out = rest
    out[...] = summed(own, parts) * scale


def shards(fwd_in, bwd_in, fresh, top_cot, conv_weight):
    dp = lax.axis_size("dp")
    places = dp // 2
    dp_pos = lax.axis_index("dp")
    segment_pos = lax.axis_index("segment")
    height, width, channels = fwd_in.shape[3:]
    shard = conv_weight[0].transpose(1, 0, 2)
    rows = shard.shape[1]
    outs = shard.shape[2]
    direct = places in DIRECT and rows % 16 == 0
    info = jnp.stack(
        [
            dp_pos % 2,
            (segment_pos == 0).astype(jnp.int32),
            (segment_pos == lax.axis_size("segment") - 1).astype(jnp.int32),
            dp_pos // 2,
            segment_pos % 2,
        ]
    ).astype(jnp.int32)
    like = lambda x, dtype: jax.ShapeDtypeStruct(x.shape, dtype)
    taller = lambda *lead: jax.ShapeDtypeStruct(lead + ((height + 1) * width, channels), BF16)
    ext = pltpu.VMEM(((height + 4) * width, 3 * channels), BF16)
    conv_flops = 2 * height * width * channels * TAPS * outs

    if direct:
        mine = [shard]
        for k in range(1, places):
            low = k & -k
            mine.append(swapped(mine[k - low], 2 * low, "weight_z%d" % k))

    tile = lambda *lead: jax.ShapeDtypeStruct(lead + (height, width, channels), BF16)
    lines, back, cross, around = call(
        collect_kernel,
        (jax.ShapeDtypeStruct((LINES, width, channels), BF16), tile(), tile(), tile()),
        (info, fwd_in, bwd_in, fresh, top_cot),
        COLLECT * conv_flops,
        limit=60,
    )
    if direct:
        lines = after(lines, *mine[1:-1])
    lines = swapped(lines, 1, "lines")
    back = passed_along(back, -1, "back")
    around = moved(around, "around_first", lambda i: i + 2 if i % 2 else i - 2)

    def grads(kernel, operands, weight):
        if not direct:
            return call(kernel, (jax.ShapeDtypeStruct((TAPS, channels, outs), F32),), operands, weight, [ext])
        split = (places, TAPS, rows, outs)
        shape = (jax.ShapeDtypeStruct(split, F32), jax.ShapeDtypeStruct(split, BF16))
        return call(kernel, shape, operands, weight, [ext])

    def scattered(name, keep, give=None, hold=()):
        if not direct:
            return lax.psum_scatter(keep, "dp", scatter_dimension=1, tiled=True), []
        amount = places // 2
        shape = lambda dtype: jax.ShapeDtypeStruct((amount,) + shard.shape, dtype)
        got = swapped(give, 1, name)
        stay, send = call(pair_sum_kernel, (shape(F32), shape(BF16)), (after(info, *hold[:1]), keep, got))
        bit = 2
        while amount > 1:
            got = swapped(send, bit, name + "_near")
            amount, bit = amount // 2, 2 * bit
            stay, send = call(fold_kernel, (shape(F32), shape(BF16)), (after(info, *hold[1:]), stay, got))
        return stay[0], [swapped(send, bit, name + "_far")[0]]

    terms_one = grads(grad_one_kernel, (after(info, back), lines, fwd_in, bwd_in, top_cot), GRAD_ONE * conv_flops)
    if direct:
        others = mine[:-1] + [after(mine[-1], terms_one[0])]
        pieces = mine + [swapped(x, 1, "weight_core%d" % k) for k, x in enumerate(others)]
        cross = after(cross, pieces[-2])
    else:
        pieces = [lax.all_gather(shard, "dp", axis=1, tiled=True)]

    cross = moved(cross, "cross", lambda i: i ^ 1)

    message, second, weight = call(
        step_one_kernel,
        (taller(2), taller(), jax.ShapeDtypeStruct((TAPS, channels, outs), BF16)),
        (info, lines, fwd_in, bwd_in, *pieces),
        1,
        [ext],
    )
    late_back = passed_along(message, -1, "late_back")
    late_fwd = passed_along(second, 1, "late_fwd")
    last = lax.axis_size("segment") - 1
    first_hop = around
    turn = lambda i: i ^ 1 if (i >= 2 if i % 2 else i <= last - 2) else -1
    around = moved(after(around, message), "around_second", turn)

    terms_two = grads(functools.partial(grad_two_kernel, height, width), (after(info, cross, first_hop), message), 1)
    own_two, parts_two = scattered("term_two", *terms_two)
    below = call(gather_sum_kernel, like(shard, BF16), (info, own_two, *parts_two))
    from_above = passed_along(below, -1, "below")
    own_one, parts_one = scattered("term_one", *terms_one, hold=(info, below))

    fwd_out = call(
        forward_two_kernel,
        like(fwd_in, BF16),
        (info, lines, cross, around, late_fwd, fresh, weight),
        STEP_TWO * conv_flops,
        [ext],
    )
    bwd_out = call(
        backward_two_kernel,
        like(bwd_in, BF16),
        (info, lines, back, cross, around, late_back, second, fwd_in, top_cot, weight),
        STEP_TWO * conv_flops,
        [ext],
    )
    scale = (2.0 * dp * height * width) ** -0.5
    finish = functools.partial(finish_kernel, scale)
    grad = call(finish, like(shard, F32), (info, own_one, *parts_one, from_above))
    return fwd_out, bwd_out, grad.transpose(1, 0, 2)[None]


def solution(mesh):
    in_specs = (
        P(None, "segment", "dp", None, None, None),
        P(None, "segment", "dp", None, None, None),
        P(None, "dp", None, None, None),
        P(None, "dp", None, None, None),
        P("segment", "dp", None, None),
    )
    out_specs = (
        P(None, "segment", "dp", None, None, None),
        P(None, "segment", "dp", None, None, None),
        P("segment", "dp", None, None),
    )
    return jax.shard_map(shards, mesh=mesh, in_specs=in_specs, out_specs=out_specs, check_vma=False)
```

```python
import functools

import jax
import jax.numpy as jnp
from jax import lax
from jax.experimental import pallas as pl
from jax.experimental.pallas import tpu as pltpu
from jax.sharding import PartitionSpec as P

BF16 = jnp.bfloat16
F32 = jnp.float32
VMEM = pl.BlockSpec(memory_space=pltpu.VMEM)
SMEM = pl.BlockSpec(memory_space=pltpu.SMEM)
TAPS = 9
PARITY, FIRST, LAST, PLACE, ODD = range(5)
X2, Y1, G2, X1, Y2, G1, FRESH, TOP, LINES = 0, 2, 4, 6, 7, 8, 9, 10, 11
DIRECT = (2, 4, 8)
STEP_TWO = 2
COLLECT = 0
GRAD_ONE = 0


def call(kernel, out_shape, operands, weight=0, scratch=(), limit=32):
    name = getattr(kernel, "func", kernel).__name__
    return pl.pallas_call(
        kernel,
        name=name,
        out_shape=out_shape,
        in_specs=[SMEM] + [VMEM] * (len(operands) - 1),
        out_specs=jax.tree.map(lambda _: VMEM, out_shape),
        scratch_shapes=list(scratch),
        compiler_params=pltpu.CompilerParams(vmem_limit_bytes=limit * 1024 * 1024),
        cost_estimate=pl.CostEstimate(flops=int(weight), bytes_accessed=1, transcendentals=0),
    )(*operands)


def swapped(x, bit, name="halves"):
    with jax.named_scope(name):
        return lax.ppermute(x, "dp", [(i, i ^ bit) for i in range(lax.axis_size("dp"))])


def moved(block, name, target):
    devices = range(lax.axis_size("segment"))
    with jax.named_scope(name):
        return lax.ppermute(block, "segment", [(i, target(i)) for i in devices if target(i) in devices])


def passed_along(block, distance, name):
    return moved(block, name, lambda i: i + distance)


def after(x, *others):
    return lax.optimization_barrier((x, *others))[0]


def flat(tile):
    return tile.reshape(-1, tile.shape[-1])


def unfold(ext, tile, near, beyond, parity, relu):
    width, channels = near.shape
    blank = jnp.zeros_like(near)
    around = [near] if beyond is None else [near, beyond]
    above = [jnp.where(parity == 1, line, blank) for line in around[::-1]]
    below = [jnp.where(parity == 0, line, blank) for line in around]
    rows = jnp.concatenate(above + [flat(tile)] + below, axis=0)
    if relu:
        rows = jnp.maximum(rows, jnp.zeros_like(rows))
    amount = rows.shape[0]
    wide = rows.astype(F32)
    col = lax.rem(lax.broadcasted_iota(jnp.int32, wide.shape, 0), width)
    left = jnp.where(col == 0, 0.0, pltpu.roll(wide, 1, 0))
    right = jnp.where(col == width - 1, 0.0, pltpu.roll(wide, amount - 1, 0))
    ext[:amount, :channels] = left.astype(BF16)
    ext[:amount, channels : 2 * channels] = rows
    ext[:amount, 2 * channels :] = right.astype(BF16)


def windows(ext, height, width):
    return jnp.concatenate([ext[a * width : (a + height) * width, :] for a in range(3)], axis=1)


def windows_and_near(ext, height, width, parity):
    parts = []
    for a in range(3):
        upper = ext[a * width : (a + 1) * width, :]
        lower = ext[(height + 1 + a) * width : (height + 2 + a) * width, :]
        inside = ext[(a + 1) * width : (a + 1 + height) * width, :]
        parts.append(jnp.concatenate([inside, jnp.where(parity == 0, lower, upper)], axis=0))
    return jnp.concatenate(parts, axis=1)


def conv(wide, weight):
    return jnp.dot(wide, weight[...].reshape(-1, weight.shape[2]), preferred_element_type=F32)


def conv_transposed(wide, weight):
    turned = jnp.concatenate([weight[TAPS - 1 - t] for t in range(TAPS)], axis=1)
    return lax.dot_general(wide, turned, (((1,), (1,)), ((), ())), preferred_element_type=F32)


def grad_into(store, stream, wide):
    lines = flat(stream)
    turned = jnp.maximum(lines, jnp.zeros_like(lines)).astype(F32).T.astype(BF16)
    outs = wide.shape[1] // TAPS
    for t in range(TAPS):
        other = TAPS - 1 - t
        store(t, jnp.dot(turned, wide[:, other * outs : (other + 1) * outs], preferred_element_type=F32))


def storing(info, outs, add):
    if len(outs) == 1:

        def store(t, total):
            outs[0][t] = total + outs[0][t] if add else total

        return store
    keep, give = outs

    def store_halves(t, total):
        parts, _, rows, channels = keep.shape
        cut = total.reshape(parts, 2, rows, channels)
        mine = jnp.where(info[PARITY] == 0, cut[:, 0], cut[:, 1])
        theirs = jnp.where(info[PARITY] == 0, cut[:, 1], cut[:, 0])
        if add:
            mine = mine + keep[:, t]
            theirs = theirs + give[:, t].astype(F32)
        keep[:, t] = mine
        give[:, t] = theirs.astype(BF16)

    return store_halves


def collect_kernel(info, fwd_in, bwd_in, fresh, top_cot, lines, back, cross, around):
    parity = info[PARITY]

    def put(slot, tile, amount):
        height = tile.shape[0]
        for i in range(amount):
            lines[slot + i] = jnp.where(parity == 0, tile[height - 1 - i], tile[i])

    put(X2, fwd_in.at[1, 0, 0], 2)
    put(Y1, bwd_in.at[0, 0, 0], 2)
    put(G2, bwd_in.at[3, 0, 0], 2)
    put(X1, fwd_in.at[0, 0, 0], 1)
    put(Y2, bwd_in.at[1, 0, 0], 1)
    put(G1, bwd_in.at[2, 0, 0], 1)
    put(FRESH, fresh.at[1, 0], 1)
    put(TOP, top_cot.at[1, 0], 1)
    odd = info[ODD] == 1
    back[...] = bwd_in[0, 0, 0]
    cross[...] = jnp.where(odd, bwd_in[3, 0, 0], fwd_in[1, 0, 0])
    around[...] = jnp.where(odd, fwd_in[1, 0, 0], bwd_in[3, 0, 0])


def grad_one_kernel(info, lines, fwd_in, bwd_in, top_cot, *rest):
    *outs, ext = rest
    height, width = fwd_in.shape[3:5]
    unfold(ext, bwd_in[3, 0, 0], lines[G2], None, info[PARITY], False)
    grad_into(storing(info, outs, False), bwd_in[0, 0, 0], windows(ext, height, width))

    @pl.when(info[LAST] == 1)
    def _():
        unfold(ext, top_cot[1, 0], lines[TOP], None, info[PARITY], False)
        grad_into(storing(info, outs, True), fwd_in[1, 0, 0], windows(ext, height, width))


def pair_sum_kernel(info, keep, got, stay, send):
    place = info[PLACE]
    for k in range(stay.shape[0]):
        here, there = lax.bitwise_xor(place, 2 * k), lax.bitwise_xor(place, 2 * k + 1)
        stay[k] = keep[here] + got[here].astype(F32)
        send[k] = (keep[there] + got[there].astype(F32)).astype(BF16)


def fold_kernel(info, held, got, stay, send):
    for k in range(stay.shape[0]):
        stay[k] = held[2 * k] + got[2 * k].astype(F32)
        send[k] = (held[2 * k + 1] + got[2 * k + 1].astype(F32)).astype(BF16)


def grown(tile, line):
    return jnp.concatenate([flat(tile), line], axis=0)


def step_one_kernel(info, lines, fwd_in, bwd_in, *rest):
    *pieces, message, second, weight, ext = rest
    height, width = bwd_in.shape[3:5]
    parity = info[PARITY]
    if len(pieces) == 1:
        weight[...] = pieces[0][...]
    else:
        rows = pieces[0].shape[1]
        half = len(pieces) // 2
        for k in range(half):
            there = 2 * lax.bitwise_xor(info[PLACE], k)
            for piece, slot in ((pieces[k], there + parity), (pieces[half + k], there + 1 - parity)):
                weight[:, pl.ds(pl.multiple_of(slot * rows, rows), rows), :] = piece[...]
    first_out = bwd_in[0, 0, 0]
    unfold(ext, first_out, lines[Y1], lines[Y1 + 1], parity, True)
    branch = conv(windows_and_near(ext, height, width, parity), weight)
    message[0] = (grown(bwd_in[1, 0, 0], lines[Y2]).astype(F32) - branch).astype(BF16)
    unfold(ext, bwd_in[3, 0, 0], lines[G2], lines[G2 + 1], parity, False)
    through = conv_transposed(windows_and_near(ext, height, width, parity), weight)
    kept = jnp.where(grown(first_out, lines[Y1]).astype(F32) > 0, through, 0.0)
    message[1] = (grown(bwd_in[2, 0, 0], lines[G1]).astype(F32) + kept).astype(BF16)
    unfold(ext, fwd_in[1, 0, 0], lines[X2], lines[X2 + 1], parity, True)
    branch = conv(windows_and_near(ext, height, width, parity), weight)
    second[...] = (grown(fwd_in[0, 0, 0], lines[X1]).astype(F32) + branch).astype(BF16)


def grad_two_kernel(height, width, info, message, *rest):
    *outs, ext = rest
    amount = height * width
    unfold(ext, message[1, :amount], message[1, amount:], None, info[PARITY], False)
    grad_into(storing(info, outs, False), message[0, :amount], windows(ext, height, width))


def forward_two_kernel(info, lines, cross, around, second, fresh, weight, out, ext):
    height, width = fresh.shape[2:4]
    amount = height * width
    shape = cross.shape
    first = info[FIRST] == 1
    stream = jnp.where(first, flat(fresh[1, 0]), second[:amount])
    near = jnp.where(first, lines[FRESH], second[amount:])
    unfold(ext, stream, near, None, info[PARITY], True)
    out[0, 0, 0] = stream.reshape(shape)
    early = jnp.where(info[ODD] == 1, cross[...], around[...])
    other = jnp.where(first, fresh[0, 0], early)
    branch = conv(windows(ext, height, width), weight).reshape(shape)
    out[1, 0, 0] = (other.astype(F32) + branch).astype(BF16)


def backward_two_kernel(info, lines, back, cross, around, message, own_second, fwd_in, top_cot, weight, out, ext):
    height, width = top_cot.shape[2:4]
    amount = height * width
    shape = back.shape
    last = info[LAST] == 1
    out_first = jnp.where(last, flat(fwd_in[1, 0, 0]), message[0, :amount])
    near = jnp.where(last, lines[X2], message[0, amount:])
    out[1, 0, 0] = out_first.reshape(shape)
    unfold(ext, out_first, near, None, info[PARITY], True)
    out_second = jnp.where(last, own_second[:amount], flat(back[...])).reshape(shape)
    branch = conv(windows(ext, height, width), weight).reshape(shape)
    out[0, 0, 0] = (out_second.astype(F32) - branch).astype(BF16)
    cot_second = jnp.where(last, flat(top_cot[1, 0]), message[1, :amount])
    near = jnp.where(last, lines[TOP], message[1, amount:])
    out[2, 0, 0] = cot_second.reshape(shape)
    unfold(ext, cot_second, near, None, info[PARITY], False)
    through = conv_transposed(windows(ext, height, width), weight).reshape(shape)
    early = jnp.where(info[ODD] == 1, around[...], cross[...])
    cot_first = jnp.where(last, top_cot[0, 0], early)
    kept = jnp.where(out[1, 0, 0].astype(F32) > 0, through, 0.0)
    out[3, 0, 0] = (cot_first.astype(F32) + kept).astype(BF16)


def summed(own, parts):
    return functools.reduce(lambda x, y: x + y, [own[...]] + [p[...].astype(F32) for p in parts])


def gather_sum_kernel(info, own, *rest):
    *parts, out = rest
    out[...] = summed(own, parts).astype(BF16)


def finish_kernel(scale, info, own, *rest):
    *parts, out = rest
    out[...] = summed(own, parts) * scale


def shards(fwd_in, bwd_in, fresh, top_cot, conv_weight):
    dp = lax.axis_size("dp")
    places = dp // 2
    dp_pos = lax.axis_index("dp")
    segment_pos = lax.axis_index("segment")
    height, width, channels = fwd_in.shape[3:]
    shard = conv_weight[0].transpose(1, 0, 2)
    rows = shard.shape[1]
    outs = shard.shape[2]
    direct = places in DIRECT and rows % 16 == 0
    info = jnp.stack(
        [
            dp_pos % 2,
            (segment_pos == 0).astype(jnp.int32),
            (segment_pos == lax.axis_size("segment") - 1).astype(jnp.int32),
            dp_pos // 2,
            segment_pos % 2,
        ]
    ).astype(jnp.int32)
    like = lambda x, dtype: jax.ShapeDtypeStruct(x.shape, dtype)
    taller = lambda *lead: jax.ShapeDtypeStruct(lead + ((height + 1) * width, channels), BF16)
    ext = pltpu.VMEM(((height + 4) * width, 3 * channels), BF16)
    conv_flops = 2 * height * width * channels * TAPS * outs

    if direct:
        mine = [shard]
        for k in range(1, places):
            low = k & -k
            mine.append(swapped(mine[k - low], 2 * low, "weight_z%d" % k))

    tile = lambda *lead: jax.ShapeDtypeStruct(lead + (height, width, channels), BF16)
    lines, back, cross, around = call(
        collect_kernel,
        (jax.ShapeDtypeStruct((LINES, width, channels), BF16), tile(), tile(), tile()),
        (info, fwd_in, bwd_in, fresh, top_cot),
        COLLECT * conv_flops,
        limit=60,
    )
    if direct:
        lines = after(lines, *mine[1:-1])
    lines = swapped(lines, 1, "lines")
    back = passed_along(back, -1, "back")
    around = moved(around, "around_first", lambda i: i + 2 if i % 2 else i - 2)

    def grads(kernel, operands, weight):
        if not direct:
            return call(kernel, (jax.ShapeDtypeStruct((TAPS, channels, outs), F32),), operands, weight, [ext])
        split = (places, TAPS, rows, outs)
        shape = (jax.ShapeDtypeStruct(split, F32), jax.ShapeDtypeStruct(split, BF16))
        return call(kernel, shape, operands, weight, [ext])

    def scattered(name, keep, give=None, hold=()):
        if not direct:
            return lax.psum_scatter(keep, "dp", scatter_dimension=1, tiled=True), []
        amount = places // 2
        shape = lambda dtype: jax.ShapeDtypeStruct((amount,) + shard.shape, dtype)
        got = swapped(give, 1, name)
        stay, send = call(pair_sum_kernel, (shape(F32), shape(BF16)), (after(info, *hold[:1]), keep, got))
        bit = 2
        while amount > 1:
            got = swapped(send, bit, name + "_near")
            amount, bit = amount // 2, 2 * bit
            stay, send = call(fold_kernel, (shape(F32), shape(BF16)), (after(info, *hold[1:]), stay, got))
        return stay[0], [swapped(send, bit, name + "_far")[0]]

    terms_one = grads(grad_one_kernel, (after(info, back), lines, fwd_in, bwd_in, top_cot), GRAD_ONE * conv_flops)
    if direct:
        others = mine[:-1] + [after(mine[-1], terms_one[0])]
        pieces = mine + [swapped(x, 1, "weight_core%d" % k) for k, x in enumerate(others)]
        cross = after(cross, pieces[-2])
    else:
        pieces = [lax.all_gather(shard, "dp", axis=1, tiled=True)]

    cross = moved(cross, "cross", lambda i: i ^ 1)

    message, second, weight = call(
        step_one_kernel,
        (taller(2), taller(), jax.ShapeDtypeStruct((TAPS, channels, outs), BF16)),
        (info, lines, fwd_in, bwd_in, *pieces),
        1,
        [ext],
    )
    late_back = passed_along(message, -1, "late_back")
    late_fwd = passed_along(second, 1, "late_fwd")
    last = lax.axis_size("segment") - 1
    first_hop = around
    turn = lambda i: i ^ 1 if (i >= 2 if i % 2 else i <= last - 2) else -1

    terms_two = grads(functools.partial(grad_two_kernel, height, width), (after(info, cross, first_hop), message), 1)
    own_two, parts_two = scattered("term_two", *terms_two)
    around = moved(after(around, own_two), "around_second", turn)
    below = call(gather_sum_kernel, like(shard, BF16), (info, own_two, *parts_two))
    from_above = passed_along(below, -1, "below")
    own_one, parts_one = scattered("term_one", *terms_one, hold=(info, below))

    fwd_out = call(
        forward_two_kernel,
        like(fwd_in, BF16),
        (info, lines, cross, around, late_fwd, fresh, weight),
        STEP_TWO * conv_flops,
        [ext],
    )
    bwd_out = call(
        backward_two_kernel,
        like(bwd_in, BF16),
        (info, lines, back, cross, around, late_back, second, fwd_in, top_cot, weight),
        STEP_TWO * conv_flops,
        [ext],
    )
    scale = (2.0 * dp * height * width) ** -0.5
    finish = functools.partial(finish_kernel, scale)
    grad = call(finish, like(shard, F32), (info, own_one, *parts_one, from_above))
    return fwd_out, bwd_out, grad.transpose(1, 0, 2)[None]


def solution(mesh):
    in_specs = (
        P(None, "segment", "dp", None, None, None),
        P(None, "segment", "dp", None, None, None),
        P(None, "dp", None, None, None),
        P(None, "dp", None, None, None),
        P("segment", "dp", None, None),
    )
    out_specs = (
        P(None, "segment", "dp", None, None, None),
        P(None, "segment", "dp", None, None, None),
        P("segment", "dp", None, None),
    )
    return jax.shard_map(shards, mesh=mesh, in_specs=in_specs, out_specs=out_specs, check_vma=False)
```
